32 devices in a mesh: dp: 8 (over z, x), tensor: 4 (over y, core).
Axes of the slice: x: 2, y: 2, z: 4, core: 2. Of those that a mesh axis runs over, the one named last changes fastest.
Arguments:
- layer_in: bfloat16 [16, 532, 768], P('dp', 'tensor'), may hold values from -6 to 6
- cotangent: bfloat16 [16, 532, 768], P('dp', 'tensor'), may hold values from -6 to 6
- doc_ids: int32 [16, 512], P('dp'), may hold values from 0 to 7, never falling along the last dimension, each value on 1 to 128 neighbouring positions
- reset_flags: int32 [16], P('dp'), may hold values 0 or 1
- block_slot: int32 [192], replicated, may hold values from 0 to 191, as said below
- master: float32 [4, 192, 96, 96], P('tensor', 'dp'), as said below
- first_moment: float32 [4, 192, 96, 96], P('tensor', 'dp'), as said below
- second_moment: float32 [4, 192, 96, 96], P('tensor', 'dp'), as said below
- left_stats: float32 [4, 192, 96, 96], P('tensor', 'dp'), as said below
- right_stats: float32 [4, 192, 96, 96], P('tensor', 'dp'), as said below
- left_basis: float32 [4, 192, 96, 96], P('tensor', 'dp'), as said below
- right_basis: float32 [4, 192, 96, 96], P('tensor', 'dp'), as said below
- split_params: float32 [4, 1152], P('tensor'), may hold values from -1.2 to 1.2
- split_first: float32 [4, 1152], P('tensor'), as said below
- split_second: float32 [4, 1152], P('tensor'), as said below
- shared: float32 [16, 768], replicated, as said below
- shared_first: float32 [16, 768], replicated, as said below
- shared_second: float32 [16, 768], replicated, as said below
Outputs:
- layer_out: bfloat16 [16, 532, 768], P('dp', 'tensor')
- grad_in: bfloat16 [16, 532, 768], P('dp', 'tensor')
- new_master: float32 [4, 192, 96, 96], P('tensor', 'dp')
- new_copy: bfloat16 [4, 192, 96, 96], P('tensor', 'dp')
- new_first: float32 [4, 192, 96, 96], P('tensor', 'dp')
- new_second: float32 [4, 192, 96, 96], P('tensor', 'dp')
- new_left: float32 [4, 192, 96, 96], P('tensor', 'dp')
- new_right: float32 [4, 192, 96, 96], P('tensor', 'dp')
- new_split: float32 [4, 1152], P('tensor')
- new_split_first: float32 [4, 1152], P('tensor')
- new_split_second: float32 [4, 1152], P('tensor')
- new_shared: float32 [16, 768], replicated
- new_shared_first: float32 [16, 768], replicated
- new_shared_second: float32 [16, 768], replicated
The draws below stay inside these ranges and needn't reach their ends.
Inputs may be any that keep to these rules, and one draw needn't show every extreme that they name: `block_slot`: a permutation; slot s is owned by dp index s // 24. `master`: weights scaled by one over the square root of the fan-in of their matrix, four times that for Wo. `first_moment`: of both signs, no entry near zero. `second_moment`: positive. `left_stats`: symmetric with a dominant diagonal. `right_stats`: symmetric with a dominant diagonal. `left_basis`: orthogonal matrices. `right_basis`: orthogonal matrices. `split_first`: of both signs, no entry near zero. `split_second`: positive. `shared`: gains near one, biases small, memory rows of order one. `shared_first`: of both signs, no entry near zero. `shared_second`: positive.
All inputs are finite; a program needn't handle non-finite values. No bound on the sum of `reset_flags` on one device may be relied on, other than what follows from the above.
Results may differ from the reference program's by a relative error of at most 0.018.
Values may be sent and summed in bfloat16 or wider, within the bound.
No kernel may reach another device: no remote copies, remote signals or barrier semaphores. Data moves between devices by JAX's collectives and lax.ppermute only.
A program may use at most 128 MiB of HBM per device.

```python
import math
import jax
import jax.numpy as jnp
import numpy as np
from jax import lax

D = 768
HEADS = 12
HEAD_DIM = 64
FF = 3072
SEG_TOK = 512
MEM = 10
BLK = 96
STEP = 10
ROWS_SEG = 532
SEGS = 16
TOTAL_ROWS = 8512
SPLIT_W = 1152
NB = 192
VROWS = 16
N_TENSOR = 4


def block_order(key):
    return jax.random.permutation(jax.random.fold_in(key, 11), NB).astype(jnp.int32)


def draw_block_slot(key, part):
    return block_order(key)


def draw_master(key, part):
    order = block_order(key)
    inverse = jnp.zeros((NB,), jnp.int32).at[order].set(jnp.arange(NB, dtype=jnp.int32))
    first_end = D * (3 * D // N_TENSOR) // (BLK * BLK)
    second_end = first_end + D // N_TENSOR * D // (BLK * BLK)
    third_end = second_end + D * (FF // N_TENSOR) // (BLK * BLK)
    scales = jnp.where(inverse < first_end, 1.0, jnp.where(inverse < second_end, 4.0, jnp.where(inverse < third_end, 1.0, math.sqrt(D / FF)))) / math.sqrt(D)
    shape = (N_TENSOR, NB, BLK, BLK)
    noise = jnp.clip(jax.random.normal(jax.random.fold_in(key, 13), shape, jnp.float32), -6.0, 6.0)
    return noise * scales[None, :, None, None]


def signed_moment(key, shape, grad_scale):
    signs = jnp.where(jax.random.bernoulli(jax.random.fold_in(key, 1), 0.5, shape), 1.0, -1.0)
    magnitude = jax.random.uniform(jax.random.fold_in(key, 2), shape, jnp.float32, 0.5, 2.0)
    return signs * magnitude * grad_scale * (0.1 / 0.9)


def square_moment(key, shape, grad_scale):
    factor = jax.random.uniform(jax.random.fold_in(key, 3), shape, jnp.float32, 1.0, 4.0)
    spread = jnp.exp2(jax.random.uniform(jax.random.fold_in(key, 4), shape, jnp.float32, -1.0, 1.0))
    return factor * spread * grad_scale * grad_scale * (0.05 / 0.95)


def block_scale():
    return 0.3 * math.sqrt(TOTAL_ROWS)


def draw_first_moment(key, part):
    return signed_moment(jax.random.fold_in(key, 21), (N_TENSOR, NB, BLK, BLK), block_scale())


def draw_second_moment(key, part):
    return square_moment(jax.random.fold_in(key, 22), (N_TENSOR, NB, BLK, BLK), block_scale())


def statistics(key):
    base = jax.random.uniform(jax.random.fold_in(key, 1), (N_TENSOR, NB, 1, 1), jnp.float32, 1.0, 4.0)
    base = base * (0.05 / 0.95) * BLK * block_scale() ** 2
    noise = jax.random.normal(jax.random.fold_in(key, 2), (N_TENSOR, NB, BLK, BLK), jnp.float32)
    symmetric = (noise + jnp.swapaxes(noise, -1, -2)) * (0.15 / math.sqrt(BLK))
    return base * (jnp.eye(BLK, dtype=jnp.float32) + symmetric)


def draw_left_stats(key, part):
    return statistics(jax.random.fold_in(key, 23))


def draw_right_stats(key, part):
    return statistics(jax.random.fold_in(key, 24))


def rotation(key):
    count = N_TENSOR * NB
    keys = jax.random.split(jax.random.fold_in(key, 3), count)
    orders = jax.vmap(lambda sub_key: jax.random.permutation(sub_key, BLK))(keys)
    signs = jnp.where(jax.random.bernoulli(jax.random.fold_in(key, 5), 0.5, (count, BLK)), 1.0, -1.0)
    index = jnp.arange(BLK, dtype=jnp.float32)
    freq = orders.astype(jnp.float32)[:, None, :]
    cosine = jnp.cos(math.pi * (2.0 * index[None, :, None] + 1.0) * freq / (2.0 * BLK))
    weight = jnp.where(freq == 0.0, math.sqrt(1.0 / BLK), math.sqrt(2.0 / BLK))
    return (signs[:, :, None] * cosine * weight).reshape(N_TENSOR, NB, BLK, BLK)


def draw_left_basis(key, part):
    return rotation(jax.random.fold_in(key, 25))


def draw_right_basis(key, part):
    return rotation(jax.random.fold_in(key, 26))


def draw_split_first(key, part):
    return signed_moment(jax.random.fold_in(key, 27), (N_TENSOR, SPLIT_W), block_scale())


def draw_split_second(key, part):
    return square_moment(jax.random.fold_in(key, 28), (N_TENSOR, SPLIT_W), block_scale())


def draw_shared(key, part):
    noise = jnp.clip(jax.random.normal(jax.random.fold_in(key, 29), (VROWS, D), jnp.float32), -5.0, 5.0)
    row_ids = jnp.arange(VROWS)[:, None]
    is_gain = (row_ids == 1) | (row_ids == 4)
    return jnp.where(is_gain, 1.0 + 0.1 * noise, jnp.where(row_ids < 6, 0.2 * noise, noise))


def shared_scale():
    row_ids = jnp.arange(VROWS)[:, None]
    return jnp.where(row_ids < 6, 0.5 * math.sqrt(TOTAL_ROWS), 0.5 * math.sqrt(SEGS)) * jnp.ones((VROWS, D), jnp.float32)


def draw_shared_first(key, part):
    return signed_moment(jax.random.fold_in(key, 30), (VROWS, D), shared_scale())


def draw_shared_second(key, part):
    return square_moment(jax.random.fold_in(key, 31), (VROWS, D), shared_scale())


def place_ends(entries, key, least, top_value):
    shape = entries.shape
    index_at = [jax.random.randint(jax.random.fold_in(key, axis), (), 0, shape[axis]) for axis in range(len(shape))]
    entries = entries.at[tuple(index_at)].set(least)
    longest = shape.index(max(shape))
    index_at[longest] = (index_at[longest] + 1) % shape[longest]
    return entries.at[tuple(index_at)].set(top_value)


def level_of(rng, dims, cuts, least, top_value):
    def one(dim, shards_of):
        steps = jax.random.uniform(jax.random.fold_in(jax.random.fold_in(rng, 6), dim), (shards_of,), jnp.float32, least / len(cuts), top_value / len(cuts))
        return jnp.repeat(jnp.exp(steps), dims[dim] // shards_of).reshape((-1,) + (1,) * (len(dims) - dim - 1))

    level = one(*cuts[0])
    for cut in cuts[1:]:
        level = level * one(*cut)
    return level


def split_up(number_of, total, most, skew):
    loads = [(1 << 20) // math.isqrt(standing ** skew) + 1 for standing in range(2, number_of + 1)]
    surplus, counts = total - most - (number_of - 1), [1] * (number_of - 1)
    while surplus > 0:
        candidates = [i for i in range(number_of - 1) if counts[i] < most]
        whole, left = sum([loads[i] for i in candidates]), surplus
        for i in candidates:
            extra = min(most - counts[i], max(1, left * loads[i] // whole), surplus)
            counts[i] = counts[i] + extra
            surplus = surplus - extra
    return np.array([most] + counts)


def uneven_parts(rng, count, total, reach, slope):
    if count == 2:
        one = jax.random.randint(rng, (), max(1, total - reach), min(reach, total - 1) + 1)
        return jnp.stack([one, total - one])
    tallies = jnp.asarray(split_up(count, total, reach, slope), jnp.int32)
    pairs = (count - 1) // 2
    giver, receiver = tallies[1:1 + 2 * pairs:2], tallies[2:2 + 2 * pairs:2]
    margin = jnp.minimum(giver - 1, reach - receiver)
    moved = jax.random.randint(jax.random.fold_in(rng, 1), (pairs,), 0, 1 << 20) % (margin + 1)
    tallies = tallies.at[1:1 + 2 * pairs:2].set(giver - moved).at[2:2 + 2 * pairs:2].set(receiver + moved)
    return tallies[jax.random.permutation(jax.random.fold_in(rng, 2), count)]


def gaussian(rng, shape, scale, reach, cuts=(), kind=jnp.bfloat16):
    loudness = level_of(rng, shape, cuts, -0.22, 0.18) if cuts else 1.0
    entries = jax.random.normal(rng, shape, jnp.float32) * scale * loudness
    return jnp.minimum(jnp.maximum(entries, -reach), reach).astype(kind)


def setup_inputs(seed: int = 0) -> dict:
    seeds = jax.random.split(jax.random.key(seed), 19)
    layer_in = gaussian(seeds[0], (SEGS, ROWS_SEG, D), 1.0, 6.0, ((0, 8), (1, 4)))
    cotangent = gaussian(seeds[1], (SEGS, ROWS_SEG, D), 1.0, 6.0, ((0, 8), (1, 4)))
    doc_ids = jax.vmap(lambda own: jnp.searchsorted(jnp.cumsum(uneven_parts(own, 8, SEG_TOK, SEG_TOK // 4, 1)), jnp.arange(SEG_TOK), side="right"))(jax.random.split(seeds[2], SEGS)).reshape((SEGS, SEG_TOK)).astype(jnp.int32)
    reset_flags = place_ends((jax.random.randint(seeds[3], (SEGS,), 0, 2) < 1).astype(jnp.int32), jax.random.fold_in(seeds[3], 1), 0, 1)
    block_slot = draw_block_slot(jax.random.fold_in(seeds[18], 71), 0)
    master = draw_master(jax.random.fold_in(seeds[18], 71), 0)
    first_moment = draw_first_moment(jax.random.fold_in(seeds[18], 71), 0)
    second_moment = draw_second_moment(jax.random.fold_in(seeds[18], 71), 0)
    left_stats = draw_left_stats(jax.random.fold_in(seeds[18], 71), 0)
    right_stats = draw_right_stats(jax.random.fold_in(seeds[18], 71), 0)
    left_basis = draw_left_basis(jax.random.fold_in(seeds[18], 71), 0)
    right_basis = draw_right_basis(jax.random.fold_in(seeds[18], 71), 0)
    split_params = gaussian(seeds[12], (N_TENSOR, SPLIT_W), 0.2, 1.2, ((0, 4),), jnp.float32)
    split_first = draw_split_first(jax.random.fold_in(seeds[18], 71), 0)
    split_second = draw_split_second(jax.random.fold_in(seeds[18], 71), 0)
    shared = draw_shared(jax.random.fold_in(seeds[18], 71), 0)
    shared_first = draw_shared_first(jax.random.fold_in(seeds[18], 71), 0)
    shared_second = draw_shared_second(jax.random.fold_in(seeds[18], 71), 0)
    return dict(layer_in=layer_in, cotangent=cotangent, doc_ids=doc_ids, reset_flags=reset_flags, block_slot=block_slot, master=master, first_moment=first_moment, second_moment=second_moment, left_stats=left_stats, right_stats=right_stats, left_basis=left_basis, right_basis=right_basis, split_params=split_params, split_first=split_first, split_second=split_second, shared=shared, shared_first=shared_first, shared_second=shared_second)


highest_precision_flag = lax.Precision.HIGHEST
beta_one = 0.9
beta_two = 0.95
adam_eps = 1e-08
norm_eps = 1e-12
rate_matrix = 0.05
rate_vector = 0.1
rate_shared = 0.75

@jax.custom_vjp
def low(v):
    return lax.optimization_barrier(v.astype(jnp.bfloat16)).astype(jnp.float32)

@jax.custom_vjp
def low_back(v):
    return v

def low_keep(v):
    return (low(v), None)

def low_pass(kept, grad):
    return (grad,)

def back_keep(v):
    return (v, None)

def back_low(kept, grad):
    return (low(grad),)
low.defvjp(low_keep, low_pass)
low_back.defvjp(back_keep, back_low)

def unpack(blocks, height, breadth):
    blk_size = blocks.shape[-1]
    leading = blocks.shape[:-3]
    grid = blocks.reshape(leading + (height // blk_size, breadth // blk_size, blk_size, blk_size))
    return jnp.swapaxes(grid, -2, -3).reshape(leading + (height, breadth))

def split_blocks(blocks, model_width, tensors):
    blk_size = blocks.shape[-1]
    qkv_cols = 3 * model_width // tensors
    ctx_cols = model_width // tensors
    ffn_cols = FF // tensors
    first_end = model_width * qkv_cols // (blk_size * blk_size)
    second_end = first_end + ctx_cols * model_width // (blk_size * blk_size)
    third_end = second_end + model_width * ffn_cols // (blk_size * blk_size)
    return (unpack(blocks[..., :first_end, :, :], model_width, qkv_cols), unpack(blocks[..., first_end:second_end, :, :], ctx_cols, model_width), unpack(blocks[..., second_end:third_end, :, :], model_width, ffn_cols), unpack(blocks[..., third_end:, :, :], ffn_cols, model_width))

def layer_norm(values, gain_vec, shift_vec):
    centred = values - lax.optimization_barrier(jnp.mean(values, axis=-1, keepdims=True))
    spread = lax.optimization_barrier(jnp.mean(centred * centred, axis=-1, keepdims=True))
    return centred * lax.rsqrt(spread + norm_eps) * gain_vec + shift_vec

def seg_forward(wblocks, split_vals, shared_vals, seg_rows, seg_docs, seg_reset):
    tensors = N_TENSOR
    w_qkv, w_out, up_weight, down_weight = split_blocks(low(wblocks), D, tensors)
    ctx_cols = D // tensors
    heads_here = HEADS // tensors
    q_bias = split_vals[:, :ctx_cols]
    v_bias = split_vals[:, ctx_cols:2 * ctx_cols]
    feedforward_up_bias = split_vals[:, 2 * ctx_cols:]
    row_ids = jnp.arange(ROWS_SEG)
    read_rows = (row_ids[:, None] == jnp.arange(MEM)[None, :]).astype(jnp.float32) * (seg_reset == 1).astype(jnp.float32)
    replaced = lax.optimization_barrier(jnp.sum(read_rows, axis=1)) > 0.5
    x_zero = jnp.where(replaced[:, None], jnp.dot(read_rows, shared_vals[6:], precision=highest_precision_flag), seg_rows)
    whole_in = low(x_zero)
    projected = low_back(jnp.einsum('rd,tdc->trc', whole_in, w_qkv, precision=highest_precision_flag))
    qkv_bias = jnp.concatenate([q_bias, jnp.zeros_like(q_bias), v_bias], axis=1)
    projected = low(projected + qkv_bias[:, None, :])
    query_part = projected[:, :, :ctx_cols].reshape(tensors, ROWS_SEG, heads_here, HEAD_DIM)
    key_part = projected[:, :, ctx_cols:2 * ctx_cols].reshape(tensors, ROWS_SEG, heads_here, HEAD_DIM)
    value_part = projected[:, :, 2 * ctx_cols:].reshape(tensors, ROWS_SEG, heads_here, HEAD_DIM)
    is_memory = (row_ids < MEM) | (row_ids >= MEM + SEG_TOK)
    doc_full = jnp.concatenate([jnp.zeros((MEM,), jnp.int32), seg_docs.astype(jnp.int32), jnp.zeros((MEM,), jnp.int32)])
    visible = is_memory[:, None] | is_memory[None, :] | (doc_full[:, None] == doc_full[None, :])
    raw_scores = low_back(jnp.einsum('tqhd,tkhd->thqk', query_part, key_part, precision=highest_precision_flag))
    scores = jnp.where(visible, raw_scores * HEAD_DIM ** (-0.5), -1000000000.0)
    row_max = lax.optimization_barrier(jnp.max(scores, axis=-1, keepdims=True))
    expo_vals = jnp.exp(scores - row_max)
    attn_probs = expo_vals / lax.optimization_barrier(jnp.sum(expo_vals, axis=-1, keepdims=True))
    context = jnp.einsum('thqk,tkhd->tqhd', low(attn_probs), value_part, precision=highest_precision_flag)
    context = low_back(low(context)).reshape(tensors, ROWS_SEG, ctx_cols)
    attn_sum = low_back(jnp.einsum('trc,tcd->rd', context, w_out, precision=highest_precision_flag))
    h_one = layer_norm(attn_sum + shared_vals[0] + x_zero, shared_vals[1], shared_vals[2])
    hidden_input_rows = low(h_one)
    preactivation_values = low_back(jnp.einsum('pj,kjo->kpo', hidden_input_rows, up_weight, precision=highest_precision_flag)) + feedforward_up_bias[:, None, :]
    gelu_activation_output = low(jax.nn.gelu(preactivation_values, approximate=False))
    feedforward_total = low_back(jnp.einsum('sia,sam->im', gelu_activation_output, down_weight, precision=highest_precision_flag))
    return layer_norm(feedforward_total + shared_vals[3] + h_one, shared_vals[4], shared_vals[5])

def soap_update(weight, grad_mat, first_mom, second_mom, left_stat, right_stat, left_rot, right_rot):
    turned = jnp.einsum('...ia,...ij->...aj', left_rot, grad_mat, precision=highest_precision_flag)
    turned = jnp.einsum('...aj,...jb->...ab', turned, right_rot, precision=highest_precision_flag)
    new_first = beta_one * first_mom + (1.0 - beta_one) * turned
    new_second = beta_two * second_mom + (1.0 - beta_two) * turned * turned
    direction = new_first / (1.0 - beta_one ** STEP) / (jnp.sqrt(new_second / (1.0 - beta_two ** STEP)) + adam_eps)
    back_rot = jnp.einsum('...ia,...ab->...ib', left_rot, direction, precision=highest_precision_flag)
    back_rot = jnp.einsum('...ib,...jb->...ij', back_rot, right_rot, precision=highest_precision_flag)
    new_weight = weight - rate_matrix * back_rot
    new_left = beta_two * left_stat + (1.0 - beta_two) * jnp.einsum('...ik,...jk->...ij', grad_mat, grad_mat, precision=highest_precision_flag)
    new_right = beta_two * right_stat + (1.0 - beta_two) * jnp.einsum('...ki,...kj->...ij', grad_mat, grad_mat, precision=highest_precision_flag)
    return (new_weight, new_first, new_second, new_left, new_right)

def adam_update(values, grad_vec, first_mom, second_mom, step_rate):
    new_first = beta_one * first_mom + (1.0 - beta_one) * grad_vec
    new_second = beta_two * second_mom + (1.0 - beta_two) * grad_vec * grad_vec
    direction = new_first / (1.0 - beta_one ** STEP) / (jnp.sqrt(new_second / (1.0 - beta_two ** STEP)) + adam_eps)
    return (values - step_rate * direction, new_first, new_second)

def reference(layer_in, cotangent, doc_ids, reset_flags, block_slot, master, first_moment, second_moment, left_stats, right_stats, left_basis, right_basis, split_params, split_first, split_second, shared, shared_first, shared_second):
    wblocks = master[:, block_slot]

    def one_segment(totals, seg_item):
        seg_rows, seg_cot, seg_docs, seg_reset = seg_item

        def forward_only(wb_arg, split_arg, shared_arg, rows_arg):
            return seg_forward(wb_arg, split_arg, shared_arg, rows_arg, seg_docs, seg_reset)
        seg_out, pullback = jax.vjp(forward_only, wblocks, split_params, shared, seg_rows)
        grad_w, grad_s, grad_h, grad_x = pullback(seg_cot)
        new_totals = (totals[0] + grad_w, totals[1] + grad_s, totals[2] + grad_h)
        return (new_totals, (seg_out.astype(jnp.bfloat16), grad_x.astype(jnp.bfloat16)))
    start = (jnp.zeros_like(wblocks), jnp.zeros_like(split_params), jnp.zeros_like(shared))
    totals, (out_rows, grad_rows) = lax.scan(one_segment, start, (layer_in.astype(jnp.float32), cotangent.astype(jnp.float32), doc_ids, reset_flags))
    grad_slots = jnp.zeros_like(master).at[:, block_slot].set(totals[0])
    new_master, new_first, new_second, new_left, new_right = soap_update(master, grad_slots, first_moment, second_moment, left_stats, right_stats, left_basis, right_basis)
    new_split, new_split_first, new_split_second = adam_update(split_params, totals[1], split_first, split_second, rate_vector)
    new_shared, new_shared_first, new_shared_second = adam_update(shared, totals[2], shared_first, shared_second, rate_shared)
    return (out_rows, grad_rows, new_master, new_master.astype(jnp.bfloat16), new_first, new_second, new_left, new_right, new_split, new_split_first, new_split_second, new_shared, new_shared_first, new_shared_second)
```

```python
import functools

import jax
import jax.numpy as jnp
from jax import lax
from jax.experimental import pallas as pl
from jax.experimental.pallas import tpu as pltpu
from jax.sharding import PartitionSpec as P

HEADS = 12
HEAD_DIM = 64
FF = 3072
SEG_TOK = 512
MEM = 10
STEP = 10

highest = lax.Precision.HIGHEST
beta_one = 0.9
beta_two = 0.95
adam_eps = 1e-08
norm_eps = 1e-12
rate_matrix = 0.05
rate_vector = 0.1
rate_shared = 0.75

BF = jnp.bfloat16
F32 = jnp.float32
VMEM_LIMIT = 56 * 1024 * 1024
VMEM_SPEC = pl.BlockSpec(memory_space=pltpu.VMEM)
SMEM_SPEC = pl.BlockSpec(memory_space=pltpu.SMEM)
ANY_SPEC = pl.BlockSpec(memory_space=pl.ANY)
GROUP = 4
TILES = 3
RP = 144
AG_ORDER = (0, 1, 3, 2)
RS_ORDER = (2, 3, 1, 0)


def sds(shape, dtype):
    return jax.ShapeDtypeStruct(shape, dtype)


def params(**kw):
    return pltpu.CompilerParams(vmem_limit_bytes=VMEM_LIMIT, **kw)


def xor_pairs(size, step):
    return [(i, i ^ step) for i in range(size)]


def pack_plain(blocks):
    lead = blocks.shape[:-3]
    grp = blocks.reshape(lead + (-1, GROUP, 96, 96))
    last = jnp.swapaxes(grp[..., 3, :, :].reshape(lead + (-1, 96, 3, 32)), -3, -2)
    return jnp.concatenate([grp[..., :3, :, :], last], axis=-1)


def unpack_plain(groups):
    last = jnp.swapaxes(groups[..., 96:], -3, -2)
    last = last.reshape(groups.shape[:-3] + (1, 96, 96))
    grp = jnp.concatenate([groups[..., :96], last], axis=-3)
    return grp.reshape(groups.shape[:-4] + (-1, 96, 96))


def pack_body(m_ref, out_ref):
    for g in range(out_ref.shape[0]):
        last = m_ref[GROUP * g + 3].astype(BF)
        for k in range(TILES):
            out_ref[g, k] = jnp.concatenate(
                [m_ref[GROUP * g + k].astype(BF), last[:, 32 * k : 32 * k + 32]], axis=-1
            )


def pack_owned(blocks):
    n = blocks.shape[0] // GROUP
    return pl.pallas_call(
        pack_body,
        out_shape=sds((n, TILES, 96, 128), BF),
        in_specs=[VMEM_SPEC],
        out_specs=VMEM_SPEC,
        compiler_params=params(),
        name="pack_owned",
    )(blocks)


def weights_body(n_pieces, places, pos_ref, me_ref, *refs):
    pieces = refs[:n_pieces]
    wqkv_ref, wo_ref, w1_ref, w2_ref, al, sem = refs[n_pieces:]
    dp, t = me_ref[0], me_ref[1]
    copies = []
    for ref, (jt, jd, first) in zip(pieces, places):
        n = ref.shape[-4]
        if jd is None:
            copy = pltpu.make_async_copy(ref, al.at[:, :, pl.ds(0, TILES)], sem)
        else:
            base = (dp ^ jd) * (al.shape[1] // 8) + first
            copy = pltpu.make_async_copy(
                ref, al.at[t ^ jt, pl.ds(base, n), pl.ds(0, TILES)], sem
            )
        copy.start()
        copies.append(copy)
    for copy in copies:
        copy.wait()
    groups = al.shape[1]

    for s in range(4):

        def fix(g, carry, s=s):
            al[s, g, 3, :, 0:96] = jnp.concatenate(
                [al[s, g, k, :, 96:128] for k in range(TILES)], axis=-1
            )
            return carry

        lax.fori_loop(0, groups, fix, 0, unroll=8)

    def block(s, b):
        p = pos_ref[b]
        return al[s, p // GROUP, p % GROUP][:, :96]

    def strip(i, carry):
        rows = pl.ds(pl.multiple_of(i * 96, 96), 96)
        for part in range(3):
            for half in range(2):
                col = part * 768 + half * 384
                wqkv_ref[rows, col : col + 384] = jnp.concatenate(
                    [block(2 * half + j // 2, i * 6 + part * 2 + j % 2) for j in range(4)],
                    axis=-1,
                )
        for s in range(4):
            for half in range(2):
                w1_ref[rows, s * 768 + half * 384 : s * 768 + half * 384 + 384] = jnp.concatenate(
                    [block(s, 64 + i * 8 + half * 4 + j) for j in range(4)], axis=-1
                )
                lower = pl.ds(pl.multiple_of(s * 768 + i * 96, 96), 96)
                w2_ref[lower, half * 384 : half * 384 + 384] = jnp.concatenate(
                    [block(s, 128 + i * 8 + half * 4 + j) for j in range(4)], axis=-1
                )
        for half in range(2):
            wo_ref[rows, half * 384 : half * 384 + 384] = jnp.concatenate(
                [block(i // 2, 48 + (i % 2) * 8 + half * 4 + j) for j in range(4)], axis=-1
            )
        return carry

    lax.fori_loop(0, 8, strip, 0)


def build_weights(pos, me, pieces, places, slots):
    return pl.pallas_call(
        functools.partial(weights_body, len(pieces), places),
        out_shape=(
            sds((768, 2304), BF),
            sds((768, 768), BF),
            sds((768, 3072), BF),
            sds((3072, 768), BF),
        ),
        in_specs=[SMEM_SPEC, SMEM_SPEC] + [ANY_SPEC] * len(pieces),
        out_specs=(VMEM_SPEC,) * 4,
        scratch_shapes=[
            pltpu.VMEM((4, slots // GROUP, GROUP, 96, 128), BF),
            pltpu.SemaphoreType.DMA,
        ],
        compiler_params=params(),
        name="build_weights",
    )(pos, me, *pieces)


def grads_body(places, pos_ref, me_ref, gq_ref, go_ref, g1_ref, g2_ref, *refs):
    outs = refs[: len(places)]
    al, sem = refs[len(places) :]
    groups = al.shape[1]

    def put(s, b, blk):
        p = pos_ref[b]
        al[s, p // GROUP, p % GROUP, :, 0:96] = blk

    def strip(i, carry):
        rows = pl.ds(pl.multiple_of(i * 96, 96), 96)
        for s in range(2):
            strip_q = gq_ref[s, rows, :]
            for j in range(6):
                put(s, i * 6 + j, strip_q[:, 96 * j : 96 * j + 96])
            for ref, first in ((g1_ref, 64), (g2_ref, 128)):
                for half in range(2):
                    vals = ref[s, rows, half * 384 : half * 384 + 384]
                    for j in range(4):
                        put(s, first + i * 8 + half * 4 + j, vals[:, 96 * j : 96 * j + 96])
        return carry

    lax.fori_loop(0, 8, strip, 0)
    for i in range(2):
        for s in range(2):
            for half in range(2):
                vals = go_ref[s, i * 96 : i * 96 + 96, half * 384 : half * 384 + 384]
                for j in range(4):
                    put(s, 48 + i * 8 + half * 4 + j, vals[:, 96 * j : 96 * j + 96])
    for s in range(2):

        def fix(g, carry, s=s):
            last = al[s, g, 3]
            for k in range(TILES):
                al[s, g, k, :, 96:128] = last[:, 32 * k : 32 * k + 32]
            return carry

        lax.fori_loop(0, groups, fix, 0, unroll=8)

    dp, y = me_ref[0], me_ref[1] // 2
    copies = []
    for ref, (jy, jd, first) in zip(outs, places):
        if jd is None:
            copy = pltpu.make_async_copy(al.at[:, :, pl.ds(0, TILES)], ref, sem)
        else:
            base = (dp ^ jd) * (groups // 8) + first
            copy = pltpu.make_async_copy(
                al.at[y ^ jy, pl.ds(base, ref.shape[0]), pl.ds(0, TILES)], ref, sem
            )
        copy.start()
        copies.append(copy)
    for copy in copies:
        copy.wait()


def pack_grads(pos, me, gq, go, g1, g2, places, out_shapes, slots):
    return pl.pallas_call(
        functools.partial(grads_body, places),
        out_shape=tuple(sds(s, BF) for s in out_shapes),
        in_specs=[SMEM_SPEC, SMEM_SPEC] + [VMEM_SPEC] * 4,
        out_specs=(ANY_SPEC,) * len(places),
        scratch_shapes=[
            pltpu.VMEM((2, slots // GROUP, GROUP, 96, 128), BF),
            pltpu.SemaphoreType.DMA,
        ],
        compiler_params=params(),
        name="pack_grads",
    )(pos, me, gq, go, g1, g2)


def attend_body(cq_ref, ck_ref, q_ref, ka_ref, va_ref, kb_ref, vb_ref, ctx_ref, p_ref, vis):
    @pl.when(pl.program_id(0) == 0)
    def _():
        cq, ck = cq_ref[...], ck_ref[...]
        seen = ((cq == -1) | (ck == -1) | (cq == ck)) & (ck != -2)
        vis[...] = jnp.where(seen, 1.0, 0.0)

    q = q_ref[...]
    k = jnp.concatenate([ka_ref[...], kb_ref[...]], axis=0)
    v = jnp.concatenate([va_ref[...], vb_ref[...]], axis=0)
    lane = lax.broadcasted_iota(jnp.int32, q.shape, 1)
    outs = []
    for h in range(2):
        mine = (lane < HEAD_DIM) if h == 0 else (lane >= HEAD_DIM)
        qh = jnp.where(mine, q, jnp.zeros_like(q))
        raw = lax.dot_general(qh, k, (((1,), (1,)), ((), ())), preferred_element_type=F32)
        scores = jnp.where(vis[...] > 0.5, raw * HEAD_DIM ** (-0.5), -1000000000.0)
        e = jnp.exp(scores - jnp.max(scores, axis=-1, keepdims=True))
        p = (e / jnp.sum(e, axis=-1, keepdims=True)).astype(BF)
        p_ref[h] = p
        outs.append(jnp.dot(p, v, preferred_element_type=F32))
    ctx_ref[...] = jnp.where(lane < HEAD_DIM, outs[0], outs[1]).astype(BF)


def attend(code_q, code_k, proj, kv_other):
    rows = proj.shape[0]
    pairs = HEADS // 2

    def col(off):
        return pl.BlockSpec((rows, 128), lambda h: (0, h + off))

    return pl.pallas_call(
        attend_body,
        grid=(pairs,),
        out_shape=(sds((rows, 768), BF), sds((HEADS, rows, 2 * rows), BF)),
        in_specs=[
            pl.BlockSpec((rows, 1), lambda h: (0, 0)),
            pl.BlockSpec((1, 2 * rows), lambda h: (0, 0)),
            col(0),
            col(pairs),
            col(2 * pairs),
            col(0),
            col(pairs),
        ],
        out_specs=(col(0), pl.BlockSpec((2, rows, 2 * rows), lambda h: (h, 0, 0))),
        scratch_shapes=[pltpu.VMEM((rows, 2 * rows), F32)],
        compiler_params=params(),
        name="attend",
    )(code_q, code_k, proj, proj, proj, kv_other, kv_other)


def attend_back_body(
    dc_ref, p_ref, q_ref, ka_ref, va_ref, kb_ref, vb_ref, dq_ref, dka_ref, dva_ref, dkb_ref, dvb_ref
):
    q, dc = q_ref[...], dc_ref[...]
    rows = q.shape[0]
    k = jnp.concatenate([ka_ref[...], kb_ref[...]], axis=0)
    v = jnp.concatenate([va_ref[...], vb_ref[...]], axis=0)
    lane = lax.broadcasted_iota(jnp.int32, q.shape, 1)
    lane_all = lax.broadcasted_iota(jnp.int32, k.shape, 1)
    dqs, dks, dvs = [], [], []
    for h in range(2):
        mine = (lane < HEAD_DIM) if h == 0 else (lane >= HEAD_DIM)
        dch = jnp.where(mine, dc, jnp.zeros_like(dc))
        p = p_ref[h]
        dvs.append(lax.dot_general(p, dc, (((0,), (0,)), ((), ())), preferred_element_type=F32))
        dp = lax.dot_general(dch, v, (((1,), (1,)), ((), ())), preferred_element_type=F32)
        pf = p.astype(F32)
        row = jnp.sum(dp * pf, axis=-1, keepdims=True)
        ds = (pf * (dp - row) * HEAD_DIM ** (-0.5)).astype(BF)
        dqs.append(jnp.dot(ds, k, preferred_element_type=F32))
        dks.append(lax.dot_general(ds, q, (((0,), (0,)), ((), ())), preferred_element_type=F32))
    dq_ref[...] = jnp.where(lane < HEAD_DIM, dqs[0], dqs[1])
    dk = jnp.where(lane_all < HEAD_DIM, dks[0], dks[1])
    dv = jnp.where(lane_all < HEAD_DIM, dvs[0], dvs[1])
    dka_ref[...] = dk[:rows]
    dkb_ref[...] = dk[rows:]
    dva_ref[...] = dv[:rows]
    dvb_ref[...] = dv[rows:]


def attend_back(dctx, probs, proj, kv_other):
    rows = proj.shape[0]
    pairs = HEADS // 2

    def col(off):
        return pl.BlockSpec((rows, 128), lambda h: (0, h + off))

    return pl.pallas_call(
        attend_back_body,
        grid=(pairs,),
        out_shape=(sds((rows, 768), F32),) * 5,
        in_specs=[
            col(0),
            pl.BlockSpec((2, rows, 2 * rows), lambda h: (h, 0, 0)),
            col(0),
            col(pairs),
            col(2 * pairs),
            col(0),
            col(pairs),
        ],
        out_specs=(col(0),) * 5,
        compiler_params=params(),
        name="attend_back",
    )(dctx, probs, proj, proj, proj, kv_other, kv_other)


def norm_parts(values, gain_vec, shift_vec):
    centred = values - jnp.mean(values, axis=-1, keepdims=True)
    inverse = lax.rsqrt(jnp.mean(centred * centred, axis=-1, keepdims=True) + norm_eps)
    normed = centred * inverse
    return (normed * gain_vec + shift_vec, normed, inverse)


def norm_back(upstream, normed, inverse, gain_vec):
    scaled = upstream * gain_vec
    result = inverse * (
        scaled
        - jnp.mean(scaled, axis=-1, keepdims=True)
        - normed * jnp.mean(scaled * normed, axis=-1, keepdims=True)
    )
    return (result, jnp.sum(upstream * normed, axis=0), jnp.sum(upstream, axis=0))


def dot(left, right):
    return jnp.dot(left, right, preferred_element_type=F32)


def dot_back(left, right):
    return lax.dot_general(left, right, (((1,), (1,)), ((), ())), preferred_element_type=F32)


def inner_rows(left, right):
    return lax.dot_general(left, right, (((0,), (0,)), ((), ())), preferred_element_type=F32)


def soap_update(weight, grad, first_mom, second_mom, left_stat, right_stat, left_rot, right_rot):
    turned = jnp.einsum("...ia,...ij->...aj", left_rot, grad, precision=highest)
    turned = jnp.einsum("...aj,...jb->...ab", turned, right_rot, precision=highest)
    new_first = beta_one * first_mom + (1.0 - beta_one) * turned
    new_second = beta_two * second_mom + (1.0 - beta_two) * turned * turned
    direction = (
        new_first
        / (1.0 - beta_one**STEP)
        / (jnp.sqrt(new_second / (1.0 - beta_two**STEP)) + adam_eps)
    )
    back = jnp.einsum("...ia,...ab->...ib", left_rot, direction, precision=highest)
    back = jnp.einsum("...ib,...jb->...ij", back, right_rot, precision=highest)
    new_weight = weight - rate_matrix * back
    new_left = beta_two * left_stat + (1.0 - beta_two) * jnp.einsum(
        "...ik,...jk->...ij", grad, grad, precision=highest
    )
    new_right = beta_two * right_stat + (1.0 - beta_two) * jnp.einsum(
        "...ki,...kj->...ij", grad, grad, precision=highest
    )
    return (new_weight, new_first, new_second, new_left, new_right)


def adam_update(values, grad_vec, first_mom, second_mom, step_rate):
    new_first = beta_one * first_mom + (1.0 - beta_one) * grad_vec
    new_second = beta_two * second_mom + (1.0 - beta_two) * grad_vec * grad_vec
    direction = (
        new_first
        / (1.0 - beta_one**STEP)
        / (jnp.sqrt(new_second / (1.0 - beta_two**STEP)) + adam_eps)
    )
    return (values - step_rate * direction, new_first, new_second)


def per_device(
    n_dp,
    n_tensor,
    layer_in,
    cotangent,
    doc_ids,
    reset_flags,
    block_slot,
    master,
    first_moment,
    second_moment,
    left_stats,
    right_stats,
    left_basis,
    right_basis,
    split_params,
    split_first,
    split_second,
    shared,
    shared_first,
    shared_second,
):
    meshed = n_dp == 8 and master.shape[1] % GROUP == 0
    dp = lax.axis_index("dp")
    t = lax.axis_index("tensor")
    y, c = t // 2, t % 2
    me = jnp.stack([dp, t])
    slots = block_slot.shape[0]
    quarter = layer_in.shape[1]

    def swap(axis, step):
        size = n_dp if axis == "dp" else n_tensor
        return lambda v: lax.ppermute(v, axis, xor_pairs(size, step))

    core, yswap, xswap = swap("tensor", 1), swap("tensor", 2), swap("dp", 1)

    def two_quarters(arr):
        other = yswap(lax.dynamic_index_in_dim(arr, 1 - y, 0, keepdims=False))
        mine = lax.dynamic_index_in_dim(arr, y, 0, keepdims=False)
        return mine, other

    def pad_rows(arr):
        return jnp.pad(arr, ((0, RP - quarter), (0, 0)))

    in_mine, in_other = two_quarters(layer_in)

    if meshed:
        own = pack_owned(master[0])
        half = own.shape[0] // 2
        pieces, places = [], []
        for jz in AG_ORDER:
            unit = own if jz == 0 else swap("dp", 2 * jz)(own)
            x_unit, y_unit = xswap(unit), yswap(unit)
            diag_a, diag_b = yswap(x_unit[:half]), xswap(y_unit[half:])
            for val, jy, jx, first in (
                (unit, 0, 0, 0),
                (x_unit, 0, 1, 0),
                (y_unit, 1, 0, 0),
                (diag_a, 1, 1, 0),
                (diag_b, 1, 1, half),
            ):
                for jc in range(2):
                    pieces.append(val if jc == 0 else core(val))
                    places.append((2 * jy + jc, 2 * jz + jx, first))
    else:
        every = lax.all_gather(master.astype(BF), "dp", axis=1, tiled=True)
        every = lax.all_gather(every, "tensor", axis=0, tiled=True)
        pieces, places = [pack_plain(every)], [(0, None, 0)]
    w_qkv, w_out, w_up, w_down = build_weights(block_slot, me, pieces, tuple(places), slots)

    pair = jnp.concatenate([split_params, core(split_params)], axis=0)
    quad = jnp.concatenate([pair, yswap(pair)], axis=0)
    quad = jnp.take(quad, jnp.arange(4) ^ t, axis=0)
    qb, vb, up_bias = (quad[:, :192].reshape(-1), quad[:, 192:384].reshape(-1), quad[:, 384:].reshape(-1))
    qkv_bias = jnp.concatenate([qb, jnp.zeros_like(qb), vb])
    attn_bias, gain_one, shift_one = (shared[0], shared[1], shared[2])
    ffn_bias, gain_two, shift_two = (shared[3], shared[4], shared[5])

    docs = lax.dynamic_index_in_dim(doc_ids, y, 0, keepdims=False)
    edge = jnp.full((MEM,), -1, jnp.int32)
    codes = jnp.concatenate([edge, docs, edge]).reshape(4, quarter)
    codes = jnp.pad(codes, ((0, 0), (0, RP - quarter)), constant_values=-2)
    codes = jnp.take(codes, t ^ jnp.array([0, 2, 1, 3]), axis=0).reshape(-1)
    code_q, code_k = codes[: 2 * RP, None], codes[None, :]

    reset_now = lax.dynamic_index_in_dim(reset_flags, y, 0, keepdims=False) == 1
    has_read = (c == 0) & reset_now
    row = jnp.arange(2 * RP)
    replaced = ((row - y * RP >= 0) & (row - y * RP < MEM) & has_read)[:, None]
    memory_rows = jnp.pad(shared[6:], ((0, RP - MEM), (0, 0)))
    memory_rows = jnp.concatenate([memory_rows, memory_rows], axis=0)
    x_zero = jnp.where(
        replaced,
        memory_rows,
        jnp.concatenate([pad_rows(in_mine), pad_rows(in_other)], axis=0).astype(F32),
    )
    x_in = x_zero.astype(BF)

    proj = (dot(x_in, w_qkv) + qkv_bias).astype(BF)
    kv_other = core(proj[:, 768:])
    context, probs = attend(code_q, code_k, proj, kv_other)
    h_one, normed_one, inverse_one = norm_parts(
        dot(context, w_out) + attn_bias + x_zero, gain_one, shift_one
    )
    h_in = h_one.astype(BF)
    pre = dot(h_in, w_up) + up_bias
    cdf = 0.5 * (1.0 + lax.erf(pre * 0.7071067811865476))
    act = (pre * cdf).astype(BF)
    slope = cdf + pre * jnp.exp(-0.5 * pre * pre) * 0.3989422804014327
    rows_out, normed_two, inverse_two = norm_parts(
        dot(act, w_down) + ffn_bias + h_one, gain_two, shift_two
    )

    def to_owner(arr):
        mine, other = arr[:quarter], yswap(arr[RP : RP + quarter])
        both = jnp.stack([mine, other])
        return jnp.where(y == 0, both, both[::-1])

    layer_out = to_owner(rows_out.astype(BF))

    cot_mine, cot_other = two_quarters(cotangent)
    grad_out = jnp.concatenate([pad_rows(cot_mine), pad_rows(cot_other)], axis=0).astype(F32)
    d_two, gain_two_g, shift_two_g = norm_back(grad_out, normed_two, inverse_two, gain_two)
    d_two_b = d_two.astype(BF)
    d_pre = dot_back(d_two_b, w_down) * slope
    d_pre_b = d_pre.astype(BF)
    d_hidden = dot_back(d_pre_b, w_up) + d_two
    d_one, gain_one_g, shift_one_g = norm_back(d_hidden, normed_one, inverse_one, gain_one)
    d_one_b = d_one.astype(BF)
    d_context = dot_back(d_one_b, w_out).astype(BF)
    d_q, dk_a, dv_a, dk_b, dv_b = attend_back(d_context, probs, proj, kv_other)
    back = core(jnp.concatenate([dk_b, dv_b], axis=1).astype(BF)).astype(F32)
    d_proj = jnp.concatenate([d_q, dk_a + back[:, :768], dv_a + back[:, 768:]], axis=1).astype(BF)
    d_zero = dot_back(d_proj, w_qkv) + d_one
    grad_in = to_owner(jnp.where(replaced, 0.0, d_zero).astype(BF))
    memory_grad = lax.dynamic_slice_in_dim(d_zero, y * RP, MEM, 0)
    memory_grad = jnp.where(has_read, memory_grad, 0.0)

    def both_rows(arr):
        return jnp.concatenate([arr, core(arr)], axis=0)

    def own_slices(arr, width):
        parts = arr.reshape(arr.shape[0], -1, 2, 2, width)
        mine = lax.dynamic_index_in_dim(parts, c, 3, keepdims=False)
        other = core(lax.dynamic_index_in_dim(parts, 1 - c, 3, keepdims=False))
        parts = jnp.concatenate([mine, other], axis=0)
        return [parts[:, :, k].reshape(parts.shape[0], -1) for k in range(2)]

    x_rows, h_rows, d2_rows, d1_rows = (both_rows(v) for v in (x_in, h_in, d_two_b, d_one_b))
    act_s, dpre_s = own_slices(act, 768), own_slices(d_pre_b, 768)
    ctx_s, dproj_s = own_slices(context, 192), own_slices(d_proj, 192)
    g_down = jnp.stack([inner_rows(act_s[k], d2_rows).astype(BF) for k in range(2)])
    g_up = jnp.stack([inner_rows(h_rows, dpre_s[k]).astype(BF) for k in range(2)])
    g_out = jnp.stack([inner_rows(ctx_s[k], d1_rows).astype(BF) for k in range(2)])
    g_qkv = jnp.stack([inner_rows(x_rows, dproj_s[k]).astype(BF) for k in range(2)])

    if meshed:
        per = master.shape[1] // GROUP
        half = per // 2
        places, shapes = [], []
        for jz in RS_ORDER:
            for jy, jx, first, n in ((0, 0, 0, per), (0, 1, 0, per), (1, 0, 0, per), (1, 1, 0, half), (1, 1, half, per - half)):
                places.append((jy, 2 * jz + jx, first))
                shapes.append((n, TILES, 96, 128))
        packed = pack_grads(block_slot, me, g_qkv, g_out, g_up, g_down, tuple(places), shapes, slots)

        def plus(a, b):
            return (a.astype(F32) + b.astype(F32)).astype(BF)

        total = None
        for n, jz in enumerate(RS_ORDER):
            own, x_unit, y_unit, diag_a, diag_b = packed[5 * n : 5 * n + 5]
            from_y, from_x = yswap(diag_a), xswap(diag_b)
            x_unit = jnp.concatenate([plus(x_unit[:half], from_y), x_unit[half:]], axis=0)
            y_unit = jnp.concatenate([y_unit[:half], plus(y_unit[half:], from_x)], axis=0)
            part = own.astype(F32) + xswap(x_unit).astype(F32) + yswap(y_unit).astype(F32)
            if jz:
                part = swap("dp", 2 * jz)(part.astype(BF)).astype(F32)
            total = part if total is None else total + part
        owned = unpack_plain(total)
    else:
        packed = pack_grads(
            block_slot,
            me,
            g_qkv,
            g_out,
            g_up,
            g_down,
            ((0, None, 0),),
            [(2, slots // GROUP, TILES, 96, 128)],
            slots,
        )[0]
        blocks = unpack_plain(packed)
        blocks = lax.psum_scatter(blocks, "dp", scatter_dimension=1, tiled=True)
        mine = lax.dynamic_index_in_dim(blocks, y, 0, keepdims=False)
        other = yswap(lax.dynamic_index_in_dim(blocks, 1 - y, 0, keepdims=False))
        owned = mine.astype(F32) + other.astype(F32)

    vec = jnp.concatenate(
        [
            jnp.stack(
                [
                    jnp.sum(d_one, axis=0),
                    gain_one_g,
                    shift_one_g,
                    jnp.sum(d_two, axis=0),
                    gain_two_g,
                    shift_two_g,
                ]
            ),
            memory_grad,
            jnp.sum(d_q, axis=0)[None],
            (jnp.sum(dv_a, axis=0) + jnp.sum(dv_b, axis=0))[None],
            jnp.sum(d_pre, axis=0).reshape(4, 768),
        ],
        axis=0,
    )
    for axis, size in (("tensor", n_tensor), ("dp", n_dp)):
        step = 1
        while step < size:
            vec = vec + swap(axis, step)(vec)
            step *= 2
    total_shared = vec[:16]
    grad_split = jnp.concatenate(
        [
            lax.dynamic_slice_in_dim(vec[16], t * 192, 192, 0),
            lax.dynamic_slice_in_dim(vec[17], t * 192, 192, 0),
            lax.dynamic_index_in_dim(vec[18:], t, 0, keepdims=False),
        ]
    )[None]

    new_master, new_first, new_second, new_left, new_right = soap_update(
        master[0],
        owned,
        first_moment[0],
        second_moment[0],
        left_stats[0],
        right_stats[0],
        left_basis[0],
        right_basis[0],
    )
    new_split, new_split_first, new_split_second = adam_update(
        split_params, grad_split, split_first, split_second, rate_vector
    )
    new_shared, new_shared_first, new_shared_second = adam_update(
        shared, total_shared, shared_first, shared_second, rate_shared
    )
    return (
        layer_out,
        grad_in,
        new_master[None],
        new_master[None].astype(BF),
        new_first[None],
        new_second[None],
        new_left[None],
        new_right[None],
        new_split,
        new_split_first,
        new_split_second,
        new_shared,
        new_shared_first,
        new_shared_second,
    )


def solution(mesh):
    rows = P("dp", "tensor", None)
    state = P("tensor", "dp", None, None)
    split = P("tensor", None)
    return jax.shard_map(
        functools.partial(per_device, mesh.shape["dp"], mesh.shape["tensor"]),
        mesh=mesh,
        in_specs=(rows, rows, P("dp", None), P("dp"), P()) + (state,) * 7 + (split,) * 3 + (P(),) * 3,
        out_specs=(rows, rows) + (state,) * 6 + (split,) * 3 + (P(),) * 3,
        check_vma=False,
    )
```

```python
import functools

import jax
import jax.numpy as jnp
from jax import lax
from jax.experimental import pallas as pl
from jax.experimental.pallas import tpu as pltpu
from jax.sharding import PartitionSpec as P

HEADS = 12
HEAD_DIM = 64
FF = 3072
SEG_TOK = 512
MEM = 10
STEP = 10

beta_one = 0.9
beta_two = 0.95
adam_eps = 1e-08
norm_eps = 1e-12
rate_matrix = 0.05
rate_vector = 0.1
rate_shared = 0.75

BF = jnp.bfloat16
F32 = jnp.float32
VMEM_LIMIT = 56 * 1024 * 1024
VMEM_SPEC = pl.BlockSpec(memory_space=pltpu.VMEM)
SMEM_SPEC = pl.BlockSpec(memory_space=pltpu.SMEM)
ANY_SPEC = pl.BlockSpec(memory_space=pl.ANY)
GROUP = 4
TILES = 3
RP = 144
RS_ORDER = (3, 2, 1, 0)


def sds(shape, dtype):
    return jax.ShapeDtypeStruct(shape, dtype)


def params(**kw):
    return pltpu.CompilerParams(vmem_limit_bytes=VMEM_LIMIT, **kw)


def after(vals, deps):
    return lax.optimization_barrier((vals, deps))[0]


def cost(gflop, mbytes):
    return pl.CostEstimate(
        flops=int(gflop * 1e9), bytes_accessed=int(mbytes * 1e6), transcendentals=0
    )


def xor_pairs(size, step):
    return [(i, i ^ step) for i in range(size)]


def z_pairs(pairs):
    return [(2 * a + x, 2 * b + x) for a, b in pairs for x in range(2)]


def pack_plain(blocks):
    lead = blocks.shape[:-3]
    grp = blocks.reshape(lead + (-1, GROUP, 96, 96))
    last = jnp.swapaxes(grp[..., 3, :, :].reshape(lead + (-1, 96, 3, 32)), -3, -2)
    return jnp.concatenate([grp[..., :3, :, :], last], axis=-1)


def unpack_plain(groups):
    last = jnp.swapaxes(groups[..., 96:], -3, -2)
    last = last.reshape(groups.shape[:-3] + (1, 96, 96))
    grp = jnp.concatenate([groups[..., :96], last], axis=-3)
    return grp.reshape(groups.shape[:-4] + (-1, 96, 96))


def pack_body(m_ref, out_ref):
    for g in range(out_ref.shape[0]):
        last = m_ref[GROUP * g + 3].astype(BF)
        for k in range(TILES):
            out_ref[g, k] = jnp.concatenate(
                [m_ref[GROUP * g + k].astype(BF), last[:, 32 * k : 32 * k + 32]], axis=-1
            )


def pack_owned(blocks):
    n = blocks.shape[0] // GROUP
    return pl.pallas_call(
        pack_body,
        out_shape=sds((n, TILES, 96, 128), BF),
        in_specs=[VMEM_SPEC],
        out_specs=VMEM_SPEC,
        compiler_params=params(),
        cost_estimate=cost(0.1, 2),
        name="pack_owned",
    )(blocks)


def weights_body(n_pieces, places, pos_ref, me_ref, *refs):
    pieces = refs[:n_pieces]
    wqkv_ref, wo_ref, w1_ref, w2_ref, al, sem = refs[n_pieces:]
    dp, y = me_ref[0], me_ref[1] // 2
    copies = []
    for ref, (jy, jd) in zip(pieces, places):
        n = ref.shape[-4]
        if jd is None:
            copy = pltpu.make_async_copy(ref, al.at[:, :, pl.ds(0, TILES)], sem)
        else:
            copy = pltpu.make_async_copy(
                ref, al.at[y ^ jy, pl.ds((dp ^ jd) * n, n), pl.ds(0, TILES)], sem
            )
        copy.start()
        copies.append(copy)
    for copy in copies:
        copy.wait()
    groups = al.shape[1]

    for s in range(2):

        def fix(g, carry, s=s):
            al[s, g, 3, :, 0:96] = jnp.concatenate(
                [al[s, g, k, :, 96:128] for k in range(TILES)], axis=-1
            )
            return carry

        lax.fori_loop(0, groups, fix, 0, unroll=8)

    def block(s, b):
        p = pos_ref[b]
        return al[s, p // GROUP, p % GROUP][:, :96]

    def strip(i, carry):
        rows = pl.ds(pl.multiple_of(i * 96, 96), 96)
        for part in range(3):
            wqkv_ref[rows, part * 384 : part * 384 + 384] = jnp.concatenate(
                [block(j // 2, i * 6 + part * 2 + j % 2) for j in range(4)], axis=-1
            )
        for s in range(2):
            for half in range(2):
                cols = slice(half * 384, half * 384 + 384)
                w1_ref[s, rows, cols] = jnp.concatenate(
                    [block(s, 64 + i * 8 + half * 4 + j) for j in range(4)], axis=-1
                )
                w2_ref[s, rows, cols] = jnp.concatenate(
                    [block(s, 128 + i * 8 + half * 4 + j) for j in range(4)], axis=-1
                )
        return carry

    lax.fori_loop(0, 8, strip, 0, unroll=2)
    for i in range(4):
        for half in range(2):
            wo_ref[i * 96 : i * 96 + 96, half * 384 : half * 384 + 384] = jnp.concatenate(
                [block(i // 2, 48 + (i % 2) * 8 + half * 4 + j) for j in range(4)], axis=-1
            )


def build_weights(pos, me, pieces, places, slots):
    return pl.pallas_call(
        functools.partial(weights_body, len(pieces), places),
        out_shape=(
            sds((768, 1152), BF),
            sds((384, 768), BF),
            sds((2, 768, 768), BF),
            sds((2, 768, 768), BF),
        ),
        in_specs=[SMEM_SPEC, SMEM_SPEC] + [ANY_SPEC] * len(pieces),
        out_specs=(VMEM_SPEC,) * 4,
        scratch_shapes=[
            pltpu.VMEM((2, slots // GROUP, GROUP, 96, 128), BF),
            pltpu.SemaphoreType.DMA,
        ],
        compiler_params=params(),
        cost_estimate=cost(0.1, 30),
        name="build_weights",
    )(pos, me, *pieces)


def product(left, right, out, width=256):
    def step(i, carry):
        col = pl.multiple_of(i * width, width)
        out[pl.ds(col, width), :] = inner_rows(left[:, pl.ds(col, width)], right[...]).astype(BF)
        return carry

    lax.fori_loop(0, out.shape[0] // width, step, 0)


def feed_grads_body(act_ref, d2_ref, h_ref, dpre_ref, g1_ref, g2_ref):
    for s in range(2):
        product(act_ref.at[s], d2_ref, g2_ref.at[s])
        product(h_ref, dpre_ref.at[s], g1_ref.at[s])


def feed_grads(act, d_two, h_in, d_pre):
    rows = h_in.shape[0]
    return pl.pallas_call(
        feed_grads_body,
        out_shape=(sds((2, 768, 768), BF),) * 2,
        in_specs=[VMEM_SPEC] * 4,
        out_specs=(VMEM_SPEC,) * 2,
        compiler_params=params(),
        cost_estimate=pl.CostEstimate(
            flops=2 * rows * 768 * 768 * 4, bytes_accessed=10 * 1024 * 1024, transcendentals=0
        ),
        name="feed_grads",
    )(act, d_two, h_in, d_pre)


def grads_body(places, pos_ref, me_ref, *refs):
    x, dproj, ctx, d1, g1, g2 = refs[:6]
    outs = refs[6 : 6 + len(places)]
    gq, go, al, sem = refs[6 + len(places) :]
    groups = al.shape[1]
    product(ctx, d1, go, 128)
    product(x, dproj, gq)

    def put(s, b, blk):
        p = pos_ref[b]
        al[s, p // GROUP, p % GROUP, :, 0:96] = blk

    def strip(i, carry):
        rows = pl.ds(pl.multiple_of(i * 96, 96), 96)
        for part in range(3):
            vals = gq[rows, part * 384 : part * 384 + 384]
            for j in range(4):
                put(j // 2, i * 6 + part * 2 + j % 2, vals[:, 96 * j : 96 * j + 96])
        for s in range(2):
            for ref, first in ((g1, 64), (g2, 128)):
                for half in range(2):
                    vals = ref[s, rows, half * 384 : half * 384 + 384]
                    for j in range(4):
                        put(s, first + i * 8 + half * 4 + j, vals[:, 96 * j : 96 * j + 96])
        return carry

    lax.fori_loop(0, 8, strip, 0, unroll=2)
    for i in range(4):
        for half in range(2):
            vals = go[i * 96 : i * 96 + 96, half * 384 : half * 384 + 384]
            for j in range(4):
                put(i // 2, 48 + (i % 2) * 8 + half * 4 + j, vals[:, 96 * j : 96 * j + 96])
    for s in range(2):

        def fix(g, carry, s=s):
            last = al[s, g, 3]
            for k in range(TILES):
                al[s, g, k, :, 96:128] = last[:, 32 * k : 32 * k + 32]
            return carry

        lax.fori_loop(0, groups, fix, 0, unroll=8)

    dp, y = me_ref[0], me_ref[1] // 2
    copies = []
    for ref, (jy, jd, first) in zip(outs, places):
        if jd is None:
            copy = pltpu.make_async_copy(al.at[:, :, pl.ds(0, TILES)], ref, sem)
        else:
            base = (dp ^ jd) * (groups // 8) + first
            copy = pltpu.make_async_copy(
                al.at[y ^ jy, pl.ds(base, ref.shape[0]), pl.ds(0, TILES)], ref, sem
            )
        copy.start()
        copies.append(copy)
    for copy in copies:
        copy.wait()


def weight_grads(pos, me, srcs, places, out_shapes, slots):
    return pl.pallas_call(
        functools.partial(grads_body, places),
        out_shape=tuple(sds(s, BF) for s in out_shapes),
        in_specs=[SMEM_SPEC, SMEM_SPEC] + [VMEM_SPEC] * 6,
        out_specs=(ANY_SPEC,) * len(places),
        scratch_shapes=[
            pltpu.VMEM((768, 1152), BF),
            pltpu.VMEM((384, 768), BF),
            pltpu.VMEM((2, slots // GROUP, GROUP, 96, 128), BF),
            pltpu.SemaphoreType.DMA,
        ],
        compiler_params=params(),
        cost_estimate=cost(2.0, 30),
        name="weight_grads",
    )(pos, me, *srcs)


def project_body(flags_ref, xa, xb, xc, xd, sh_ref, w_ref, b_ref, proj_ref, x0_ref, xin_ref, bias):
    @pl.when(pl.program_id(0) == 0)
    def _():
        n = xa.shape[0]
        gap = jnp.zeros((RP - n, x0_ref.shape[1]), F32)
        for k, ref in enumerate((xa, xb, xc, xd)):
            x0_ref[k * RP : k * RP + n, :] = ref[...].astype(F32)
            x0_ref[k * RP + n : k * RP + RP, :] = gap

            @pl.when((flags_ref[0] == k) & (flags_ref[1] == 1))
            def _(k=k):
                x0_ref[k * RP : k * RP + MEM, :] = sh_ref[6 : 6 + MEM, :]

        xin_ref[...] = x0_ref[...].astype(BF)
        for part, col in ((0, 0), (2, 192)):
            bias[part] = jnp.concatenate([b_ref[s : s + 1, col : col + 192] for s in range(2)], axis=1)
        bias[1] = jnp.zeros((1, 384), F32)

    proj_ref[...] = (dot(xin_ref[...], w_ref[...]) + bias[pl.program_id(0)]).astype(BF)


def project(flags, quarters, shared, w_qkv, biases):
    rows = 4 * RP

    def whole(shape):
        return pl.BlockSpec(shape, lambda i: (0, 0))

    return pl.pallas_call(
        project_body,
        grid=(3,),
        out_shape=(sds((rows, 1152), BF), sds((rows, 768), F32), sds((rows, 768), BF)),
        in_specs=[
            SMEM_SPEC,
            *[whole(q.shape) for q in quarters],
            whole(shared.shape),
            pl.BlockSpec((768, 384), lambda i: (0, i)),
            whole(biases.shape),
        ],
        out_specs=(
            pl.BlockSpec((rows, 384), lambda i: (0, i)),
            whole((rows, 768)),
            whole((rows, 768)),
        ),
        scratch_shapes=[pltpu.VMEM((3, 1, 384), F32)],
        compiler_params=params(),
        cost_estimate=cost(1.0, 5),
        name="project",
    )(flags, *quarters, shared, w_qkv, biases)


def head_masks(shape):
    lane = lax.broadcasted_iota(jnp.int32, shape, 1)
    return lane < HEAD_DIM, lane >= HEAD_DIM


def attend_body(cq_ref, ck_ref, q_ref, k_ref, v_ref, wo_ref, ctx_ref, p_ref, part_ref, vis):
    h = pl.program_id(0)

    @pl.when(h == 0)
    def _():
        cq, ck = cq_ref[...], ck_ref[...]
        seen = ((cq == -1) | (ck == -1) | (cq == ck)) & (ck != -2)
        vis[...] = jnp.where(seen, 1.0, 0.0)

    q, k, v = q_ref[...], k_ref[...], v_ref[...]
    masks = head_masks(q.shape)
    outs = []
    for n in range(2):
        qh = jnp.where(masks[n], q, jnp.zeros_like(q))
        scores = jnp.where(vis[...] > 0.5, dot_back(qh, k) * HEAD_DIM ** (-0.5), -1000000000.0)
        e = jnp.exp(scores - jnp.max(scores, axis=-1, keepdims=True))
        p = (e * (1.0 / jnp.sum(e, axis=-1, keepdims=True))).astype(BF)
        p_ref[n] = p
        outs.append(dot(p, v))
    ctx_ref[:, pl.ds(pl.multiple_of(h * 128, 128), 128)] = jnp.where(masks[0], outs[0], outs[1]).astype(BF)

    @pl.when(h == pl.num_programs(0) - 1)
    def _():
        part_ref[...] = dot(ctx_ref[...], wo_ref[...]).astype(BF)


def head_col(rows, off):
    return pl.BlockSpec((rows, 128), lambda h: (0, h + off))


def all_steps(shape):
    return pl.BlockSpec(shape, lambda h: (0,) * len(shape))


def attend(code_q, code_k, proj, w_out):
    rows = proj.shape[0]
    pairs = HEADS // 4
    return pl.pallas_call(
        attend_body,
        grid=(pairs,),
        out_shape=(sds((rows, 384), BF), sds((2 * pairs, rows, rows), BF), sds((rows, 768), BF)),
        in_specs=[
            all_steps((rows, 1)),
            all_steps((1, rows)),
            head_col(rows, 0),
            head_col(rows, pairs),
            head_col(rows, 2 * pairs),
            all_steps((384, 768)),
        ],
        out_specs=(
            all_steps((rows, 384)),
            pl.BlockSpec((2, rows, rows), lambda h: (h, 0, 0)),
            all_steps((rows, 768)),
        ),
        scratch_shapes=[pltpu.VMEM((rows, rows), F32)],
        compiler_params=params(),
        cost_estimate=cost(2.5, 8),
        name="attend",
    )(code_q, code_k, proj, proj, proj, w_out)


def both_cores(mine_ref, other_ref):
    half = mine_ref.shape[0] // 2
    other = jnp.concatenate([other_ref[half:, :], other_ref[:half, :]], axis=0)
    return mine_ref[...].astype(F32) + other.astype(F32)


def col_sum(v):
    return jnp.sum(v, axis=0, keepdims=True)


def feed_body(mine_ref, other_ref, x0_ref, sh_ref, b_ref, w1_hbm, w2_hbm, h_ref, n_ref, r_ref, act_ref, slope_ref, part_ref, w1, w2, acc, sems):
    copies = []
    for s in range(2):
        copies.append(pltpu.make_async_copy(w1_hbm.at[s], w1.at[s], sems.at[s]))
        copies.append(pltpu.make_async_copy(w2_hbm.at[s], w2.at[s], sems.at[2 + s]))
    for copy in copies:
        copy.start()
    total = both_cores(mine_ref, other_ref) + sh_ref[0:1, :] + x0_ref[...]
    h_one, normed, inverse = norm_parts(total, sh_ref[1:2, :], sh_ref[2:3, :])
    h_ref[...] = h_one.astype(BF)
    n_ref[...] = normed
    r_ref[...] = inverse
    for s in range(2):
        copies[2 * s].wait()
        pre = dot(h_ref[...], w1[s]) + b_ref[s : s + 1, 384:]
        cdf = 0.5 * (1.0 + lax.erf(pre * 0.7071067811865476))
        act_ref[s] = (pre * cdf).astype(BF)
        slope_ref[s] = (cdf + pre * jnp.exp(-0.5 * pre * pre) * 0.3989422804014327).astype(BF)
        copies[2 * s + 1].wait()
        part = dot(act_ref[s], w2[s])
        acc[...] = part if s == 0 else acc[...] + part
    part_ref[...] = acc[...].astype(BF)


def feed(mine, other, x_zero, shared, biases, w1, w2):
    rows = x_zero.shape[0]
    one, two = sds((rows, 768), BF), sds((2, rows, 768), BF)
    return pl.pallas_call(
        feed_body,
        out_shape=(one, sds((rows, 768), F32), sds((rows, 1), F32), two, two, one),
        in_specs=[VMEM_SPEC] * 5 + [ANY_SPEC] * 2,
        out_specs=(VMEM_SPEC,) * 6,
        scratch_shapes=[
            pltpu.VMEM((2, 768, 768), BF),
            pltpu.VMEM((2, 768, 768), BF),
            pltpu.VMEM((rows, 768), F32),
            pltpu.SemaphoreType.DMA((4,)),
        ],
        compiler_params=params(),
        cost_estimate=cost(2.8, 16),
        name="feed",
    )(mine, other, x_zero, shared, biases, w1, w2)


def feed_back_body(mine_ref, other_ref, n_ref, slope_ref, ca, cb, cc, cd, sh_ref, w1_hbm, w2_hbm, out_ref, d2_ref, d2b_ref, dpre_ref, part_ref, sums_ref, bsum_ref, w1, w2, g, acc, sems):
    copies = []
    for s in range(2):
        copies.append(pltpu.make_async_copy(w2_hbm.at[s], w2.at[s], sems.at[2 + s]))
        copies.append(pltpu.make_async_copy(w1_hbm.at[s], w1.at[s], sems.at[s]))
    for copy in copies:
        copy.start()
    n = ca.shape[0]
    for k, ref in enumerate((ca, cb, cc, cd)):
        g[k * RP : k * RP + n, :] = ref[...].astype(F32)
        g[k * RP + n : k * RP + RP, :] = jnp.zeros((RP - n, 768), F32)
    own = g.shape[0] // 2

    def row(i):
        return sh_ref[i : i + 1, :]

    h_one = n_ref[...] * row(1) + row(2)
    total = both_cores(mine_ref, other_ref) + row(3) + h_one
    rows_out, normed, inverse = norm_parts(total, row(4), row(5))
    out_ref[...] = rows_out[:own].astype(BF)
    grad = g[...]
    d_two = norm_back(grad, normed, inverse, row(4))
    d2_ref[...] = d_two
    d2b_ref[...] = d_two.astype(BF)
    sums_ref[0:3, :] = jnp.concatenate(
        [col_sum(d_two[:own]), col_sum(grad[:own] * normed[:own]), col_sum(grad[:own])], axis=0
    )
    sums_ref[3:8, :] = jnp.zeros((5, 768), F32)
    for s in range(2):
        copies[2 * s].wait()
        d_pre = dot_back(d2b_ref[...], w2[s]) * slope_ref[s].astype(F32)
        bsum_ref[s : s + 1, :] = col_sum(d_pre)
        dpre_ref[s] = d_pre.astype(BF)
        copies[2 * s + 1].wait()
        part = dot_back(dpre_ref[s], w1[s])
        acc[...] = part if s == 0 else acc[...] + part
    part_ref[...] = acc[...].astype(BF)


def feed_back(mine, other, normed, slope, cots, shared, w1, w2):
    rows = normed.shape[0]
    one = sds((rows, 768), BF)
    return pl.pallas_call(
        feed_back_body,
        out_shape=(
            sds((rows // 2, 768), BF),
            sds((rows, 768), F32),
            one,
            sds((2, rows, 768), BF),
            one,
            sds((8, 768), F32),
            sds((2, 768), F32),
        ),
        in_specs=[VMEM_SPEC] * 9 + [ANY_SPEC] * 2,
        out_specs=(VMEM_SPEC,) * 7,
        scratch_shapes=[
            pltpu.VMEM((2, 768, 768), BF),
            pltpu.VMEM((2, 768, 768), BF),
            pltpu.VMEM((rows, 768), F32),
            pltpu.VMEM((rows, 768), F32),
            pltpu.SemaphoreType.DMA((4,)),
        ],
        compiler_params=params(),
        cost_estimate=cost(2.8, 16),
        name="feed_back",
    )(mine, other, normed, slope, *cots, shared, w1, w2)


def attend_back_body(mine_ref, other_ref, d2_ref, n_ref, r_ref, sh_ref, wo_ref, wqkv_ref, p_ref, q_ref, k_ref, v_ref, d1_ref, d1b_ref, dproj_ref, part_ref, sums_ref, bsum_ref, dctx):
    h = pl.program_id(0)
    pairs = pl.num_programs(0)
    own = d1_ref.shape[0]

    @pl.when(h == 0)
    def _():
        dh = both_cores(mine_ref, other_ref) + d2_ref[...]
        normed = n_ref[...]
        d_one = norm_back(dh, normed, r_ref[...], sh_ref[1:2, :])
        d1_ref[...] = d_one[:own]
        d1b_ref[...] = d_one.astype(BF)
        sums_ref[0:3, :] = jnp.concatenate(
            [col_sum(d_one[:own]), col_sum(dh[:own] * normed[:own]), col_sum(dh[:own])], axis=0
        )
        sums_ref[3:8, :] = jnp.zeros((5, 768), F32)
        back = dot_back(d1b_ref[...], wo_ref[...]).astype(BF)
        for m in range(3):
            dctx[m] = back[:, m * 128 : m * 128 + 128]

    q, k, v, dc = q_ref[...], k_ref[...], v_ref[...], dctx[h]
    masks = head_masks(q.shape)
    dqs, dks, dvs = [], [], []
    for m in range(2):
        dch = jnp.where(masks[m], dc, jnp.zeros_like(dc))
        p = p_ref[m]
        dvs.append(inner_rows(p, dc))
        dp = dot_back(dch, v)
        pf = p.astype(F32)
        row = jnp.sum(dp * pf, axis=-1, keepdims=True)
        ds = (pf * (dp - row) * HEAD_DIM ** (-0.5)).astype(BF)
        dqs.append(dot(ds, k))
        dks.append(inner_rows(ds, q))
    dq, dk, dv = (jnp.where(masks[0], d[0], d[1]) for d in (dqs, dks, dvs))
    for part, d in enumerate((dq, dk, dv)):
        dproj_ref[:, pl.ds(pl.multiple_of(part * 384 + h * 128, 128), 128)] = d.astype(BF)
    bsum_ref[...] = jnp.concatenate([col_sum(dq), col_sum(dv), jnp.zeros((6, 128), F32)], axis=0)

    @pl.when(h == pairs - 1)
    def _():
        part_ref[...] = dot_back(dproj_ref[...], wqkv_ref[...]).astype(BF)


def attend_back(mine, other, d_two, normed, inverse, shared, w_out, w_qkv, probs, proj):
    rows = proj.shape[0]
    pairs = HEADS // 4
    return pl.pallas_call(
        attend_back_body,
        grid=(pairs,),
        out_shape=(
            sds((rows // 2, 768), F32),
            sds((rows, 768), BF),
            sds((rows, 1152), BF),
            sds((rows, 768), BF),
            sds((8, 768), F32),
            sds((8, 384), F32),
        ),
        in_specs=[
            all_steps((rows, 768)),
            all_steps((rows, 768)),
            all_steps((rows, 768)),
            all_steps((rows, 768)),
            all_steps((rows, 1)),
            all_steps(shared.shape),
            all_steps((384, 768)),
            all_steps((768, 1152)),
            pl.BlockSpec((2, rows, rows), lambda h: (h, 0, 0)),
            head_col(rows, 0),
            head_col(rows, pairs),
            head_col(rows, 2 * pairs),
        ],
        out_specs=(
            all_steps((rows // 2, 768)),
            all_steps((rows, 768)),
            all_steps((rows, 1152)),
            all_steps((rows, 768)),
            all_steps((8, 768)),
            pl.BlockSpec((8, 128), lambda h: (0, h)),
        ),
        scratch_shapes=[pltpu.VMEM((3, rows, 128), BF)],
        compiler_params=params(),
        cost_estimate=pl.CostEstimate(
            flops=2 * rows * rows * 64 * 4 * HEADS, bytes_accessed=10 * 1024 * 1024, transcendentals=0
        ),
        name="attend_back",
    )(mine, other, d_two, normed, inverse, shared, w_out, w_qkv, probs, proj, proj, proj)


def finish_body(flags_ref, part_ref, other_ref, d1_ref, gin_ref, mem_ref):
    own = d1_ref.shape[0]
    d_zero = part_ref[:own, :].astype(F32) + other_ref[...].astype(F32) + d1_ref[...]
    gin_ref[...] = d_zero.astype(BF)
    mem_ref[...] = jnp.zeros_like(mem_ref)
    for k in range(2):

        @pl.when((flags_ref[0] == k) & (flags_ref[1] == 1))
        def _(k=k):
            row = lax.broadcasted_iota(jnp.int32, (16, d_zero.shape[1]), 0)
            top = d_zero[k * RP : k * RP + 16, :]
            mem_ref[...] = jnp.where(row < MEM, top, 0.0)
            gin_ref[k * RP : k * RP + 16, :] = jnp.where(row < MEM, 0.0, top).astype(BF)


def finish(flags, part, other, d_one):
    return pl.pallas_call(
        finish_body,
        out_shape=(sds(d_one.shape, BF), sds((16, 768), F32)),
        in_specs=[SMEM_SPEC] + [VMEM_SPEC] * 3,
        out_specs=(VMEM_SPEC,) * 2,
        compiler_params=params(),
        cost_estimate=cost(0.1, 4),
        name="finish",
    )(flags, part, other, d_one)


def soap_body(n_terms, *refs):
    terms = refs[:n_terms]
    w_ref, m_ref, v_ref, sl_ref, sr_ref, l_ref, r_ref = refs[n_terms : n_terms + 7]
    nw_ref, nc_ref, nm_ref, nv_ref, nl_ref, nr_ref = refs[n_terms + 7 :]
    blocks = w_ref.shape[0]
    if n_terms == 1:
        grads = [terms[0][b] for b in range(blocks)]
    else:
        tiles = [sum(ref[0, k].astype(F32) for ref in terms) for k in range(TILES)]
        grads = [tile[:, :96] for tile in tiles]
        grads.append(jnp.concatenate([tile[:, 96:] for tile in tiles], axis=-1))
    for b in range(blocks):
        gb = grads[b].astype(BF)
        lb, rb = l_ref[b].astype(BF), r_ref[b].astype(BF)
        turned = dot(inner_rows(lb, gb).astype(BF), rb)
        new_first = beta_one * m_ref[b] + (1.0 - beta_one) * turned
        new_second = beta_two * v_ref[b] + (1.0 - beta_two) * turned * turned
        direction = (
            new_first
            / (1.0 - beta_one**STEP)
            / (jnp.sqrt(new_second / (1.0 - beta_two**STEP)) + adam_eps)
        )
        back = dot_back(dot(lb, direction.astype(BF)).astype(BF), rb)
        new_weight = w_ref[b] - rate_matrix * back
        nw_ref[b] = new_weight
        nc_ref[b] = new_weight.astype(BF)
        nm_ref[b] = new_first
        nv_ref[b] = new_second
        nl_ref[b] = beta_two * sl_ref[b] + (1.0 - beta_two) * dot_back(gb, gb)
        nr_ref[b] = beta_two * sr_ref[b] + (1.0 - beta_two) * inner_rows(gb, gb)


def soap(terms, master, first, second, left, right, left_rot, right_rot):
    count = master.shape[0]
    step = GROUP if len(terms) > 1 else 1
    spec = pl.BlockSpec((step, 96, 96), lambda i: (i, 0, 0))
    packed = pl.BlockSpec((1, TILES, 96, 128), lambda i: (i, 0, 0, 0))
    full = sds(master.shape, F32)
    return pl.pallas_call(
        functools.partial(soap_body, len(terms)),
        grid=(count // step,),
        out_shape=(full, sds(master.shape, BF), full, full, full, full),
        in_specs=[packed if len(terms) > 1 else spec] * len(terms) + [spec] * 7,
        out_specs=(spec,) * 6,
        compiler_params=params(),
        cost_estimate=cost(0.3, 24),
        name="soap",
    )(*terms, master, first, second, left, right, left_rot, right_rot)


def norm_parts(values, gain_vec, shift_vec):
    centred = values - jnp.mean(values, axis=-1, keepdims=True)
    inverse = lax.rsqrt(jnp.mean(centred * centred, axis=-1, keepdims=True) + norm_eps)
    normed = centred * inverse
    return (normed * gain_vec + shift_vec, normed, inverse)


def norm_back(upstream, normed, inverse, gain_vec):
    scaled = upstream * gain_vec
    result = inverse * (
        scaled
        - jnp.mean(scaled, axis=-1, keepdims=True)
        - normed * jnp.mean(scaled * normed, axis=-1, keepdims=True)
    )
    return result


def dot(left, right):
    return jnp.dot(left, right, preferred_element_type=F32)


def dot_back(left, right):
    return lax.dot_general(left, right, (((1,), (1,)), ((), ())), preferred_element_type=F32)


def inner_rows(left, right):
    return lax.dot_general(left, right, (((0,), (0,)), ((), ())), preferred_element_type=F32)


def adam_update(values, grad_vec, first_mom, second_mom, step_rate):
    new_first = beta_one * first_mom + (1.0 - beta_one) * grad_vec
    new_second = beta_two * second_mom + (1.0 - beta_two) * grad_vec * grad_vec
    direction = (
        new_first
        / (1.0 - beta_one**STEP)
        / (jnp.sqrt(new_second / (1.0 - beta_two**STEP)) + adam_eps)
    )
    return (values - step_rate * direction, new_first, new_second)


def per_device(
    n_dp,
    n_tensor,
    layer_in,
    cotangent,
    doc_ids,
    reset_flags,
    block_slot,
    master,
    first_moment,
    second_moment,
    left_stats,
    right_stats,
    left_basis,
    right_basis,
    split_params,
    split_first,
    split_second,
    shared,
    shared_first,
    shared_second,
):
    meshed = n_dp == 8 and master.shape[1] % GROUP == 0
    dp = lax.axis_index("dp")
    t = lax.axis_index("tensor")
    y, c = t // 2, t % 2
    me = jnp.stack([dp, t])
    barrier = lax.optimization_barrier
    slots = block_slot.shape[0]
    quarter = layer_in.shape[1]

    def swap(axis, step):
        size = n_dp if axis == "dp" else n_tensor
        return lambda v: lax.ppermute(v, axis, xor_pairs(size, step))

    core, yswap, xswap = swap("tensor", 1), swap("tensor", 2), swap("dp", 1)

    def along_z(*pairs):
        return lambda v: lax.ppermute(v, "dp", z_pairs(pairs))

    outer, middle = along_z((0, 1), (1, 0), (2, 3), (3, 2)), along_z((1, 2), (2, 1))
    inward, outward = along_z((0, 1), (3, 2)), along_z((1, 0), (2, 3))

    docs = lax.dynamic_index_in_dim(doc_ids, y, 0, keepdims=False)
    edge = jnp.full((MEM,), -1, jnp.int32)
    codes = jnp.concatenate([edge, docs, edge]).reshape(4, quarter)
    codes = jnp.pad(codes, ((0, 0), (0, RP - quarter)), constant_values=-2)
    codes = jnp.concatenate(
        [lax.dynamic_index_in_dim(codes, t ^ j, 0, keepdims=False) for j in (0, 2, 1, 3)]
    )
    code_q, code_k = codes[:, None], codes[None, :]
    reset_now = lax.dynamic_index_in_dim(reset_flags, y, 0, keepdims=False) == 1
    flags = jnp.stack([y + 2 * c, reset_now.astype(jnp.int32)])

    split_other = yswap(split_params)
    biases = jnp.concatenate(
        [jnp.where(y == 0, split_params, split_other), jnp.where(y == 0, split_other, split_params)], axis=0
    )
    def inputs_of(arr):
        mine = lax.dynamic_index_in_dim(arr, y, 0, keepdims=False)
        other = lax.dynamic_index_in_dim(arr, 1 - y, 0, keepdims=False)
        return mine, other

    (in_mine, in_send), (cot_mine, cot_send) = inputs_of(layer_in), inputs_of(cotangent)

    if meshed:
        own = pack_owned(master[0])
        near = outer(own)
        mid = middle(own)
        x0, y0 = xswap(own), yswap(own)
        near, mid, x0, y0 = barrier((near, mid, x0, y0))
        far_mid, far_end = middle(near), outward(mid)
        x1, diag0 = xswap(near), yswap(x0)
        small = (code_q, code_k, flags, biases, me, in_mine, in_send, cot_mine, cot_send)
        x1, diag0, far_mid, far_end, y0, small = barrier((x1, diag0, far_mid, far_end, y0, small))
        code_q, code_k, flags, biases, me, in_mine, in_send, cot_mine, cot_send = small
        far = far_mid + far_end
        last_end = outward(far_mid)
        x2, y2 = xswap(far), yswap(far)
        x2, y2, last_end, y0, diag0, in_send = barrier((x2, y2, last_end, y0, diag0, in_send))
        last = mid + last_end
        x3, y3, y1 = xswap(last), yswap(last), outer(y0)
        x3, y3, y1, x2, diag0 = barrier((x3, y3, y1, x2, diag0))
        diag3, diag2, diag1 = xswap(y3), yswap(x2), outer(diag0)
        in_other = yswap(in_send)
        diag3, diag2, diag1, cot_send = barrier((diag3, diag2, diag1, cot_send))
        pieces, places = [], []
        for jz, vals in enumerate(
            ((own, x0, y0, diag0), (near, x1, y1, diag1), (far, x2, y2, diag2), (last, x3, y3, diag3))
        ):
            pieces.extend(vals)
            places.extend([(0, 2 * jz), (0, 2 * jz + 1), (1, 2 * jz), (1, 2 * jz + 1)])
    else:
        every = lax.all_gather(master.astype(BF), "dp", axis=1, tiled=True)
        every_other = yswap(every)
        every = jnp.concatenate(
            [jnp.where(y == 0, every, every_other), jnp.where(y == 0, every_other, every)], axis=0
        )
        pieces, places = [pack_plain(every)], [(0, None)]
        in_other = yswap(in_send)
    w_qkv, w_out, w_up, w_down = build_weights(block_slot, me, pieces, tuple(places), slots)

    cot_other = yswap(cot_send)
    quarters = (in_mine, in_other, core(in_mine), core(in_other))
    cots = (cot_mine, cot_other, core(cot_mine), core(cot_other))
    proj, x_zero, x_in = project(flags, quarters, shared, w_qkv, biases)
    proj, cots = barrier((proj, cots))
    context, probs, attn = attend(code_q, code_k, proj, w_out)
    h_in, normed, inverse, act, slope, ffn = feed(attn, core(attn), x_zero, shared, biases, w_up, w_down)
    rows_out, d_two, d_two_b, d_pre, d_hidden, sums_two, up_sums = feed_back(
        ffn, core(ffn), normed, slope, cots, shared, w_up, w_down
    )
    d_hidden_other = core(d_hidden)
    g_up, g_down = feed_grads(act, d_two_b, h_in, d_pre)
    d_one, d_one_b, d_proj, d_in, sums_one, head_sums = attend_back(
        d_hidden, d_hidden_other, d_two, normed, inverse, shared, w_out, w_qkv, probs, proj
    )
    d_in_send = d_in[2 * RP :]

    def to_owner(arr):
        mine, other = arr[:quarter], yswap(arr[RP : RP + quarter])
        both = jnp.stack([mine, other])
        return jnp.where(y == 0, both, both[::-1])

    layer_out = to_owner(rows_out)
    d_proj, layer_out = barrier((d_proj, layer_out))
    d_in_other = core(d_in_send)
    srcs = (x_in, d_proj, context, d_one_b, g_up, g_down)
    grad_rows, memory_grad = finish(flags, d_in, d_in_other, d_one)
    vec = jnp.concatenate([sums_one[:3], sums_two[:3], memory_grad[:MEM]], axis=0)
    halves = head_sums[:2].reshape(2, 2, 192).swapaxes(0, 1).reshape(2, 384)
    splits = jnp.concatenate([halves, up_sums], axis=1).reshape(3, 768)

    def add_core(vec):
        return jnp.concatenate([vec + core(vec), splits], axis=0)

    if meshed:
        per = master.shape[1] // GROUP
        half = per // 2
        places, shapes = [], []
        for jz in RS_ORDER:
            for jy in range(2):
                for jx in range(2):
                    places.append((jy, 2 * jz + jx, 0))
                    shapes.append((per, TILES, 96, 128))
        packed = weight_grads(block_slot, me, srcs, tuple(places), shapes, slots)
        own, x_unit, y_unit, diag = {}, {}, {}, {}
        for n, jz in enumerate(RS_ORDER):
            own[jz], x_unit[jz], y_unit[jz], diag[jz] = packed[4 * n : 4 * n + 4]

        def plus(*vals):
            return sum(v.astype(F32) for v in vals).astype(BF)

        d3, d2, n1 = xswap(diag[3]), yswap(diag[2]), outer(diag[1])
        vec = add_core(after(vec, packed[0]))
        d3, d2, n1, vec, x_unit[3], y_unit[1] = barrier((d3, d2, n1, vec, x_unit[3], y_unit[1]))
        x3, y3, m1 = xswap(x_unit[3]), yswap(plus(y_unit[3], d3)), outer(y_unit[1])
        vec = vec + yswap(vec)
        x3, y3, m1, vec, y_unit[2] = barrier((x3, y3, m1, vec, y_unit[2]))
        x2, y2 = xswap(plus(x_unit[2], d2)), yswap(y_unit[2])
        part3 = plus(own[3], x3, y3)
        e3 = inward(part3)
        vec = vec + swap("dp", 1)(vec)
        x2, y2, e3, x_unit[1], vec = barrier((x2, y2, e3, x_unit[1], vec))
        x1, d0 = xswap(x_unit[1]), yswap(plus(diag[0], n1))
        part2 = plus(own[2], x2, y2, e3)
        fm, fe = middle(part2), inward(part2)
        vec = vec + swap("dp", 2)(vec)
        x1, d0, fm, fe, vec, m1 = barrier((x1, d0, fm, fe, vec, m1))
        x0, y0 = xswap(plus(x_unit[0], d0)), yswap(plus(y_unit[0], m1))
        near, mid = outer(plus(own[1], x1, fm)), middle(plus(part3, fe))
        vec = vec + swap("dp", 4)(vec)
        x0, y0, near, mid, vec, grad_rows = barrier((x0, y0, near, mid, vec, grad_rows))
        terms = (own[0], x0, y0, near, mid)
    else:
        packed = weight_grads(
            block_slot, me, srcs, ((0, None, 0),), [(2, slots // GROUP, TILES, 96, 128)], slots
        )[0]
        blocks = unpack_plain(packed)
        blocks = lax.psum_scatter(blocks, "dp", scatter_dimension=1, tiled=True)
        mine = lax.dynamic_index_in_dim(blocks, y, 0, keepdims=False)
        other = yswap(lax.dynamic_index_in_dim(blocks, 1 - y, 0, keepdims=False))
        terms = (mine.astype(F32) + other.astype(F32),)

        vec = add_core(vec)
        vec = vec + yswap(vec)
        step = 1
        while step < n_dp:
            vec = vec + swap("dp", step)(vec)
            step *= 2

    grad_in = to_owner(grad_rows)
    total_shared = vec[:16]
    grad_split = lax.dynamic_index_in_dim(vec[16:].reshape(2, -1), y, 0, keepdims=True)

    new_master, new_copy, new_first, new_second, new_left, new_right = soap(
        terms,
        master[0],
        first_moment[0],
        second_moment[0],
        left_stats[0],
        right_stats[0],
        left_basis[0],
        right_basis[0],
    )
    new_split, new_split_first, new_split_second = adam_update(
        split_params, grad_split, split_first, split_second, rate_vector
    )
    new_shared, new_shared_first, new_shared_second = adam_update(
        shared, total_shared, shared_first, shared_second, rate_shared
    )
    return (
        layer_out,
        grad_in,
        new_master[None],
        new_copy[None],
        new_first[None],
        new_second[None],
        new_left[None],
        new_right[None],
        new_split,
        new_split_first,
        new_split_second,
        new_shared,
        new_shared_first,
        new_shared_second,
    )


def solution(mesh):
    rows = P("dp", "tensor", None)
    state = P("tensor", "dp", None, None)
    split = P("tensor", None)
    return jax.shard_map(
        functools.partial(per_device, mesh.shape["dp"], mesh.shape["tensor"]),
        mesh=mesh,
        in_specs=(rows, rows, P("dp", None), P("dp"), P()) + (state,) * 7 + (split,) * 3 + (P(),) * 3,
        out_specs=(rows, rows) + (state,) * 6 + (split,) * 3 + (P(),) * 3,
        check_vma=False,
    )
```

```python
import functools

import jax
import jax.numpy as jnp
from jax import lax
from jax.experimental import pallas as pl
from jax.experimental.pallas import tpu as pltpu
from jax.sharding import PartitionSpec as P

HEADS = 12
HEAD_DIM = 64
FF = 3072
SEG_TOK = 512
MEM = 10
STEP = 10

beta_one = 0.9
beta_two = 0.95
adam_eps = 1e-08
norm_eps = 1e-12
rate_matrix = 0.05
rate_vector = 0.1
rate_shared = 0.75

BF = jnp.bfloat16
F32 = jnp.float32
VMEM_LIMIT = 24 * 1024 * 1024
BIG_LIMIT = 61 * 1024 * 1024
VMEM_SPEC = pl.BlockSpec(memory_space=pltpu.VMEM)
SMEM_SPEC = pl.BlockSpec(memory_space=pltpu.SMEM)
ANY_SPEC = pl.BlockSpec(memory_space=pl.ANY)
HBM_SPEC = pl.BlockSpec(memory_space=pltpu.HBM)
GROUP = 4
TILES = 3
UNROLL = 4
RP = 144
RS_ORDER = (3, 2, 1, 0)


def sds(shape, dtype):
    return jax.ShapeDtypeStruct(shape, dtype)


def params(limit=VMEM_LIMIT):
    return pltpu.CompilerParams(vmem_limit_bytes=limit)


def after(vals, deps):
    return lax.optimization_barrier((vals, deps))[0]


def cost(gflop, mbytes):
    return pl.CostEstimate(
        flops=int(gflop * 1e9), bytes_accessed=int(mbytes * 1e6), transcendentals=0
    )


def copy_body(v_ref, out_ref):
    out_ref[...] = v_ref[...]


def fence(token):
    return pl.pallas_call(
        copy_body,
        out_shape=sds(token.shape, token.dtype),
        in_specs=[VMEM_SPEC],
        out_specs=VMEM_SPEC,
        compiler_params=params(BIG_LIMIT),
        name="fence",
    )(token)


def xor_pairs(size, step):
    return [(i, i ^ step) for i in range(size)]


def z_pairs(pairs):
    return [(2 * a + x, 2 * b + x) for a, b in pairs for x in range(2)]


def pack_plain(blocks):
    lead = blocks.shape[:-3]
    grp = blocks.reshape(lead + (-1, GROUP, 96, 96))
    last = jnp.swapaxes(grp[..., 3, :, :].reshape(lead + (-1, 96, 3, 32)), -3, -2)
    return jnp.concatenate([grp[..., :3, :, :], last], axis=-1)


def unpack_plain(groups):
    last = jnp.swapaxes(groups[..., 96:], -3, -2)
    last = last.reshape(groups.shape[:-3] + (1, 96, 96))
    grp = jnp.concatenate([groups[..., :96], last], axis=-3)
    return grp.reshape(groups.shape[:-4] + (-1, 96, 96))


def pack_owned_body(m_ref, out_ref):
    for g in range(out_ref.shape[0]):
        last = m_ref[GROUP * g + 3].astype(BF)
        for k in range(TILES):
            out_ref[g, k] = jnp.concatenate(
                [m_ref[GROUP * g + k].astype(BF), last[:, 32 * k : 32 * k + 32]], axis=-1
            )


def pack_owned(blocks):
    n = blocks.shape[0] // GROUP
    return pl.pallas_call(
        pack_owned_body,
        out_shape=sds((n, TILES, 96, 128), BF),
        in_specs=[VMEM_SPEC],
        out_specs=VMEM_SPEC,
        compiler_params=params(),
        cost_estimate=cost(0.1, 2),
        name="pack_owned",
    )(blocks)


def weights_body(n_pieces, places, pos_ref, me_ref, *refs):
    pieces = refs[:n_pieces]
    outs = refs[n_pieces : n_pieces + 4]
    wqkv_ref, wo_ref, w1_ref, w2_ref, al, sems, out_sem = refs[n_pieces + 4 :]
    dp, y = me_ref[0], me_ref[1] // 2
    groups = al.shape[1]
    copies = []
    for ref, (jy, jd) in zip(pieces, places):
        n = ref.shape[-4]
        if jd is None:
            for s in range(2):
                dst = al.at[s, :, pl.ds(0, TILES)]
                copies.append(((s,), pltpu.make_async_copy(ref.at[s], dst, sems.at[s])))
        else:
            dst = al.at[y ^ jy, pl.ds((dp ^ jd) * n, n), pl.ds(0, TILES)]
            copies.append(((0, 1), pltpu.make_async_copy(ref, dst, sems.at[y ^ jy])))
    for _, copy in copies:
        copy.start()
    for s in range(2):
        whole = al.at[s, :, pl.ds(0, TILES)]
        pltpu.make_async_copy(whole, whole, sems.at[s]).wait()

        def fix(g, carry, s=s):
            al[s, g, 3, :, 0:96] = jnp.concatenate(
                [al[s, g, k, :, 96:128] for k in range(TILES)], axis=-1
            )
            return carry

        lax.fori_loop(0, groups, fix, 0, unroll=16)

    def block(s, b):
        p = pos_ref[b]
        return al[s, p // GROUP, p % GROUP][:, :96]

    def strip_qkv(i, carry):
        rows = pl.ds(pl.multiple_of(i * 96, 96), 96)
        for part in range(3):
            wqkv_ref[rows, part * 384 : part * 384 + 384] = jnp.concatenate(
                [block(j // 2, i * 6 + part * 2 + j % 2) for j in range(4)], axis=-1
            )
        return carry

    def strip(i, carry, ref, first):
        rows = pl.ds(pl.multiple_of(i * 96, 96), 96)
        for s in range(2):
            for half in range(2):
                ref[s, rows, half * 384 : half * 384 + 384] = jnp.concatenate(
                    [block(s, first + i * 8 + half * 4 + j) for j in range(4)], axis=-1
                )
        return carry

    def send(k):
        copy = pltpu.make_async_copy((wqkv_ref, wo_ref, w1_ref, w2_ref)[k], outs[k], out_sem.at[k])
        copy.start()
        return copy

    lax.fori_loop(0, 8, functools.partial(strip, ref=w1_ref, first=64), 0, unroll=UNROLL)
    sent = [send(2)]
    lax.fori_loop(0, 8, functools.partial(strip, ref=w2_ref, first=128), 0, unroll=UNROLL)
    sent.append(send(3))
    lax.fori_loop(0, 8, strip_qkv, 0, unroll=UNROLL)
    sent.append(send(0))
    for i in range(4):
        for half in range(2):
            wo_ref[i * 96 : i * 96 + 96, half * 384 : half * 384 + 384] = jnp.concatenate(
                [block(i // 2, 48 + (i % 2) * 8 + half * 4 + j) for j in range(4)], axis=-1
            )
    sent.append(send(1))
    for copy in sent:
        copy.wait()


def build_weights(pos, me, pieces, places, slots):
    return pl.pallas_call(
        functools.partial(weights_body, len(pieces), places),
        out_shape=(
            sds((768, 1152), BF),
            sds((384, 768), BF),
            sds((2, 768, 768), BF),
            sds((2, 768, 768), BF),
        ),
        in_specs=[SMEM_SPEC, SMEM_SPEC] + [HBM_SPEC] * len(pieces),
        out_specs=(HBM_SPEC,) * 4,
        scratch_shapes=[
            pltpu.VMEM((768, 1152), BF),
            pltpu.VMEM((384, 768), BF),
            pltpu.VMEM((2, 768, 768), BF),
            pltpu.VMEM((2, 768, 768), BF),
            pltpu.VMEM((2, slots // GROUP, GROUP, 96, 128), BF),
            pltpu.SemaphoreType.DMA((2,)),
            pltpu.SemaphoreType.DMA((4,)),
        ],
        compiler_params=params(BIG_LIMIT),
        cost_estimate=cost(0.1, 30),
        name="build_weights",
    )(pos, me, *pieces)


def product(left, right, out, width=256):
    def step(i, carry):
        col = pl.multiple_of(i * width, width)
        out[pl.ds(col, width), :] = inner_rows(left[:, pl.ds(col, width)], right[...]).astype(BF)
        return carry

    lax.fori_loop(0, out.shape[0] // width, step, 0)


def down_grads_body(act_ref, d2_ref, out_ref):
    for s in range(2):
        product(act_ref.at[s], d2_ref, out_ref.at[s])


def up_grads_body(h_ref, dpre_ref, later_ref, out_ref):
    for s in range(2):
        product(h_ref, dpre_ref.at[s], out_ref.at[s])


def down_grads(act, d_two):
    return pl.pallas_call(
        down_grads_body,
        out_shape=sds((2, 768, 768), BF),
        in_specs=[VMEM_SPEC] * 2,
        out_specs=VMEM_SPEC,
        compiler_params=params(),
        cost_estimate=cost(1.4, 8),
        name="down_grads",
    )(act, d_two)


def up_grads(h_in, d_pre, later):
    return pl.pallas_call(
        up_grads_body,
        out_shape=sds((2, 768, 768), BF),
        in_specs=[VMEM_SPEC] * 2 + [ANY_SPEC],
        out_specs=VMEM_SPEC,
        compiler_params=params(),
        cost_estimate=cost(1.4, 8),
        name="up_grads",
    )(h_in, d_pre, later)


def pack_body(places, pos_ref, me_ref, *refs):
    token_ref = refs[5]
    outs = refs[6 : 6 + len(places)]
    g2, g1, go, gq, al, sem, sems = refs[6 + len(places) :]
    loads = [pltpu.make_async_copy(src, dst, sems.at[k]) for k, (src, dst) in enumerate(zip(refs, (g2, g1, go, gq)))]
    for load in loads:
        load.start()
    groups = al.shape[1]
    token_ref[...] = jnp.zeros_like(token_ref)

    def put(s, b, blk):
        p = pos_ref[b]
        al[s, p // GROUP, p % GROUP, :, 0:96] = blk

    def strip(i, carry, ref, first):
        rows = pl.ds(pl.multiple_of(i * 96, 96), 96)
        for s in range(2):
            for half in range(2):
                vals = ref[s, rows, half * 384 : half * 384 + 384]
                for j in range(4):
                    put(s, first + i * 8 + half * 4 + j, vals[:, 96 * j : 96 * j + 96])
        return carry

    def strip_qkv(i, carry):
        rows = pl.ds(pl.multiple_of(i * 96, 96), 96)
        for part in range(3):
            vals = gq[rows, part * 384 : part * 384 + 384]
            for j in range(4):
                put(j // 2, i * 6 + part * 2 + j % 2, vals[:, 96 * j : 96 * j + 96])
        return carry

    loads[0].wait()
    lax.fori_loop(0, 8, functools.partial(strip, ref=g2, first=128), 0, unroll=UNROLL)
    loads[1].wait()
    lax.fori_loop(0, 8, functools.partial(strip, ref=g1, first=64), 0, unroll=UNROLL)
    loads[2].wait()
    for i in range(4):
        for half in range(2):
            vals = go[i * 96 : i * 96 + 96, half * 384 : half * 384 + 384]
            for j in range(4):
                put(i // 2, 48 + (i % 2) * 8 + half * 4 + j, vals[:, 96 * j : 96 * j + 96])
    loads[3].wait()
    lax.fori_loop(0, 8, strip_qkv, 0, unroll=UNROLL)

    dp, y = me_ref[0], me_ref[1] // 2
    copies = []
    for s in range(2):

        def fix(g, carry, s=s):
            last = al[s, g, 3]
            for k in range(TILES):
                al[s, g, k, :, 96:128] = last[:, 32 * k : 32 * k + 32]
            return carry

        lax.fori_loop(0, groups, fix, 0, unroll=16)
        for ref, (jy, jd) in zip(outs, places):
            if jd is None:
                copies.append((None, pltpu.make_async_copy(al.at[s, :, pl.ds(0, TILES)], ref.at[s], sem)))
            else:
                n = ref.shape[0]
                src = al.at[s, pl.ds((dp ^ jd) * n, n), pl.ds(0, TILES)]
                copies.append(((y ^ jy) == s, pltpu.make_async_copy(src, ref, sem)))
        for mine, copy in copies[s * len(outs) :]:
            if mine is None:
                copy.start()
            else:
                pl.when(mine)(copy.start)
    for mine, copy in copies:
        if mine is None:
            copy.wait()
        else:
            pl.when(mine)(copy.wait)


def pack_grads(pos, me, grads, places, out_shapes, slots):
    return pl.pallas_call(
        functools.partial(pack_body, places),
        out_shape=(sds((8, 128), F32), *(sds(s, BF) for s in out_shapes)),
        in_specs=[SMEM_SPEC, SMEM_SPEC] + [HBM_SPEC] * 4 + [ANY_SPEC],
        out_specs=(VMEM_SPEC,) + (HBM_SPEC,) * len(places),
        scratch_shapes=[
            pltpu.VMEM((2, 768, 768), BF),
            pltpu.VMEM((2, 768, 768), BF),
            pltpu.VMEM((384, 768), BF),
            pltpu.VMEM((768, 1152), BF),
            pltpu.VMEM((2, slots // GROUP, GROUP, 96, 128), BF),
            pltpu.SemaphoreType.DMA,
            pltpu.SemaphoreType.DMA((4,)),
        ],
        compiler_params=params(BIG_LIMIT),
        cost_estimate=cost(0.1, 30),
        name="pack_grads",
    )(pos, me, *grads)


def project_body(flags_ref, xa, xb, xc, xd, sh_ref, w_ref, b_ref, later_ref, proj_ref, x0_ref, xin_ref, bias):
    @pl.when(pl.program_id(0) == 0)
    def _():
        n = xa.shape[0]
        gap = jnp.zeros((RP - n, x0_ref.shape[1]), F32)
        for k, ref in enumerate((xa, xb, xc, xd)):
            x0_ref[k * RP : k * RP + n, :] = ref[...].astype(F32)
            x0_ref[k * RP + n : k * RP + RP, :] = gap

            @pl.when((flags_ref[0] == k) & (flags_ref[1] == 1))
            def _(k=k):
                x0_ref[k * RP : k * RP + MEM, :] = sh_ref[6 : 6 + MEM, :]

        xin_ref[...] = x0_ref[...].astype(BF)
        for part, col in ((0, 0), (2, 192)):
            bias[part] = jnp.concatenate([b_ref[s : s + 1, col : col + 192] for s in range(2)], axis=1)
        bias[1] = jnp.zeros((1, 384), F32)

    proj_ref[...] = (dot(xin_ref[...], w_ref[...]) + bias[pl.program_id(0)]).astype(BF)


def project(flags, quarters, shared, w_qkv, biases, later):
    rows = 4 * RP

    def whole(shape):
        return pl.BlockSpec(shape, lambda i: (0, 0))

    return pl.pallas_call(
        project_body,
        grid=(3,),
        out_shape=(sds((rows, 1152), BF), sds((rows, 768), F32), sds((rows, 768), BF)),
        in_specs=[
            SMEM_SPEC,
            *[whole(q.shape) for q in quarters],
            whole(shared.shape),
            pl.BlockSpec((768, 384), lambda i: (0, i)),
            whole(biases.shape),
            ANY_SPEC,
        ],
        out_specs=(
            pl.BlockSpec((rows, 384), lambda i: (0, i)),
            whole((rows, 768)),
            whole((rows, 768)),
        ),
        scratch_shapes=[pltpu.VMEM((3, 1, 384), F32)],
        compiler_params=params(),
        cost_estimate=cost(1.0, 5),
        name="project",
    )(flags, *quarters, shared, w_qkv, biases, later)


def head_masks(shape):
    lane = lax.broadcasted_iota(jnp.int32, shape, 1)
    return lane < HEAD_DIM, lane >= HEAD_DIM


def attend_body(cq_ref, ck_ref, q_ref, k_ref, v_ref, wo_ref, ctx_ref, p_ref, part_ref, vis):
    h = pl.program_id(0)

    @pl.when(h == 0)
    def _():
        cq, ck = cq_ref[...], ck_ref[...]
        seen = ((cq == -1) | (ck == -1) | (cq == ck)) & (ck != -2)
        vis[...] = jnp.where(seen, 1.0, 0.0)

    q, k, v = q_ref[...], k_ref[...], v_ref[...]
    masks = head_masks(q.shape)
    outs = []
    for n in range(2):
        qh = jnp.where(masks[n], q, jnp.zeros_like(q))
        scores = jnp.where(vis[...] > 0.5, dot_back(qh, k) * HEAD_DIM ** (-0.5), -1000000000.0)
        e = jnp.exp(scores - jnp.max(scores, axis=-1, keepdims=True))
        p = (e * (1.0 / jnp.sum(e, axis=-1, keepdims=True))).astype(BF)
        p_ref[n] = p
        outs.append(dot(p, v))
    ctx_ref[:, pl.ds(pl.multiple_of(h * 128, 128), 128)] = jnp.where(masks[0], outs[0], outs[1]).astype(BF)

    @pl.when(h == pl.num_programs(0) - 1)
    def _():
        part_ref[...] = dot(ctx_ref[...], wo_ref[...]).astype(BF)


def head_col(rows, off):
    return pl.BlockSpec((rows, 128), lambda h: (0, h + off))


def all_steps(shape):
    return pl.BlockSpec(shape, lambda h: (0,) * len(shape))


def attend(code_q, code_k, proj, w_out):
    rows = proj.shape[0]
    pairs = HEADS // 4
    return pl.pallas_call(
        attend_body,
        grid=(pairs,),
        out_shape=(sds((rows, 384), BF), sds((2 * pairs, rows, rows), BF), sds((rows, 768), BF)),
        in_specs=[
            all_steps((rows, 1)),
            all_steps((1, rows)),
            head_col(rows, 0),
            head_col(rows, pairs),
            head_col(rows, 2 * pairs),
            all_steps((384, 768)),
        ],
        out_specs=(
            all_steps((rows, 384)),
            pl.BlockSpec((2, rows, rows), lambda h: (h, 0, 0)),
            all_steps((rows, 768)),
        ),
        scratch_shapes=[pltpu.VMEM((rows, rows), F32)],
        compiler_params=params(),
        cost_estimate=cost(2.5, 8),
        name="attend",
    )(code_q, code_k, proj, proj, proj, w_out)


def both_cores(mine_ref, other_ref):
    half = mine_ref.shape[0] // 2
    other = jnp.concatenate([other_ref[half:, :], other_ref[:half, :]], axis=0)
    return mine_ref[...].astype(F32) + other.astype(F32)


def col_sum(v):
    return jnp.sum(v, axis=0, keepdims=True)


def feed_body(mine_ref, other_ref, x0_ref, sh_ref, b_ref, w1_hbm, w2_hbm, h_ref, n_ref, r_ref, act_ref, slope_ref, part_ref, w1, w2, acc, sems):
    copies = []
    for s in range(2):
        copies.append(pltpu.make_async_copy(w1_hbm.at[s], w1.at[s], sems.at[s]))
        copies.append(pltpu.make_async_copy(w2_hbm.at[s], w2.at[s], sems.at[2 + s]))
    for copy in copies:
        copy.start()
    total = both_cores(mine_ref, other_ref) + sh_ref[0:1, :] + x0_ref[...]
    h_one, normed, inverse = norm_parts(total, sh_ref[1:2, :], sh_ref[2:3, :])
    h_ref[...] = h_one.astype(BF)
    n_ref[...] = normed
    r_ref[...] = inverse
    for s in range(2):
        copies[2 * s].wait()
        pre = dot(h_ref[...], w1[s]) + b_ref[s : s + 1, 384:]
        cdf = 0.5 * (1.0 + lax.erf(pre * 0.7071067811865476))
        act_ref[s] = (pre * cdf).astype(BF)
        slope_ref[s] = (cdf + pre * jnp.exp(-0.5 * pre * pre) * 0.3989422804014327).astype(BF)
        copies[2 * s + 1].wait()
        part = dot(act_ref[s], w2[s])
        acc[...] = part if s == 0 else acc[...] + part
    part_ref[...] = acc[...].astype(BF)


def feed(mine, other, x_zero, shared, biases, w1, w2):
    rows = x_zero.shape[0]
    one, two = sds((rows, 768), BF), sds((2, rows, 768), BF)
    return pl.pallas_call(
        feed_body,
        out_shape=(one, sds((rows, 768), F32), sds((rows, 1), F32), two, two, one),
        in_specs=[VMEM_SPEC] * 5 + [ANY_SPEC] * 2,
        out_specs=(VMEM_SPEC,) * 6,
        scratch_shapes=[
            pltpu.VMEM((2, 768, 768), BF),
            pltpu.VMEM((2, 768, 768), BF),
            pltpu.VMEM((rows, 768), F32),
            pltpu.SemaphoreType.DMA((4,)),
        ],
        compiler_params=params(),
        cost_estimate=cost(2.8, 16),
        name="feed",
    )(mine, other, x_zero, shared, biases, w1, w2)


def feed_back_body(mine_ref, other_ref, n_ref, slope_ref, ca, cb, cc, cd, sh_ref, w1_hbm, w2_hbm, out_ref, d2_ref, d2b_ref, dpre_ref, part_ref, sums_ref, bsum_ref, w1, w2, g, acc, sems):
    copies = []
    for s in range(2):
        copies.append(pltpu.make_async_copy(w2_hbm.at[s], w2.at[s], sems.at[2 + s]))
        copies.append(pltpu.make_async_copy(w1_hbm.at[s], w1.at[s], sems.at[s]))
    for copy in copies:
        copy.start()
    n = ca.shape[0]
    for k, ref in enumerate((ca, cb, cc, cd)):
        g[k * RP : k * RP + n, :] = ref[...].astype(F32)
        g[k * RP + n : k * RP + RP, :] = jnp.zeros((RP - n, 768), F32)
    own = g.shape[0] // 2

    def row(i):
        return sh_ref[i : i + 1, :]

    h_one = n_ref[...] * row(1) + row(2)
    total = both_cores(mine_ref, other_ref) + row(3) + h_one
    rows_out, normed, inverse = norm_parts(total, row(4), row(5))
    out_ref[...] = rows_out[:own].astype(BF)
    grad = g[...]
    d_two = norm_back(grad, normed, inverse, row(4))
    d2_ref[...] = d_two
    d2b_ref[...] = d_two.astype(BF)
    sums_ref[0:3, :] = jnp.concatenate(
        [col_sum(d_two[:own]), col_sum(grad[:own] * normed[:own]), col_sum(grad[:own])], axis=0
    )
    sums_ref[3:8, :] = jnp.zeros((5, 768), F32)
    for s in range(2):
        copies[2 * s].wait()
        d_pre = dot_back(d2b_ref[...], w2[s]) * slope_ref[s].astype(F32)
        bsum_ref[s : s + 1, :] = col_sum(d_pre)
        dpre_ref[s] = d_pre.astype(BF)
        copies[2 * s + 1].wait()
        part = dot_back(dpre_ref[s], w1[s])
        acc[...] = part if s == 0 else acc[...] + part
    part_ref[...] = acc[...].astype(BF)


def feed_back(mine, other, normed, slope, cots, shared, w1, w2):
    rows = normed.shape[0]
    one = sds((rows, 768), BF)
    return pl.pallas_call(
        feed_back_body,
        out_shape=(
            sds((rows // 2, 768), BF),
            sds((rows, 768), F32),
            one,
            sds((2, rows, 768), BF),
            one,
            sds((8, 768), F32),
            sds((2, 768), F32),
        ),
        in_specs=[VMEM_SPEC] * 9 + [ANY_SPEC] * 2,
        out_specs=(VMEM_SPEC,) * 7,
        scratch_shapes=[
            pltpu.VMEM((2, 768, 768), BF),
            pltpu.VMEM((2, 768, 768), BF),
            pltpu.VMEM((rows, 768), F32),
            pltpu.VMEM((rows, 768), F32),
            pltpu.SemaphoreType.DMA((4,)),
        ],
        compiler_params=params(),
        cost_estimate=cost(2.8, 16),
        name="feed_back",
    )(mine, other, normed, slope, *cots, shared, w1, w2)


def attend_back_body(mine_ref, other_ref, d2_ref, n_ref, r_ref, sh_ref, wo_ref, wqkv_ref, x_ref, ctx_ref, later_ref, p_ref, q_ref, k_ref, v_ref, d1_ref, gq_ref, go_ref, part_ref, sums_ref, bsum_ref, d1b_ref, dproj_ref, dctx):
    h = pl.program_id(0)
    pairs = pl.num_programs(0)
    own = d1_ref.shape[0]

    @pl.when(h == 0)
    def _():
        dh = both_cores(mine_ref, other_ref) + d2_ref[...]
        normed = n_ref[...]
        d_one = norm_back(dh, normed, r_ref[...], sh_ref[1:2, :])
        d1_ref[...] = d_one[:own]
        d1b_ref[...] = d_one.astype(BF)
        sums_ref[0:3, :] = jnp.concatenate(
            [col_sum(d_one[:own]), col_sum(dh[:own] * normed[:own]), col_sum(dh[:own])], axis=0
        )
        sums_ref[3:8, :] = jnp.zeros((5, 768), F32)
        back = dot_back(d1b_ref[...], wo_ref[...]).astype(BF)
        for m in range(3):
            dctx[m] = back[:, m * 128 : m * 128 + 128]

    q, k, v, dc = q_ref[...], k_ref[...], v_ref[...], dctx[h]
    masks = head_masks(q.shape)
    dqs, dks, dvs = [], [], []
    for m in range(2):
        dch = jnp.where(masks[m], dc, jnp.zeros_like(dc))
        p = p_ref[m]
        dvs.append(inner_rows(p, dc))
        dp = dot_back(dch, v)
        pf = p.astype(F32)
        row = jnp.sum(dp * pf, axis=-1, keepdims=True)
        ds = (pf * (dp - row) * HEAD_DIM ** (-0.5)).astype(BF)
        dqs.append(dot(ds, k))
        dks.append(inner_rows(ds, q))
    dq, dk, dv = (jnp.where(masks[0], d[0], d[1]) for d in (dqs, dks, dvs))
    for part, d in enumerate((dq, dk, dv)):
        dproj_ref[:, pl.ds(pl.multiple_of(part * 384 + h * 128, 128), 128)] = d.astype(BF)
    bsum_ref[...] = jnp.concatenate([col_sum(dq), col_sum(dv), jnp.zeros((6, 128), F32)], axis=0)

    @pl.when(h == pairs - 1)
    def _():
        part_ref[...] = dot_back(dproj_ref[...], wqkv_ref[...]).astype(BF)
        product(ctx_ref, d1b_ref, go_ref, 128)
        product(x_ref, dproj_ref, gq_ref)


def attend_back(mine, other, d_two, normed, inverse, shared, w_out, w_qkv, x_in, context, later, probs, proj):
    rows = proj.shape[0]
    pairs = HEADS // 4
    return pl.pallas_call(
        attend_back_body,
        grid=(pairs,),
        out_shape=(
            sds((rows // 2, 768), F32),
            sds((768, 1152), BF),
            sds((384, 768), BF),
            sds((rows, 768), BF),
            sds((8, 768), F32),
            sds((8, 384), F32),
        ),
        in_specs=[
            all_steps((rows, 768)),
            all_steps((rows, 768)),
            all_steps((rows, 768)),
            all_steps((rows, 768)),
            all_steps((rows, 1)),
            all_steps(shared.shape),
            all_steps((384, 768)),
            all_steps((768, 1152)),
            all_steps((rows, 768)),
            all_steps((rows, 384)),
            ANY_SPEC,
            pl.BlockSpec((2, rows, rows), lambda h: (h, 0, 0)),
            head_col(rows, 0),
            head_col(rows, pairs),
            head_col(rows, 2 * pairs),
        ],
        out_specs=(
            all_steps((rows // 2, 768)),
            all_steps((768, 1152)),
            all_steps((384, 768)),
            all_steps((rows, 768)),
            all_steps((8, 768)),
            pl.BlockSpec((8, 128), lambda h: (0, h)),
        ),
        scratch_shapes=[
            pltpu.VMEM((rows, 768), BF),
            pltpu.VMEM((rows, 1152), BF),
            pltpu.VMEM((3, rows, 128), BF),
        ],
        compiler_params=params(),
        cost_estimate=pl.CostEstimate(
            flops=2 * rows * rows * 64 * 4 * HEADS, bytes_accessed=10 * 1024 * 1024, transcendentals=0
        ),
        name="attend_back",
    )(mine, other, d_two, normed, inverse, shared, w_out, w_qkv, x_in, context, later, probs, proj, proj, proj)


def finish_body(flags_ref, part_ref, other_ref, d1_ref, gin_ref, mem_ref):
    own = d1_ref.shape[0]
    d_zero = part_ref[:own, :].astype(F32) + other_ref[...].astype(F32) + d1_ref[...]
    gin_ref[...] = d_zero.astype(BF)
    mem_ref[...] = jnp.zeros_like(mem_ref)
    for k in range(2):

        @pl.when((flags_ref[0] == k) & (flags_ref[1] == 1))
        def _(k=k):
            row = lax.broadcasted_iota(jnp.int32, (16, d_zero.shape[1]), 0)
            top = d_zero[k * RP : k * RP + 16, :]
            mem_ref[...] = jnp.where(row < MEM, top, 0.0)
            gin_ref[k * RP : k * RP + 16, :] = jnp.where(row < MEM, 0.0, top).astype(BF)


def finish(flags, part, other, d_one):
    return pl.pallas_call(
        finish_body,
        out_shape=(sds(d_one.shape, BF), sds((16, 768), F32)),
        in_specs=[SMEM_SPEC] + [VMEM_SPEC] * 3,
        out_specs=(VMEM_SPEC,) * 2,
        compiler_params=params(),
        cost_estimate=cost(0.1, 4),
        name="finish",
    )(flags, part, other, d_one)


def soap_body(n_terms, *refs):
    terms = refs[:n_terms]
    w_ref, m_ref, v_ref, sl_ref, sr_ref, l_ref, r_ref = refs[n_terms : n_terms + 7]
    nw_ref, nc_ref, nm_ref, nv_ref, nl_ref, nr_ref = refs[n_terms + 7 :]
    blocks = w_ref.shape[0]
    if n_terms == 1:
        grads = [terms[0][b] for b in range(blocks)]
    else:
        tiles = [sum(ref[0, k].astype(F32) for ref in terms) for k in range(TILES)]
        grads = [tile[:, :96] for tile in tiles]
        grads.append(jnp.concatenate([tile[:, 96:] for tile in tiles], axis=-1))
    every = range(blocks)
    gb = [g.astype(BF) for g in grads]
    lb, rb = [l_ref[b].astype(BF) for b in every], [r_ref[b].astype(BF) for b in every]
    half = [inner_rows(lb[b], gb[b]).astype(BF) for b in every]
    for b in every:
        nl_ref[b] = beta_two * sl_ref[b] + (1.0 - beta_two) * dot_back(gb[b], gb[b])
    turned = [dot(half[b], rb[b]) for b in every]
    for b in every:
        nr_ref[b] = beta_two * sr_ref[b] + (1.0 - beta_two) * inner_rows(gb[b], gb[b])
    steps = []
    for b in every:
        new_first = beta_one * m_ref[b] + (1.0 - beta_one) * turned[b]
        new_second = beta_two * v_ref[b] + (1.0 - beta_two) * turned[b] * turned[b]
        nm_ref[b] = new_first
        nv_ref[b] = new_second
        direction = (
            new_first
            / (1.0 - beta_one**STEP)
            / (jnp.sqrt(new_second / (1.0 - beta_two**STEP)) + adam_eps)
        )
        steps.append(direction.astype(BF))
    half = [dot(lb[b], steps[b]).astype(BF) for b in every]
    for b in every:
        new_weight = w_ref[b] - rate_matrix * dot_back(half[b], rb[b])
        nw_ref[b] = new_weight
        nc_ref[b] = new_weight.astype(BF)


def soap(terms, master, first, second, left, right, left_rot, right_rot):
    count = master.shape[0]
    step = GROUP if len(terms) > 1 else 1
    spec = pl.BlockSpec((step, 96, 96), lambda i: (i, 0, 0))
    packed = pl.BlockSpec((1, TILES, 96, 128), lambda i: (i, 0, 0, 0))
    full = sds(master.shape, F32)
    return pl.pallas_call(
        functools.partial(soap_body, len(terms)),
        grid=(count // step,),
        out_shape=(full, sds(master.shape, BF), full, full, full, full),
        in_specs=[packed if len(terms) > 1 else spec] * len(terms) + [spec] * 7,
        out_specs=(spec,) * 6,
        compiler_params=params(BIG_LIMIT),
        cost_estimate=cost(0.3, 24),
        name="soap",
    )(*terms, master, first, second, left, right, left_rot, right_rot)


def norm_parts(values, gain_vec, shift_vec):
    centred = values - jnp.mean(values, axis=-1, keepdims=True)
    inverse = lax.rsqrt(jnp.mean(centred * centred, axis=-1, keepdims=True) + norm_eps)
    normed = centred * inverse
    return (normed * gain_vec + shift_vec, normed, inverse)


def norm_back(upstream, normed, inverse, gain_vec):
    scaled = upstream * gain_vec
    result = inverse * (
        scaled
        - jnp.mean(scaled, axis=-1, keepdims=True)
        - normed * jnp.mean(scaled * normed, axis=-1, keepdims=True)
    )
    return result


def dot(left, right):
    return jnp.dot(left, right, preferred_element_type=F32)


def dot_back(left, right):
    return lax.dot_general(left, right, (((1,), (1,)), ((), ())), preferred_element_type=F32)


def inner_rows(left, right):
    return lax.dot_general(left, right, (((0,), (0,)), ((), ())), preferred_element_type=F32)


def adam_update(values, grad_vec, first_mom, second_mom, step_rate):
    new_first = beta_one * first_mom + (1.0 - beta_one) * grad_vec
    new_second = beta_two * second_mom + (1.0 - beta_two) * grad_vec * grad_vec
    direction = (
        new_first
        / (1.0 - beta_one**STEP)
        / (jnp.sqrt(new_second / (1.0 - beta_two**STEP)) + adam_eps)
    )
    return (values - step_rate * direction, new_first, new_second)


def per_device(
    n_dp,
    n_tensor,
    layer_in,
    cotangent,
    doc_ids,
    reset_flags,
    block_slot,
    master,
    first_moment,
    second_moment,
    left_stats,
    right_stats,
    left_basis,
    right_basis,
    split_params,
    split_first,
    split_second,
    shared,
    shared_first,
    shared_second,
):
    meshed = n_dp == 8 and master.shape[1] % GROUP == 0
    dp = lax.axis_index("dp")
    t = lax.axis_index("tensor")
    y, c = t // 2, t % 2
    me = jnp.stack([dp, t])
    barrier = lax.optimization_barrier
    slots = block_slot.shape[0]
    quarter = layer_in.shape[1]

    def swap(axis, step):
        size = n_dp if axis == "dp" else n_tensor
        return lambda v: lax.ppermute(v, axis, xor_pairs(size, step))

    core, yswap, xswap = swap("tensor", 1), swap("tensor", 2), swap("dp", 1)

    def along_z(*pairs):
        return lambda v: lax.ppermute(v, "dp", z_pairs(pairs))

    outer, middle = along_z((0, 1), (1, 0), (2, 3), (3, 2)), along_z((1, 2), (2, 1))
    inward, outward = along_z((0, 1), (3, 2)), along_z((1, 0), (2, 3))

    docs = lax.dynamic_index_in_dim(doc_ids, y, 0, keepdims=False)
    edge = jnp.full((MEM,), -1, jnp.int32)
    codes = jnp.concatenate([edge, docs, edge]).reshape(4, quarter)
    codes = jnp.pad(codes, ((0, 0), (0, RP - quarter)), constant_values=-2)
    codes = jnp.concatenate(
        [lax.dynamic_index_in_dim(codes, t ^ j, 0, keepdims=False) for j in (0, 2, 1, 3)]
    )
    code_q, code_k = codes[:, None], codes[None, :]
    reset_now = lax.dynamic_index_in_dim(reset_flags, y, 0, keepdims=False) == 1
    flags = jnp.stack([y + 2 * c, reset_now.astype(jnp.int32)])

    split_other = yswap(split_params)
    biases = jnp.concatenate(
        [jnp.where(y == 0, split_params, split_other), jnp.where(y == 0, split_other, split_params)], axis=0
    )
    def inputs_of(arr):
        mine = lax.dynamic_index_in_dim(arr, y, 0, keepdims=False)
        other = lax.dynamic_index_in_dim(arr, 1 - y, 0, keepdims=False)
        return mine, other

    (in_mine, in_send), (cot_mine, cot_send) = inputs_of(layer_in), inputs_of(cotangent)

    if meshed:
        own = pack_owned(master[0])
        near, mid = outer(own), middle(own)
        x0, y0 = xswap(own), yswap(own)
        tok = biases[:, :128]
        near, mid, x0, y0, tok = barrier((near, mid, x0, y0, tok))
        far_mid, far_end = middle(near), outward(mid)
        x1, diag0 = xswap(near), yswap(x0)
        small = (code_q, code_k, flags, biases, me, in_send, cot_send, fence(tok))
        x1, diag0, far_mid, far_end, small = barrier((x1, diag0, far_mid, far_end, small))
        code_q, code_k, flags, biases, me, in_send, cot_send, tok = small
        far = far_mid + far_end
        last_end = outward(far_mid)
        x2, y2 = xswap(far), yswap(far)
        x2, y2, last_end, tok = barrier((x2, y2, last_end, fence(tok)))
        last = mid + last_end
        x3, y3, y1 = xswap(last), yswap(last), outer(y0)
        x3, y3, y1, in_send, tok = barrier((x3, y3, y1, in_send, fence(tok)))
        diag3, diag2, diag1 = xswap(y3), yswap(x2), outer(diag0)
        in_other = yswap(in_send)
        diag3, diag2, diag1, cot_send, tok = barrier((diag3, diag2, diag1, cot_send, fence(tok)))
        me = after(me, fence(tok))
        pieces, places = [], []
        for jz, vals in enumerate(
            ((own, x0, y0, diag0), (near, x1, y1, diag1), (far, x2, y2, diag2), (last, x3, y3, diag3))
        ):
            pieces.extend(vals)
            places.extend([(0, 2 * jz), (0, 2 * jz + 1), (1, 2 * jz), (1, 2 * jz + 1)])
    else:
        every = lax.all_gather(master.astype(BF), "dp", axis=1, tiled=True)
        every_other = yswap(every)
        every = jnp.concatenate(
            [jnp.where(y == 0, every, every_other), jnp.where(y == 0, every_other, every)], axis=0
        )
        pieces, places = [pack_plain(every)], [(0, None)]
        in_other = yswap(in_send)
    w_qkv, w_out, w_up, w_down = build_weights(block_slot, me, pieces, tuple(places), slots)

    cot_other = yswap(cot_send)
    quarters = (in_mine, in_other, core(in_mine), core(in_other))
    proj, x_zero, x_in = project(flags, quarters, shared, w_qkv, biases, cot_other)
    cots = (cot_mine, cot_other, core(cot_mine), core(cot_other))
    context, probs, attn = attend(code_q, code_k, proj, w_out)
    h_in, normed, inverse, act, slope, ffn = feed(attn, core(attn), x_zero, shared, biases, w_up, w_down)
    rows_out, d_two, d_two_b, d_pre, d_hidden, sums_two, up_sums = feed_back(
        ffn, core(ffn), normed, slope, cots, shared, w_up, w_down
    )
    d_hidden_other = core(d_hidden)
    g_down = down_grads(act, d_two_b)
    d_one, g_qkv, g_out, d_in, sums_one, head_sums = attend_back(
        d_hidden, d_hidden_other, d_two, normed, inverse, shared, w_out, w_qkv, x_in, context, g_down, probs, proj
    )
    d_in_send = d_in[2 * RP :]

    def to_owner(arr):
        mine, other = arr[:quarter], yswap(arr[RP : RP + quarter])
        both = jnp.stack([mine, other])
        return jnp.where(y == 0, both, both[::-1])

    layer_out = to_owner(rows_out)
    me = after(me, layer_out)
    d_in_other = core(d_in_send)
    g_up = up_grads(h_in, d_pre, d_in)
    grad_rows, memory_grad = finish(flags, d_in, d_in_other, d_one)
    grads = (g_down, g_up, g_out, g_qkv, memory_grad)
    vec = jnp.concatenate([sums_one[:3], sums_two[:3], memory_grad[:MEM]], axis=0)
    halves = head_sums[:2].reshape(2, 2, 192).swapaxes(0, 1).reshape(2, 384)
    splits = jnp.concatenate([halves, up_sums], axis=1).reshape(3, 768)

    def add_core(vec):
        return jnp.concatenate([vec + core(vec), splits], axis=0)

    if meshed:
        per = master.shape[1] // GROUP
        half = per // 2
        places, shapes = [], []
        for jz in RS_ORDER:
            for jy in range(2):
                for jx in range(2):
                    places.append((jy, 2 * jz + jx))
                    shapes.append((per, TILES, 96, 128))
        token, *packed = pack_grads(block_slot, me, grads, tuple(places), shapes, slots)
        own, x_unit, y_unit, diag = {}, {}, {}, {}
        for n, jz in enumerate(RS_ORDER):
            own[jz], x_unit[jz], y_unit[jz], diag[jz] = packed[4 * n : 4 * n + 4]

        def plus(*vals):
            return sum(v.astype(F32) for v in vals).astype(BF)

        vec = after(add_core(vec), token)
        d3, d2, n1 = xswap(diag[3]), yswap(diag[2]), outer(diag[1])
        vec = vec + yswap(vec)
        d3, d2, n1, vec, tok = barrier((d3, d2, n1, vec, fence(token)))
        x3, y3, m1 = xswap(x_unit[3]), yswap(plus(y_unit[3], d3)), outer(y_unit[1])
        vec = vec + swap("dp", 1)(vec)
        x3, y3, m1, vec, tok = barrier((x3, y3, m1, vec, fence(tok)))
        x2, y2 = xswap(plus(x_unit[2], d2)), yswap(y_unit[2])
        part3 = plus(own[3], x3, y3)
        e3 = inward(part3)
        vec = vec + swap("dp", 2)(vec)
        x2, y2, e3, vec, tok = barrier((x2, y2, e3, vec, fence(tok)))
        x1, d0 = xswap(x_unit[1]), yswap(plus(diag[0], n1))
        part2 = plus(own[2], x2, y2, e3)
        fm, fe = middle(part2), inward(part2)
        vec = vec + swap("dp", 4)(vec)
        x1, d0, fm, fe, vec, tok = barrier((x1, d0, fm, fe, vec, fence(tok)))
        x0, y0 = xswap(plus(x_unit[0], d0)), yswap(plus(y_unit[0], m1))
        near, mid = outer(plus(own[1], x1, fm)), middle(plus(part3, fe))
        x0, y0, near, mid, grad_rows, tok = barrier((x0, y0, near, mid, grad_rows, fence(tok)))
        terms = (own[0], x0, y0, near, mid)
    else:
        packed = pack_grads(
            block_slot, me, grads, ((0, None),), [(2, slots // GROUP, TILES, 96, 128)], slots
        )[1]
        blocks = unpack_plain(packed)
        blocks = lax.psum_scatter(blocks, "dp", scatter_dimension=1, tiled=True)
        mine = lax.dynamic_index_in_dim(blocks, y, 0, keepdims=False)
        other = yswap(lax.dynamic_index_in_dim(blocks, 1 - y, 0, keepdims=False))
        terms = (mine.astype(F32) + other.astype(F32),)

        vec = add_core(vec)
        vec = vec + yswap(vec)
        step = 1
        while step < n_dp:
            vec = vec + swap("dp", step)(vec)
            step *= 2

    grad_in = to_owner(grad_rows)
    total_shared = vec[:16]
    grad_split = lax.dynamic_index_in_dim(vec[16:].reshape(2, -1), y, 0, keepdims=True)

    new_master, new_copy, new_first, new_second, new_left, new_right = soap(
        terms,
        master[0],
        first_moment[0],
        second_moment[0],
        left_stats[0],
        right_stats[0],
        left_basis[0],
        right_basis[0],
    )
    new_split, new_split_first, new_split_second = adam_update(
        split_params, grad_split, split_first, split_second, rate_vector
    )
    new_shared, new_shared_first, new_shared_second = adam_update(
        shared, total_shared, shared_first, shared_second, rate_shared
    )
    return (
        layer_out,
        grad_in,
        new_master[None],
        new_copy[None],
        new_first[None],
        new_second[None],
        new_left[None],
        new_right[None],
        new_split,
        new_split_first,
        new_split_second,
        new_shared,
        new_shared_first,
        new_shared_second,
    )


def solution(mesh):
    rows = P("dp", "tensor", None)
    state = P("tensor", "dp", None, None)
    split = P("tensor", None)
    return jax.shard_map(
        functools.partial(per_device, mesh.shape["dp"], mesh.shape["tensor"]),
        mesh=mesh,
        in_specs=(rows, rows, P("dp", None), P("dp"), P()) + (state,) * 7 + (split,) * 3 + (P(),) * 3,
        out_specs=(rows, rows) + (state,) * 6 + (split,) * 3 + (P(),) * 3,
        check_vma=False,
    )
```

```python
import functools

import jax
import jax.numpy as jnp
from jax import lax
from jax.experimental import pallas as pl
from jax.experimental.pallas import tpu as pltpu
from jax.sharding import PartitionSpec as P

HEADS = 12
HEAD_DIM = 64
FF = 3072
SEG_TOK = 512
MEM = 10
STEP = 10

beta_one = 0.9
beta_two = 0.95
adam_eps = 1e-08
norm_eps = 1e-12
rate_matrix = 0.05
rate_vector = 0.1
rate_shared = 0.75

BF = jnp.bfloat16
F32 = jnp.float32
VMEM_LIMIT = 24 * 1024 * 1024
BIG_LIMIT = 61 * 1024 * 1024
VMEM_SPEC = pl.BlockSpec(memory_space=pltpu.VMEM)
SMEM_SPEC = pl.BlockSpec(memory_space=pltpu.SMEM)
ANY_SPEC = pl.BlockSpec(memory_space=pl.ANY)
HBM_SPEC = pl.BlockSpec(memory_space=pltpu.HBM)
GROUP = 4
TILES = 3
UNROLL = 4
RP = 144
RS_ORDER = (3, 2, 1, 0)


def sds(shape, dtype):
    return jax.ShapeDtypeStruct(shape, dtype)


def params(limit=VMEM_LIMIT):
    return pltpu.CompilerParams(vmem_limit_bytes=limit)


def after(vals, deps):
    return lax.optimization_barrier((vals, deps))[0]


def cost(gflop, mbytes):
    return pl.CostEstimate(
        flops=int(gflop * 1e9), bytes_accessed=int(mbytes * 1e6), transcendentals=0
    )


def copy_body(v_ref, out_ref):
    out_ref[...] = v_ref[...]


def fence(token):
    return pl.pallas_call(
        copy_body,
        out_shape=sds(token.shape, token.dtype),
        in_specs=[VMEM_SPEC],
        out_specs=VMEM_SPEC,
        compiler_params=params(BIG_LIMIT),
        name="fence",
    )(token)


def xor_pairs(size, step):
    return [(i, i ^ step) for i in range(size)]


def z_pairs(pairs):
    return [(2 * a + x, 2 * b + x) for a, b in pairs for x in range(2)]


def pack_plain(blocks):
    lead = blocks.shape[:-3]
    grp = blocks.reshape(lead + (-1, GROUP, 96, 96))
    last = jnp.swapaxes(grp[..., 3, :, :].reshape(lead + (-1, 96, 3, 32)), -3, -2)
    return jnp.concatenate([grp[..., :3, :, :], last], axis=-1)


def unpack_plain(groups):
    last = jnp.swapaxes(groups[..., 96:], -3, -2)
    last = last.reshape(groups.shape[:-3] + (1, 96, 96))
    grp = jnp.concatenate([groups[..., :96], last], axis=-3)
    return grp.reshape(groups.shape[:-4] + (-1, 96, 96))


def pack_owned_body(m_ref, out_ref):
    for g in range(out_ref.shape[0]):
        last = m_ref[GROUP * g + 3].astype(BF)
        for k in range(TILES):
            out_ref[g, k] = jnp.concatenate(
                [m_ref[GROUP * g + k].astype(BF), last[:, 32 * k : 32 * k + 32]], axis=-1
            )


def pack_owned(blocks):
    n = blocks.shape[0] // GROUP
    return pl.pallas_call(
        pack_owned_body,
        out_shape=sds((n, TILES, 96, 128), BF),
        in_specs=[VMEM_SPEC],
        out_specs=VMEM_SPEC,
        compiler_params=params(),
        cost_estimate=cost(0.1, 2),
        name="pack_owned",
    )(blocks)


def weights_body(n_pieces, places, pos_ref, me_ref, *refs):
    pieces = refs[:n_pieces]
    outs = refs[n_pieces : n_pieces + 4]
    wqkv_ref, wo_ref, w1_ref, w2_ref, al, sems, out_sem = refs[n_pieces + 4 :]
    dp, y = me_ref[0], me_ref[1] // 2
    groups = al.shape[1]
    copies = []
    for ref, (jy, jd) in zip(pieces, places):
        n = ref.shape[-4]
        if jd is None:
            for s in range(2):
                dst = al.at[s, :, pl.ds(0, TILES)]
                copies.append(((s,), pltpu.make_async_copy(ref.at[s], dst, sems.at[s])))
        else:
            dst = al.at[y ^ jy, pl.ds((dp ^ jd) * n, n), pl.ds(0, TILES)]
            copies.append(((0, 1), pltpu.make_async_copy(ref, dst, sems.at[y ^ jy])))
    for _, copy in copies:
        copy.start()
    for s in range(2):
        whole = al.at[s, :, pl.ds(0, TILES)]
        pltpu.make_async_copy(whole, whole, sems.at[s]).wait()

        def fix(g, carry, s=s):
            rolled = [pltpu.roll(al[s, g, k], 32 + 32 * k, 1) for k in range(TILES)]
            lane = lax.broadcasted_iota(jnp.int32, rolled[0].shape, 1)
            al[s, g, 3] = jnp.where(lane < 32, rolled[0], jnp.where(lane < 64, rolled[1], rolled[2]))
            return carry

        lax.fori_loop(0, groups, fix, 0, unroll=16)

    def block(s, b):
        p = pos_ref[b]
        return al[s, p // GROUP, p % GROUP][:, :96]

    def strip_qkv(i, carry):
        rows = pl.ds(pl.multiple_of(i * 96, 96), 96)
        for part in range(3):
            wqkv_ref[rows, part * 384 : part * 384 + 384] = jnp.concatenate(
                [block(j // 2, i * 6 + part * 2 + j % 2) for j in range(4)], axis=-1
            )
        return carry

    def strip(i, carry, ref, first):
        rows = pl.ds(pl.multiple_of(i * 96, 96), 96)
        for s in range(2):
            for half in range(2):
                ref[s, rows, half * 384 : half * 384 + 384] = jnp.concatenate(
                    [block(s, first + i * 8 + half * 4 + j) for j in range(4)], axis=-1
                )
        return carry

    def send(k):
        copy = pltpu.make_async_copy((wqkv_ref, wo_ref, w1_ref, w2_ref)[k], outs[k], out_sem.at[k])
        copy.start()
        return copy

    lax.fori_loop(0, 8, functools.partial(strip, ref=w1_ref, first=64), 0, unroll=UNROLL)
    sent = [send(2)]
    lax.fori_loop(0, 8, functools.partial(strip, ref=w2_ref, first=128), 0, unroll=UNROLL)
    sent.append(send(3))
    lax.fori_loop(0, 8, strip_qkv, 0, unroll=UNROLL)
    sent.append(send(0))
    for i in range(4):
        for half in range(2):
            wo_ref[i * 96 : i * 96 + 96, half * 384 : half * 384 + 384] = jnp.concatenate(
                [block(i // 2, 48 + (i % 2) * 8 + half * 4 + j) for j in range(4)], axis=-1
            )
    sent.append(send(1))
    for copy in sent:
        copy.wait()


def build_weights(pos, me, pieces, places, slots):
    return pl.pallas_call(
        functools.partial(weights_body, len(pieces), places),
        out_shape=(
            sds((768, 1152), BF),
            sds((384, 768), BF),
            sds((2, 768, 768), BF),
            sds((2, 768, 768), BF),
        ),
        in_specs=[SMEM_SPEC, SMEM_SPEC] + [HBM_SPEC] * len(pieces),
        out_specs=(HBM_SPEC,) * 4,
        scratch_shapes=[
            pltpu.VMEM((768, 1152), BF),
            pltpu.VMEM((384, 768), BF),
            pltpu.VMEM((2, 768, 768), BF),
            pltpu.VMEM((2, 768, 768), BF),
            pltpu.VMEM((2, slots // GROUP, GROUP, 96, 128), BF),
            pltpu.SemaphoreType.DMA((2,)),
            pltpu.SemaphoreType.DMA((4,)),
        ],
        compiler_params=params(BIG_LIMIT),
        cost_estimate=cost(0.1, 30),
        name="build_weights",
    )(pos, me, *pieces)


def product(left, right, out, width=256):
    def step(i, carry):
        col = pl.multiple_of(i * width, width)
        out[pl.ds(col, width), :] = inner_rows(left[:, pl.ds(col, width)], right[...]).astype(BF)
        return carry

    lax.fori_loop(0, out.shape[0] // width, step, 0)


def down_grads_body(act_ref, d2_ref, out_ref):
    for s in range(2):
        product(act_ref.at[s], d2_ref, out_ref.at[s])


def up_grads_body(h_ref, dpre_ref, out_ref):
    for s in range(2):
        product(h_ref, dpre_ref.at[s], out_ref.at[s])


def down_grads(act, d_two):
    return pl.pallas_call(
        down_grads_body,
        out_shape=sds((2, 768, 768), BF),
        in_specs=[VMEM_SPEC] * 2,
        out_specs=VMEM_SPEC,
        compiler_params=params(),
        cost_estimate=cost(1.4, 8),
        name="down_grads",
    )(act, d_two)


def up_grads(h_in, d_pre):
    return pl.pallas_call(
        up_grads_body,
        out_shape=sds((2, 768, 768), BF),
        in_specs=[VMEM_SPEC] * 2,
        out_specs=VMEM_SPEC,
        compiler_params=params(),
        cost_estimate=cost(1.4, 8),
        name="up_grads",
    )(h_in, d_pre)


def tile_of(vals, j):
    if j < 3:
        return vals[:, 96 * j : 96 * j + 128]
    return pltpu.roll(vals[:, 256:384], 96, 1)


def pack_body(places, pos_ref, me_ref, *refs):
    token_ref = refs[5]
    outs = refs[6 : 6 + len(places)]
    g2, g1, go, gq, al, sem, sems = refs[6 + len(places) :]
    loads = [pltpu.make_async_copy(src, dst, sems.at[k]) for k, (src, dst) in enumerate(zip(refs, (g2, g1, go, gq)))]
    for load in loads:
        load.start()
    groups = al.shape[1]
    token_ref[...] = jnp.zeros_like(token_ref)

    def put(s, b, blk):
        p = pos_ref[b]
        al[s, p // GROUP, p % GROUP] = blk

    def strip(i, carry, ref, first):
        rows = pl.ds(pl.multiple_of(i * 96, 96), 96)
        for s in range(2):
            for half in range(2):
                vals = ref[s, rows, half * 384 : half * 384 + 384]
                for j in range(4):
                    put(s, first + i * 8 + half * 4 + j, tile_of(vals, j))
        return carry

    def strip_qkv(i, carry):
        rows = pl.ds(pl.multiple_of(i * 96, 96), 96)
        for part in range(3):
            vals = gq[rows, part * 384 : part * 384 + 384]
            for j in range(4):
                put(j // 2, i * 6 + part * 2 + j % 2, tile_of(vals, j))
        return carry

    loads[0].wait()
    lax.fori_loop(0, 8, functools.partial(strip, ref=g2, first=128), 0, unroll=UNROLL)
    loads[1].wait()
    lax.fori_loop(0, 8, functools.partial(strip, ref=g1, first=64), 0, unroll=UNROLL)
    loads[2].wait()
    for i in range(4):
        for half in range(2):
            vals = go[i * 96 : i * 96 + 96, half * 384 : half * 384 + 384]
            for j in range(4):
                put(i // 2, 48 + (i % 2) * 8 + half * 4 + j, tile_of(vals, j))
    loads[3].wait()
    lax.fori_loop(0, 8, strip_qkv, 0, unroll=UNROLL)

    dp, y = me_ref[0], me_ref[1] // 2
    copies = []
    for s in range(2):

        def fix(g, carry, s=s):
            last = al[s, g, 3]
            low = lax.broadcasted_iota(jnp.int32, last.shape, 1) < 96
            for k in range(TILES):
                al[s, g, k] = jnp.where(low, al[s, g, k], pltpu.roll(last, 96 - 32 * k, 1))
            return carry

        lax.fori_loop(0, groups, fix, 0, unroll=16)
        for ref, (jy, jd) in zip(outs, places):
            if jd is None:
                copies.append((None, pltpu.make_async_copy(al.at[s, :, pl.ds(0, TILES)], ref.at[s], sem)))
            else:
                n = ref.shape[0]
                src = al.at[s, pl.ds((dp ^ jd) * n, n), pl.ds(0, TILES)]
                copies.append(((y ^ jy) == s, pltpu.make_async_copy(src, ref, sem)))
        for mine, copy in copies[s * len(outs) :]:
            if mine is None:
                copy.start()
            else:
                pl.when(mine)(copy.start)
    for mine, copy in copies:
        if mine is None:
            copy.wait()
        else:
            pl.when(mine)(copy.wait)


def pack_grads(pos, me, grads, places, out_shapes, slots):
    return pl.pallas_call(
        functools.partial(pack_body, places),
        out_shape=(sds((8, 128), F32), *(sds(s, BF) for s in out_shapes)),
        in_specs=[SMEM_SPEC, SMEM_SPEC] + [HBM_SPEC] * 4 + [ANY_SPEC],
        out_specs=(VMEM_SPEC,) + (HBM_SPEC,) * len(places),
        scratch_shapes=[
            pltpu.VMEM((2, 768, 768), BF),
            pltpu.VMEM((2, 768, 768), BF),
            pltpu.VMEM((384, 768), BF),
            pltpu.VMEM((768, 1152), BF),
            pltpu.VMEM((2, slots // GROUP, GROUP, 96, 128), BF),
            pltpu.SemaphoreType.DMA,
            pltpu.SemaphoreType.DMA((4,)),
        ],
        compiler_params=params(BIG_LIMIT),
        cost_estimate=cost(0.1, 30),
        name="pack_grads",
    )(pos, me, *grads)


def project_body(flags_ref, xa, xb, xc, xd, sh_ref, w_ref, b_ref, later_ref, proj_ref, x0_ref, xin_ref, bias):
    @pl.when(pl.program_id(0) == 0)
    def _():
        n = xa.shape[0]
        gap = jnp.zeros((RP - n, x0_ref.shape[1]), F32)
        for k, ref in enumerate((xa, xb, xc, xd)):
            x0_ref[k * RP : k * RP + n, :] = ref[...].astype(F32)
            x0_ref[k * RP + n : k * RP + RP, :] = gap

            @pl.when((flags_ref[0] == k) & (flags_ref[1] == 1))
            def _(k=k):
                x0_ref[k * RP : k * RP + MEM, :] = sh_ref[6 : 6 + MEM, :]

        xin_ref[...] = x0_ref[...].astype(BF)
        for part, col in ((0, 0), (2, 192)):
            bias[part] = jnp.concatenate([b_ref[s : s + 1, col : col + 192] for s in range(2)], axis=1)
        bias[1] = jnp.zeros((1, 384), F32)

    proj_ref[...] = (dot(xin_ref[...], w_ref[...]) + bias[pl.program_id(0)]).astype(BF)


def project(flags, quarters, shared, w_qkv, biases, later):
    rows = 4 * RP

    def whole(shape):
        return pl.BlockSpec(shape, lambda i: (0, 0))

    return pl.pallas_call(
        project_body,
        grid=(3,),
        out_shape=(sds((rows, 1152), BF), sds((rows, 768), F32), sds((rows, 768), BF)),
        in_specs=[
            SMEM_SPEC,
            *[whole(q.shape) for q in quarters],
            whole(shared.shape),
            pl.BlockSpec((768, 384), lambda i: (0, i)),
            whole(biases.shape),
            ANY_SPEC,
        ],
        out_specs=(
            pl.BlockSpec((rows, 384), lambda i: (0, i)),
            whole((rows, 768)),
            whole((rows, 768)),
        ),
        scratch_shapes=[pltpu.VMEM((3, 1, 384), F32)],
        compiler_params=params(),
        cost_estimate=cost(1.0, 5),
        name="project",
    )(flags, *quarters, shared, w_qkv, biases, later)


def head_masks(shape):
    lane = lax.broadcasted_iota(jnp.int32, shape, 1)
    return lane < HEAD_DIM, lane >= HEAD_DIM


def attend_body(cq_ref, ck_ref, q_ref, k_ref, v_ref, wo_ref, ctx_ref, p_ref, part_ref, vis):
    h = pl.program_id(0)

    @pl.when(h == 0)
    def _():
        cq, ck = cq_ref[...], ck_ref[...]
        seen = ((cq == -1) | (ck == -1) | (cq == ck)) & (ck != -2)
        vis[...] = jnp.where(seen, 1.0, 0.0)

    q, k, v = q_ref[...], k_ref[...], v_ref[...]
    masks = head_masks(q.shape)
    outs = []
    for n in range(2):
        qh = jnp.where(masks[n], q, jnp.zeros_like(q))
        scores = jnp.where(vis[...] > 0.5, dot_back(qh, k) * HEAD_DIM ** (-0.5), -1000000000.0)
        e = jnp.exp(scores - jnp.max(scores, axis=-1, keepdims=True))
        p = (e * (1.0 / jnp.sum(e, axis=-1, keepdims=True))).astype(BF)
        p_ref[n] = p
        outs.append(dot(p, v))
    ctx_ref[:, pl.ds(pl.multiple_of(h * 128, 128), 128)] = jnp.where(masks[0], outs[0], outs[1]).astype(BF)

    @pl.when(h == pl.num_programs(0) - 1)
    def _():
        part_ref[...] = dot(ctx_ref[...], wo_ref[...]).astype(BF)


def head_col(rows, off):
    return pl.BlockSpec((rows, 128), lambda h: (0, h + off))


def all_steps(shape):
    return pl.BlockSpec(shape, lambda h: (0,) * len(shape))


def attend(code_q, code_k, proj, w_out):
    rows = proj.shape[0]
    pairs = HEADS // 4
    return pl.pallas_call(
        attend_body,
        grid=(pairs,),
        out_shape=(sds((rows, 384), BF), sds((2 * pairs, rows, rows), BF), sds((rows, 768), BF)),
        in_specs=[
            all_steps((rows, 1)),
            all_steps((1, rows)),
            head_col(rows, 0),
            head_col(rows, pairs),
            head_col(rows, 2 * pairs),
            all_steps((384, 768)),
        ],
        out_specs=(
            all_steps((rows, 384)),
            pl.BlockSpec((2, rows, rows), lambda h: (h, 0, 0)),
            all_steps((rows, 768)),
        ),
        scratch_shapes=[pltpu.VMEM((rows, rows), F32)],
        compiler_params=params(),
        cost_estimate=cost(2.5, 8),
        name="attend",
    )(code_q, code_k, proj, proj, proj, w_out)


def both_cores(mine_ref, other_ref):
    half = mine_ref.shape[0] // 2
    other = jnp.concatenate([other_ref[half:, :], other_ref[:half, :]], axis=0)
    return mine_ref[...].astype(F32) + other.astype(F32)


def col_sum(v):
    return jnp.sum(v, axis=0, keepdims=True)


def feed_body(mine_ref, other_ref, x0_ref, sh_ref, b_ref, w1_hbm, w2_hbm, h_ref, n_ref, r_ref, act_ref, slope_ref, part_ref, w1, w2, acc, sems):
    copies = []
    for s in range(2):
        copies.append(pltpu.make_async_copy(w1_hbm.at[s], w1.at[s], sems.at[s]))
        copies.append(pltpu.make_async_copy(w2_hbm.at[s], w2.at[s], sems.at[2 + s]))
    for copy in copies:
        copy.start()
    total = both_cores(mine_ref, other_ref) + sh_ref[0:1, :] + x0_ref[...]
    h_one, normed, inverse = norm_parts(total, sh_ref[1:2, :], sh_ref[2:3, :])
    h_ref[...] = h_one.astype(BF)
    n_ref[...] = normed
    r_ref[...] = inverse
    for s in range(2):
        copies[2 * s].wait()
        pre = dot(h_ref[...], w1[s]) + b_ref[s : s + 1, 384:]
        cdf = 0.5 * (1.0 + lax.erf(pre * 0.7071067811865476))
        act_ref[s] = (pre * cdf).astype(BF)
        slope_ref[s] = (cdf + pre * jnp.exp(-0.5 * pre * pre) * 0.3989422804014327).astype(BF)
        copies[2 * s + 1].wait()
        part = dot(act_ref[s], w2[s])
        acc[...] = part if s == 0 else acc[...] + part
    part_ref[...] = acc[...].astype(BF)


def feed(mine, other, x_zero, shared, biases, w1, w2):
    rows = x_zero.shape[0]
    one, two = sds((rows, 768), BF), sds((2, rows, 768), BF)
    return pl.pallas_call(
        feed_body,
        out_shape=(one, sds((rows, 768), F32), sds((rows, 1), F32), two, two, one),
        in_specs=[VMEM_SPEC] * 5 + [ANY_SPEC] * 2,
        out_specs=(VMEM_SPEC,) * 6,
        scratch_shapes=[
            pltpu.VMEM((2, 768, 768), BF),
            pltpu.VMEM((2, 768, 768), BF),
            pltpu.VMEM((rows, 768), F32),
            pltpu.SemaphoreType.DMA((4,)),
        ],
        compiler_params=params(),
        cost_estimate=cost(2.8, 16),
        name="feed",
    )(mine, other, x_zero, shared, biases, w1, w2)


def feed_back_body(mine_ref, other_ref, n_ref, slope_ref, ca, cb, cc, cd, sh_ref, w1_hbm, w2_hbm, out_ref, d2_ref, d2b_ref, dpre_ref, part_ref, sums_ref, bsum_ref, w1, w2, g, acc, sems):
    copies = []
    for s in range(2):
        copies.append(pltpu.make_async_copy(w2_hbm.at[s], w2.at[s], sems.at[2 + s]))
        copies.append(pltpu.make_async_copy(w1_hbm.at[s], w1.at[s], sems.at[s]))
    for copy in copies:
        copy.start()
    n = ca.shape[0]
    for k, ref in enumerate((ca, cb, cc, cd)):
        g[k * RP : k * RP + n, :] = ref[...].astype(F32)
        g[k * RP + n : k * RP + RP, :] = jnp.zeros((RP - n, 768), F32)
    own = g.shape[0] // 2

    def row(i):
        return sh_ref[i : i + 1, :]

    h_one = n_ref[...] * row(1) + row(2)
    total = both_cores(mine_ref, other_ref) + row(3) + h_one
    rows_out, normed, inverse = norm_parts(total, row(4), row(5))
    out_ref[...] = rows_out[:own].astype(BF)
    grad = g[...]
    d_two = norm_back(grad, normed, inverse, row(4))
    d2_ref[...] = d_two
    d2b_ref[...] = d_two.astype(BF)
    sums_ref[0:3, :] = jnp.concatenate(
        [col_sum(d_two[:own]), col_sum(grad[:own] * normed[:own]), col_sum(grad[:own])], axis=0
    )
    sums_ref[3:8, :] = jnp.zeros((5, 768), F32)
    for s in range(2):
        copies[2 * s].wait()
        d_pre = dot_back(d2b_ref[...], w2[s]) * slope_ref[s].astype(F32)
        bsum_ref[s : s + 1, :] = col_sum(d_pre)
        dpre_ref[s] = d_pre.astype(BF)
        copies[2 * s + 1].wait()
        part = dot_back(dpre_ref[s], w1[s])
        acc[...] = part if s == 0 else acc[...] + part
    part_ref[...] = acc[...].astype(BF)


def feed_back(mine, other, normed, slope, cots, shared, w1, w2):
    rows = normed.shape[0]
    one = sds((rows, 768), BF)
    return pl.pallas_call(
        feed_back_body,
        out_shape=(
            sds((rows // 2, 768), BF),
            sds((rows, 768), F32),
            one,
            sds((2, rows, 768), BF),
            one,
            sds((8, 768), F32),
            sds((2, 768), F32),
        ),
        in_specs=[VMEM_SPEC] * 9 + [ANY_SPEC] * 2,
        out_specs=(VMEM_SPEC,) * 7,
        scratch_shapes=[
            pltpu.VMEM((2, 768, 768), BF),
            pltpu.VMEM((2, 768, 768), BF),
            pltpu.VMEM((rows, 768), F32),
            pltpu.VMEM((rows, 768), F32),
            pltpu.SemaphoreType.DMA((4,)),
        ],
        compiler_params=params(),
        cost_estimate=cost(2.8, 16),
        name="feed_back",
    )(mine, other, normed, slope, *cots, shared, w1, w2)


def attend_back_body(mine_ref, other_ref, d2_ref, n_ref, r_ref, sh_ref, wo_ref, wqkv_ref, x_ref, ctx_ref, later_ref, p_ref, q_ref, k_ref, v_ref, d1_ref, gq_ref, go_ref, part_ref, send_ref, sums_ref, bsum_ref, d1b_ref, dproj_ref, dctx):
    h = pl.program_id(0)
    pairs = pl.num_programs(0)
    own = d1_ref.shape[0]

    @pl.when(h == 0)
    def _():
        dh = both_cores(mine_ref, other_ref) + d2_ref[...]
        normed = n_ref[...]
        d_one = norm_back(dh, normed, r_ref[...], sh_ref[1:2, :])
        d1_ref[...] = d_one[:own]
        d1b_ref[...] = d_one.astype(BF)
        sums_ref[0:3, :] = jnp.concatenate(
            [col_sum(d_one[:own]), col_sum(dh[:own] * normed[:own]), col_sum(dh[:own])], axis=0
        )
        sums_ref[3:8, :] = jnp.zeros((5, 768), F32)
        back = dot_back(d1b_ref[...], wo_ref[...]).astype(BF)
        for m in range(3):
            dctx[m] = back[:, m * 128 : m * 128 + 128]

    q, k, v, dc = q_ref[...], k_ref[...], v_ref[...], dctx[h]
    masks = head_masks(q.shape)
    dqs, dks, dvs = [], [], []
    for m in range(2):
        dch = jnp.where(masks[m], dc, jnp.zeros_like(dc))
        p = p_ref[m]
        dvs.append(inner_rows(p, dc))
        dp = dot_back(dch, v)
        pf = p.astype(F32)
        row = jnp.sum(dp * pf, axis=-1, keepdims=True)
        ds = (pf * (dp - row) * HEAD_DIM ** (-0.5)).astype(BF)
        dqs.append(dot(ds, k))
        dks.append(inner_rows(ds, q))
    dq, dk, dv = (jnp.where(masks[0], d[0], d[1]) for d in (dqs, dks, dvs))
    for part, d in enumerate((dq, dk, dv)):
        dproj_ref[:, pl.ds(pl.multiple_of(part * 384 + h * 128, 128), 128)] = d.astype(BF)
    bsum_ref[...] = jnp.concatenate([col_sum(dq), col_sum(dv), jnp.zeros((6, 128), F32)], axis=0)

    @pl.when(h == pairs - 1)
    def _():
        share = dot_back(dproj_ref[...], wqkv_ref[...]).astype(BF)
        part_ref[...] = share[:own]
        send_ref[...] = share[own:]
        product(ctx_ref, d1b_ref, go_ref, 128)
        product(x_ref, dproj_ref, gq_ref)


def attend_back(mine, other, d_two, normed, inverse, shared, w_out, w_qkv, x_in, context, later, probs, proj):
    rows = proj.shape[0]
    pairs = HEADS // 4
    return pl.pallas_call(
        attend_back_body,
        grid=(pairs,),
        out_shape=(
            sds((rows // 2, 768), F32),
            sds((768, 1152), BF),
            sds((384, 768), BF),
            sds((rows // 2, 768), BF),
            sds((rows // 2, 768), BF),
            sds((8, 768), F32),
            sds((8, 384), F32),
        ),
        in_specs=[
            all_steps((rows, 768)),
            all_steps((rows, 768)),
            all_steps((rows, 768)),
            all_steps((rows, 768)),
            all_steps((rows, 1)),
            all_steps(shared.shape),
            all_steps((384, 768)),
            all_steps((768, 1152)),
            all_steps((rows, 768)),
            all_steps((rows, 384)),
            ANY_SPEC,
            pl.BlockSpec((2, rows, rows), lambda h: (h, 0, 0)),
            head_col(rows, 0),
            head_col(rows, pairs),
            head_col(rows, 2 * pairs),
        ],
        out_specs=(
            all_steps((rows // 2, 768)),
            all_steps((768, 1152)),
            all_steps((384, 768)),
            all_steps((rows // 2, 768)),
            all_steps((rows // 2, 768)),
            all_steps((8, 768)),
            pl.BlockSpec((8, 128), lambda h: (0, h)),
        ),
        scratch_shapes=[
            pltpu.VMEM((rows, 768), BF),
            pltpu.VMEM((rows, 1152), BF),
            pltpu.VMEM((3, rows, 128), BF),
        ],
        compiler_params=params(),
        cost_estimate=pl.CostEstimate(
            flops=2 * rows * rows * 64 * 4 * HEADS, bytes_accessed=10 * 1024 * 1024, transcendentals=0
        ),
        name="attend_back",
    )(mine, other, d_two, normed, inverse, shared, w_out, w_qkv, x_in, context, later, probs, proj, proj, proj)


def finish_body(flags_ref, part_ref, other_ref, d1_ref, gin_ref, mem_ref):
    d_zero = part_ref[...].astype(F32) + other_ref[...].astype(F32) + d1_ref[...]
    gin_ref[...] = d_zero.astype(BF)
    mem_ref[...] = jnp.zeros_like(mem_ref)
    for k in range(2):

        @pl.when((flags_ref[0] == k) & (flags_ref[1] == 1))
        def _(k=k):
            row = lax.broadcasted_iota(jnp.int32, (16, d_zero.shape[1]), 0)
            top = d_zero[k * RP : k * RP + 16, :]
            mem_ref[...] = jnp.where(row < MEM, top, 0.0)
            gin_ref[k * RP : k * RP + 16, :] = jnp.where(row < MEM, 0.0, top).astype(BF)


def finish(flags, part, other, d_one):
    return pl.pallas_call(
        finish_body,
        out_shape=(sds(d_one.shape, BF), sds((16, 768), F32)),
        in_specs=[SMEM_SPEC] + [VMEM_SPEC] * 3,
        out_specs=(VMEM_SPEC,) * 2,
        compiler_params=params(),
        cost_estimate=cost(0.1, 4),
        name="finish",
    )(flags, part, other, d_one)


def soap_body(n_terms, *refs):
    terms = refs[:n_terms]
    w_ref, m_ref, v_ref, sl_ref, sr_ref, l_ref, r_ref = refs[n_terms : n_terms + 7]
    nw_ref, nc_ref, nm_ref, nv_ref, nl_ref, nr_ref = refs[n_terms + 7 :]
    blocks = w_ref.shape[0]
    if n_terms == 1:
        grads = [terms[0][b] for b in range(blocks)]
    else:
        grads = []
        for g in range(blocks // GROUP):
            tiles = [sum(ref[g, k].astype(F32) for ref in terms) for k in range(TILES)]
            grads += [tile[:, :96] for tile in tiles]
            grads.append(jnp.concatenate([tile[:, 96:] for tile in tiles], axis=-1))
    every = range(blocks)
    gb = [g.astype(BF) for g in grads]
    lb, rb = [l_ref[b].astype(BF) for b in every], [r_ref[b].astype(BF) for b in every]
    half = [inner_rows(lb[b], gb[b]).astype(BF) for b in every]
    for b in every:
        nl_ref[b] = beta_two * sl_ref[b] + (1.0 - beta_two) * dot_back(gb[b], gb[b])
    turned = [dot(half[b], rb[b]) for b in every]
    for b in every:
        nr_ref[b] = beta_two * sr_ref[b] + (1.0 - beta_two) * inner_rows(gb[b], gb[b])
    steps = []
    for b in every:
        new_first = beta_one * m_ref[b] + (1.0 - beta_one) * turned[b]
        new_second = beta_two * v_ref[b] + (1.0 - beta_two) * turned[b] * turned[b]
        nm_ref[b] = new_first
        nv_ref[b] = new_second
        direction = (
            new_first
            / (1.0 - beta_one**STEP)
            / (jnp.sqrt(new_second / (1.0 - beta_two**STEP)) + adam_eps)
        )
        steps.append(direction.astype(BF))
    half = [dot(lb[b], steps[b]).astype(BF) for b in every]
    for b in every:
        new_weight = w_ref[b] - rate_matrix * dot_back(half[b], rb[b])
        nw_ref[b] = new_weight
        nc_ref[b] = new_weight.astype(BF)


def soap(terms, master, first, second, left, right, left_rot, right_rot):
    count = master.shape[0]
    many = next(n for n in (3, 2, 1) if terms[0].shape[0] % n == 0)
    step = many * GROUP if len(terms) > 1 else 1
    spec = pl.BlockSpec((step, 96, 96), lambda i: (i, 0, 0))
    packed = pl.BlockSpec((many, TILES, 96, 128), lambda i: (i, 0, 0, 0))
    full = sds(master.shape, F32)
    return pl.pallas_call(
        functools.partial(soap_body, len(terms)),
        grid=(count // step,),
        out_shape=(full, sds(master.shape, BF), full, full, full, full),
        in_specs=[packed if len(terms) > 1 else spec] * len(terms) + [spec] * 7,
        out_specs=(spec,) * 6,
        compiler_params=params(BIG_LIMIT),
        cost_estimate=cost(0.3, 24),
        name="soap",
    )(*terms, master, first, second, left, right, left_rot, right_rot)


def norm_parts(values, gain_vec, shift_vec):
    centred = values - jnp.mean(values, axis=-1, keepdims=True)
    inverse = lax.rsqrt(jnp.mean(centred * centred, axis=-1, keepdims=True) + norm_eps)
    normed = centred * inverse
    return (normed * gain_vec + shift_vec, normed, inverse)


def norm_back(upstream, normed, inverse, gain_vec):
    scaled = upstream * gain_vec
    result = inverse * (
        scaled
        - jnp.mean(scaled, axis=-1, keepdims=True)
        - normed * jnp.mean(scaled * normed, axis=-1, keepdims=True)
    )
    return result


def dot(left, right):
    return jnp.dot(left, right, preferred_element_type=F32)


def dot_back(left, right):
    return lax.dot_general(left, right, (((1,), (1,)), ((), ())), preferred_element_type=F32)


def inner_rows(left, right):
    return lax.dot_general(left, right, (((0,), (0,)), ((), ())), preferred_element_type=F32)


def adam_update(values, grad_vec, first_mom, second_mom, step_rate):
    new_first = beta_one * first_mom + (1.0 - beta_one) * grad_vec
    new_second = beta_two * second_mom + (1.0 - beta_two) * grad_vec * grad_vec
    direction = (
        new_first
        / (1.0 - beta_one**STEP)
        / (jnp.sqrt(new_second / (1.0 - beta_two**STEP)) + adam_eps)
    )
    return (values - step_rate * direction, new_first, new_second)


def per_device(
    n_dp,
    n_tensor,
    layer_in,
    cotangent,
    doc_ids,
    reset_flags,
    block_slot,
    master,
    first_moment,
    second_moment,
    left_stats,
    right_stats,
    left_basis,
    right_basis,
    split_params,
    split_first,
    split_second,
    shared,
    shared_first,
    shared_second,
):
    meshed = n_dp == 8 and master.shape[1] % GROUP == 0
    dp = lax.axis_index("dp")
    t = lax.axis_index("tensor")
    y, c = t // 2, t % 2
    me = jnp.stack([dp, t])
    barrier = lax.optimization_barrier
    slots = block_slot.shape[0]
    quarter = layer_in.shape[1]

    def swap(axis, step):
        size = n_dp if axis == "dp" else n_tensor
        return lambda v: lax.ppermute(v, axis, xor_pairs(size, step))

    core, yswap, xswap = swap("tensor", 1), swap("tensor", 2), swap("dp", 1)

    def along_z(*pairs):
        return lambda v: lax.ppermute(v, "dp", z_pairs(pairs))

    outer, middle = along_z((0, 1), (1, 0), (2, 3), (3, 2)), along_z((1, 2), (2, 1))
    inward, outward = along_z((0, 1), (3, 2)), along_z((1, 0), (2, 3))

    docs = lax.dynamic_index_in_dim(doc_ids, y, 0, keepdims=False)
    edge = jnp.full((MEM,), -1, jnp.int32)
    codes = jnp.concatenate([edge, docs, edge]).reshape(4, quarter)
    codes = jnp.pad(codes, ((0, 0), (0, RP - quarter)), constant_values=-2)
    codes = jnp.concatenate(
        [lax.dynamic_index_in_dim(codes, t ^ j, 0, keepdims=False) for j in (0, 2, 1, 3)]
    )
    code_q, code_k = codes[:, None], codes[None, :]
    reset_now = lax.dynamic_index_in_dim(reset_flags, y, 0, keepdims=False) == 1
    flags = jnp.stack([y + 2 * c, reset_now.astype(jnp.int32)])

    split_other = yswap(split_params)
    biases = jnp.concatenate(
        [jnp.where(y == 0, split_params, split_other), jnp.where(y == 0, split_other, split_params)], axis=0
    )
    def inputs_of(arr):
        mine = lax.dynamic_index_in_dim(arr, y, 0, keepdims=False)
        other = lax.dynamic_index_in_dim(arr, 1 - y, 0, keepdims=False)
        return mine, other

    (in_mine, in_send), (cot_mine, cot_send) = inputs_of(layer_in), inputs_of(cotangent)

    if meshed:
        own = pack_owned(master[0])
        near, mid = outer(own), middle(own)
        x0, y0 = xswap(own), yswap(own)
        tok = biases[:, :128]
        near, mid, x0, y0, tok = barrier((near, mid, x0, y0, tok))
        far_mid, far_end = middle(near), outward(mid)
        x1, diag0 = xswap(near), yswap(x0)
        small = (code_q, code_k, flags, biases, me, in_send, cot_send, fence(tok))
        x1, diag0, far_mid, far_end, small = barrier((x1, diag0, far_mid, far_end, small))
        code_q, code_k, flags, biases, me, in_send, cot_send, tok = small
        far = far_mid + far_end
        last_end = outward(far_mid)
        x2, y2 = xswap(far), yswap(far)
        x2, y2, last_end, tok = barrier((x2, y2, last_end, fence(tok)))
        last = mid + last_end
        x3, y3, y1 = xswap(last), yswap(last), outer(y0)
        x3, y3, y1, in_send, tok = barrier((x3, y3, y1, in_send, fence(tok)))
        diag3, diag2, diag1 = xswap(y3), yswap(x2), outer(diag0)
        in_other = yswap(in_send)
        diag3, diag2, diag1, cot_send, tok = barrier((diag3, diag2, diag1, cot_send, fence(tok)))
        me = after(me, fence(tok))
        pieces, places = [], []
        for jz, vals in enumerate(
            ((own, x0, y0, diag0), (near, x1, y1, diag1), (far, x2, y2, diag2), (last, x3, y3, diag3))
        ):
            pieces.extend(vals)
            places.extend([(0, 2 * jz), (0, 2 * jz + 1), (1, 2 * jz), (1, 2 * jz + 1)])
    else:
        every = lax.all_gather(master.astype(BF), "dp", axis=1, tiled=True)
        every_other = yswap(every)
        every = jnp.concatenate(
            [jnp.where(y == 0, every, every_other), jnp.where(y == 0, every_other, every)], axis=0
        )
        pieces, places = [pack_plain(every)], [(0, None)]
        in_other = yswap(in_send)
    w_qkv, w_out, w_up, w_down = build_weights(block_slot, me, pieces, tuple(places), slots)

    cot_other = yswap(cot_send)
    quarters = (in_mine, in_other, core(in_mine), core(in_other))
    proj, x_zero, x_in = project(flags, quarters, shared, w_qkv, biases, cot_other)
    cots = (cot_mine, cot_other, core(cot_mine), core(cot_other))
    context, probs, attn = attend(code_q, code_k, proj, w_out)
    h_in, normed, inverse, act, slope, ffn = feed(attn, core(attn), x_zero, shared, biases, w_up, w_down)
    rows_out, d_two, d_two_b, d_pre, d_hidden, sums_two, up_sums = feed_back(
        ffn, core(ffn), normed, slope, cots, shared, w_up, w_down
    )
    d_hidden_other = core(d_hidden)
    g_down, g_up = down_grads(act, d_two_b), up_grads(h_in, d_pre)
    d_one, g_qkv, g_out, d_in, d_in_send, sums_one, head_sums = attend_back(
        d_hidden, d_hidden_other, d_two, normed, inverse, shared, w_out, w_qkv, x_in, context, g_down, probs, proj
    )
    def to_owner(arr):
        mine, other = arr[:quarter], yswap(arr[RP : RP + quarter])
        both = jnp.stack([mine, other])
        return jnp.where(y == 0, both, both[::-1])

    layer_out = to_owner(rows_out)
    me = after(me, layer_out)
    d_in_other = core(d_in_send)
    grad_rows, memory_grad = finish(flags, d_in, d_in_other, d_one)
    grads = (g_down, g_up, g_out, g_qkv, memory_grad)
    vec = jnp.concatenate([sums_one[:3], sums_two[:3], memory_grad[:MEM]], axis=0)
    halves = head_sums[:2].reshape(2, 2, 192).swapaxes(0, 1).reshape(2, 384)
    splits = jnp.concatenate([halves, up_sums], axis=1).reshape(3, 768)

    def add_core(vec):
        return jnp.concatenate([vec + core(vec), splits], axis=0)

    if meshed:
        per = master.shape[1] // GROUP
        half = per // 2
        places, shapes = [], []
        for jz in RS_ORDER:
            for jy in range(2):
                for jx in range(2):
                    places.append((jy, 2 * jz + jx))
                    shapes.append((per, TILES, 96, 128))
        token, *packed = pack_grads(block_slot, me, grads, tuple(places), shapes, slots)
        own, x_unit, y_unit, diag = {}, {}, {}, {}
        for n, jz in enumerate(RS_ORDER):
            own[jz], x_unit[jz], y_unit[jz], diag[jz] = packed[4 * n : 4 * n + 4]

        def plus(*vals):
            return sum(v.astype(F32) for v in vals).astype(BF)

        vec = after(add_core(vec), token)
        d3, d2, n1 = xswap(diag[3]), yswap(diag[2]), outer(diag[1])
        vec = vec + yswap(vec)
        d3, d2, n1, vec, tok = barrier((d3, d2, n1, vec, fence(token)))
        x3, y3, m1 = xswap(x_unit[3]), yswap(plus(y_unit[3], d3)), outer(y_unit[1])
        vec = vec + swap("dp", 1)(vec)
        x3, y3, m1, vec, tok = barrier((x3, y3, m1, vec, fence(tok)))
        x2, y2 = xswap(plus(x_unit[2], d2)), yswap(y_unit[2])
        part3 = plus(own[3], x3, y3)
        e3 = inward(part3)
        vec = vec + swap("dp", 2)(vec)
        x2, y2, e3, vec, tok = barrier((x2, y2, e3, vec, fence(tok)))
        x1, d0 = xswap(x_unit[1]), yswap(plus(diag[0], n1))
        part2 = plus(own[2], x2, y2, e3)
        fm, fe = middle(part2), inward(part2)
        vec = vec + swap("dp", 4)(vec)
        x1, d0, fm, fe, vec, tok = barrier((x1, d0, fm, fe, vec, fence(tok)))
        x0, y0 = xswap(plus(x_unit[0], d0)), yswap(plus(y_unit[0], m1))
        near, mid = outer(plus(own[1], x1, fm)), middle(plus(part3, fe))
        x0, y0, near, mid, grad_rows, tok = barrier((x0, y0, near, mid, grad_rows, fence(tok)))
        terms = (own[0], x0, y0, near, mid)
    else:
        packed = pack_grads(
            block_slot, me, grads, ((0, None),), [(2, slots // GROUP, TILES, 96, 128)], slots
        )[1]
        blocks = unpack_plain(packed)
        blocks = lax.psum_scatter(blocks, "dp", scatter_dimension=1, tiled=True)
        mine = lax.dynamic_index_in_dim(blocks, y, 0, keepdims=False)
        other = yswap(lax.dynamic_index_in_dim(blocks, 1 - y, 0, keepdims=False))
        terms = (mine.astype(F32) + other.astype(F32),)

        vec = add_core(vec)
        vec = vec + yswap(vec)
        step = 1
        while step < n_dp:
            vec = vec + swap("dp", step)(vec)
            step *= 2

    grad_in = to_owner(grad_rows)
    total_shared = vec[:16]
    grad_split = lax.dynamic_index_in_dim(vec[16:].reshape(2, -1), y, 0, keepdims=True)

    new_master, new_copy, new_first, new_second, new_left, new_right = soap(
        terms,
        master[0],
        first_moment[0],
        second_moment[0],
        left_stats[0],
        right_stats[0],
        left_basis[0],
        right_basis[0],
    )
    new_split, new_split_first, new_split_second = adam_update(
        split_params, grad_split, split_first, split_second, rate_vector
    )
    new_shared, new_shared_first, new_shared_second = adam_update(
        shared, total_shared, shared_first, shared_second, rate_shared
    )
    return (
        layer_out,
        grad_in,
        new_master[None],
        new_copy[None],
        new_first[None],
        new_second[None],
        new_left[None],
        new_right[None],
        new_split,
        new_split_first,
        new_split_second,
        new_shared,
        new_shared_first,
        new_shared_second,
    )


def solution(mesh):
    rows = P("dp", "tensor", None)
    state = P("tensor", "dp", None, None)
    split = P("tensor", None)
    return jax.shard_map(
        functools.partial(per_device, mesh.shape["dp"], mesh.shape["tensor"]),
        mesh=mesh,
        in_specs=(rows, rows, P("dp", None), P("dp"), P()) + (state,) * 7 + (split,) * 3 + (P(),) * 3,
        out_specs=(rows, rows) + (state,) * 6 + (split,) * 3 + (P(),) * 3,
        check_vma=False,
    )
```

```python
import functools

import jax
import jax.numpy as jnp
from jax import lax
from jax.experimental import pallas as pl
from jax.experimental.pallas import tpu as pltpu
from jax.sharding import PartitionSpec as P

HEADS = 12
HEAD_DIM = 64
FF = 3072
SEG_TOK = 512
MEM = 10
STEP = 10

beta_one = 0.9
beta_two = 0.95
adam_eps = 1e-08
norm_eps = 1e-12
rate_matrix = 0.05
rate_vector = 0.1
rate_shared = 0.75

BF = jnp.bfloat16
F32 = jnp.float32
VMEM_LIMIT = 24 * 1024 * 1024
BIG_LIMIT = 61 * 1024 * 1024
VMEM_SPEC = pl.BlockSpec(memory_space=pltpu.VMEM)
SMEM_SPEC = pl.BlockSpec(memory_space=pltpu.SMEM)
ANY_SPEC = pl.BlockSpec(memory_space=pl.ANY)
HBM_SPEC = pl.BlockSpec(memory_space=pltpu.HBM)
GROUP = 4
TILES = 3
UNROLL = 4
RP = 144
RS_ORDER = (3, 2, 1, 0)


def sds(shape, dtype):
    return jax.ShapeDtypeStruct(shape, dtype)


def params(limit=VMEM_LIMIT):
    return pltpu.CompilerParams(vmem_limit_bytes=limit)


def after(vals, deps):
    return lax.optimization_barrier((vals, deps))[0]


def cost(gflop, mbytes):
    return pl.CostEstimate(
        flops=int(gflop * 1e9), bytes_accessed=int(mbytes * 1e6), transcendentals=0
    )


def copy_body(v_ref, out_ref):
    out_ref[...] = v_ref[...]


def fence(token):
    return pl.pallas_call(
        copy_body,
        out_shape=sds(token.shape, token.dtype),
        in_specs=[VMEM_SPEC],
        out_specs=VMEM_SPEC,
        compiler_params=params(BIG_LIMIT),
        name="fence",
    )(token)


def xor_pairs(size, step):
    return [(i, i ^ step) for i in range(size)]


def z_pairs(pairs):
    return [(2 * a + x, 2 * b + x) for a, b in pairs for x in range(2)]


def pack_plain(blocks):
    lead = blocks.shape[:-3]
    grp = blocks.reshape(lead + (-1, GROUP, 96, 96))
    last = jnp.swapaxes(grp[..., 3, :, :].reshape(lead + (-1, 96, 3, 32)), -3, -2)
    return jnp.concatenate([grp[..., :3, :, :], last], axis=-1)


def unpack_plain(groups):
    last = jnp.swapaxes(groups[..., 96:], -3, -2)
    last = last.reshape(groups.shape[:-3] + (1, 96, 96))
    grp = jnp.concatenate([groups[..., :96], last], axis=-3)
    return grp.reshape(groups.shape[:-4] + (-1, 96, 96))


def pack_owned_body(m_ref, out_ref):
    for g in range(out_ref.shape[0]):
        last = m_ref[GROUP * g + 3].astype(BF)
        for k in range(TILES):
            out_ref[g, k] = jnp.concatenate(
                [m_ref[GROUP * g + k].astype(BF), last[:, 32 * k : 32 * k + 32]], axis=-1
            )


def pack_owned(blocks):
    n = blocks.shape[0] // GROUP
    return pl.pallas_call(
        pack_owned_body,
        out_shape=sds((n, TILES, 96, 128), BF),
        in_specs=[VMEM_SPEC],
        out_specs=VMEM_SPEC,
        compiler_params=params(),
        cost_estimate=cost(0.1, 2),
        name="pack_owned",
    )(blocks)


def weights_body(n_pieces, places, pos_ref, me_ref, *refs):
    pieces = refs[:n_pieces]
    outs = refs[n_pieces : n_pieces + 4]
    wqkv_ref, wo_ref, w1_ref, w2_ref, al, sems, out_sem = refs[n_pieces + 4 :]
    dp, y = me_ref[0], me_ref[1] // 2
    groups = al.shape[1]
    copies = []
    for ref, (jy, jd) in zip(pieces, places):
        n = ref.shape[-4]
        if jd is None:
            for s in range(2):
                dst = al.at[s, :, pl.ds(0, TILES)]
                copies.append(((s,), pltpu.make_async_copy(ref.at[s], dst, sems.at[s])))
        else:
            dst = al.at[y ^ jy, pl.ds((dp ^ jd) * n, n), pl.ds(0, TILES)]
            copies.append(((0, 1), pltpu.make_async_copy(ref, dst, sems.at[y ^ jy])))
    for _, copy in copies:
        copy.start()
    for s in range(2):
        whole = al.at[s, :, pl.ds(0, TILES)]
        pltpu.make_async_copy(whole, whole, sems.at[s]).wait()

        def fix(g, carry, s=s):
            rolled = [pltpu.roll(al[s, g, k], 32 + 32 * k, 1) for k in range(TILES)]
            lane = lax.broadcasted_iota(jnp.int32, rolled[0].shape, 1)
            al[s, g, 3] = jnp.where(lane < 32, rolled[0], jnp.where(lane < 64, rolled[1], rolled[2]))
            return carry

        lax.fori_loop(0, groups, fix, 0, unroll=16)

    def block(s, b):
        p = pos_ref[b]
        return al[s, p // GROUP, p % GROUP][:, :96]

    def strip_qkv(i, carry):
        rows = pl.ds(pl.multiple_of(i * 96, 96), 96)
        for part in range(3):
            wqkv_ref[rows, part * 384 : part * 384 + 384] = jnp.concatenate(
                [block(j // 2, i * 6 + part * 2 + j % 2) for j in range(4)], axis=-1
            )
        return carry

    def strip(i, carry, ref, first):
        rows = pl.ds(pl.multiple_of(i * 96, 96), 96)
        for s in range(2):
            for half in range(2):
                ref[s, rows, half * 384 : half * 384 + 384] = jnp.concatenate(
                    [block(s, first + i * 8 + half * 4 + j) for j in range(4)], axis=-1
                )
        return carry

    def send(k):
        copy = pltpu.make_async_copy((wqkv_ref, wo_ref, w1_ref, w2_ref)[k], outs[k], out_sem.at[k])
        copy.start()
        return copy

    lax.fori_loop(0, 8, functools.partial(strip, ref=w1_ref, first=64), 0, unroll=UNROLL)
    sent = [send(2)]
    lax.fori_loop(0, 8, functools.partial(strip, ref=w2_ref, first=128), 0, unroll=UNROLL)
    sent.append(send(3))
    lax.fori_loop(0, 8, strip_qkv, 0, unroll=UNROLL)
    sent.append(send(0))
    for i in range(4):
        for half in range(2):
            wo_ref[i * 96 : i * 96 + 96, half * 384 : half * 384 + 384] = jnp.concatenate(
                [block(i // 2, 48 + (i % 2) * 8 + half * 4 + j) for j in range(4)], axis=-1
            )
    sent.append(send(1))
    for copy in sent:
        copy.wait()


def build_weights(pos, me, pieces, places, slots):
    return pl.pallas_call(
        functools.partial(weights_body, len(pieces), places),
        out_shape=(
            sds((768, 1152), BF),
            sds((384, 768), BF),
            sds((2, 768, 768), BF),
            sds((2, 768, 768), BF),
        ),
        in_specs=[SMEM_SPEC, SMEM_SPEC] + [HBM_SPEC] * len(pieces),
        out_specs=(HBM_SPEC,) * 4,
        scratch_shapes=[
            pltpu.VMEM((768, 1152), BF),
            pltpu.VMEM((384, 768), BF),
            pltpu.VMEM((2, 768, 768), BF),
            pltpu.VMEM((2, 768, 768), BF),
            pltpu.VMEM((2, slots // GROUP, GROUP, 96, 128), BF),
            pltpu.SemaphoreType.DMA((2,)),
            pltpu.SemaphoreType.DMA((4,)),
        ],
        compiler_params=params(BIG_LIMIT),
        cost_estimate=cost(0.1, 30),
        name="build_weights",
    )(pos, me, *pieces)


def product(left, right, out, width=256):
    def step(i, carry):
        col = pl.multiple_of(i * width, width)
        out[pl.ds(col, width), :] = inner_rows(left[:, pl.ds(col, width)], right[...]).astype(BF)
        return carry

    lax.fori_loop(0, out.shape[0] // width, step, 0)


def down_grads_body(act_ref, d2_ref, out_ref):
    for s in range(2):
        product(act_ref.at[s], d2_ref, out_ref.at[s])


def up_grads_body(h_ref, dpre_ref, out_ref):
    for s in range(2):
        product(h_ref, dpre_ref.at[s], out_ref.at[s])


def down_grads(act, d_two):
    return pl.pallas_call(
        down_grads_body,
        out_shape=sds((2, 768, 768), BF),
        in_specs=[VMEM_SPEC] * 2,
        out_specs=VMEM_SPEC,
        compiler_params=params(),
        cost_estimate=cost(1.4, 8),
        name="down_grads",
    )(act, d_two)


def up_grads(h_in, d_pre):
    return pl.pallas_call(
        up_grads_body,
        out_shape=sds((2, 768, 768), BF),
        in_specs=[VMEM_SPEC] * 2,
        out_specs=VMEM_SPEC,
        compiler_params=params(),
        cost_estimate=cost(1.4, 8),
        name="up_grads",
    )(h_in, d_pre)


def tile_of(vals, j):
    if j < 3:
        return vals[:, 96 * j : 96 * j + 128]
    return pltpu.roll(vals[:, 256:384], 96, 1)


def pack_body(places, pos_ref, me_ref, *refs):
    token_ref = refs[5]
    outs = refs[6 : 6 + len(places)]
    g2, g1, go, gq, al, sem, sems = refs[6 + len(places) :]
    loads = [pltpu.make_async_copy(src, dst, sems.at[k]) for k, (src, dst) in enumerate(zip(refs, (g2, g1, go, gq)))]
    for load in loads:
        load.start()
    groups = al.shape[1]
    token_ref[...] = jnp.zeros_like(token_ref)

    def put(s, b, blk):
        p = pos_ref[b]
        al[s, p // GROUP, p % GROUP] = blk

    def strip(i, carry, ref, first):
        rows = pl.ds(pl.multiple_of(i * 96, 96), 96)
        for s in range(2):
            for half in range(2):
                vals = ref[s, rows, half * 384 : half * 384 + 384]
                for j in range(4):
                    put(s, first + i * 8 + half * 4 + j, tile_of(vals, j))
        return carry

    def strip_qkv(i, carry):
        rows = pl.ds(pl.multiple_of(i * 96, 96), 96)
        for part in range(3):
            vals = gq[rows, part * 384 : part * 384 + 384]
            for j in range(4):
                put(j // 2, i * 6 + part * 2 + j % 2, tile_of(vals, j))
        return carry

    loads[0].wait()
    lax.fori_loop(0, 8, functools.partial(strip, ref=g2, first=128), 0, unroll=UNROLL)
    loads[1].wait()
    lax.fori_loop(0, 8, functools.partial(strip, ref=g1, first=64), 0, unroll=UNROLL)
    loads[2].wait()
    for i in range(4):
        for half in range(2):
            vals = go[i * 96 : i * 96 + 96, half * 384 : half * 384 + 384]
            for j in range(4):
                put(i // 2, 48 + (i % 2) * 8 + half * 4 + j, tile_of(vals, j))
    loads[3].wait()
    lax.fori_loop(0, 8, strip_qkv, 0, unroll=UNROLL)

    dp, y = me_ref[0], me_ref[1] // 2
    copies = []
    for s in range(2):

        def fix(g, carry, s=s):
            last = al[s, g, 3]
            low = lax.broadcasted_iota(jnp.int32, last.shape, 1) < 96
            for k in range(TILES):
                al[s, g, k] = jnp.where(low, al[s, g, k], pltpu.roll(last, 96 - 32 * k, 1))
            return carry

        lax.fori_loop(0, groups, fix, 0, unroll=16)
        for ref, (jy, jd) in zip(outs, places):
            if jd is None:
                copies.append((None, pltpu.make_async_copy(al.at[s, :, pl.ds(0, TILES)], ref.at[s], sem)))
            else:
                n = ref.shape[0]
                src = al.at[s, pl.ds((dp ^ jd) * n, n), pl.ds(0, TILES)]
                copies.append(((y ^ jy) == s, pltpu.make_async_copy(src, ref, sem)))
        for mine, copy in copies[s * len(outs) :]:
            if mine is None:
                copy.start()
            else:
                pl.when(mine)(copy.start)
    for mine, copy in copies:
        if mine is None:
            copy.wait()
        else:
            pl.when(mine)(copy.wait)


def pack_grads(pos, me, grads, places, out_shapes, slots):
    return pl.pallas_call(
        functools.partial(pack_body, places),
        out_shape=(sds((8, 128), F32), *(sds(s, BF) for s in out_shapes)),
        in_specs=[SMEM_SPEC, SMEM_SPEC] + [HBM_SPEC] * 4 + [ANY_SPEC],
        out_specs=(VMEM_SPEC,) + (HBM_SPEC,) * len(places),
        scratch_shapes=[
            pltpu.VMEM((2, 768, 768), BF),
            pltpu.VMEM((2, 768, 768), BF),
            pltpu.VMEM((384, 768), BF),
            pltpu.VMEM((768, 1152), BF),
            pltpu.VMEM((2, slots // GROUP, GROUP, 96, 128), BF),
            pltpu.SemaphoreType.DMA,
            pltpu.SemaphoreType.DMA((4,)),
        ],
        compiler_params=params(BIG_LIMIT),
        cost_estimate=cost(0.1, 30),
        name="pack_grads",
    )(pos, me, *grads)


def project_body(flags_ref, xa, xb, xc, xd, sh_ref, w_ref, b_ref, later_ref, proj_ref, x0_ref, xin_ref, bias):
    @pl.when(pl.program_id(0) == 0)
    def _():
        n = xa.shape[0]
        gap = jnp.zeros((RP - n, x0_ref.shape[1]), F32)
        for k, ref in enumerate((xa, xb, xc, xd)):
            x0_ref[k * RP : k * RP + n, :] = ref[...].astype(F32)
            x0_ref[k * RP + n : k * RP + RP, :] = gap

            @pl.when((flags_ref[0] == k) & (flags_ref[1] == 1))
            def _(k=k):
                x0_ref[k * RP : k * RP + MEM, :] = sh_ref[6 : 6 + MEM, :]

        xin_ref[...] = x0_ref[...].astype(BF)
        for part, col in ((0, 0), (2, 192)):
            bias[part] = jnp.concatenate([b_ref[s : s + 1, col : col + 192] for s in range(2)], axis=1)
        bias[1] = jnp.zeros((1, 384), F32)

    proj_ref[...] = (dot(xin_ref[...], w_ref[...]) + bias[pl.program_id(0)]).astype(BF)


def project(flags, quarters, shared, w_qkv, biases, later):
    rows = 4 * RP

    def whole(shape):
        return pl.BlockSpec(shape, lambda i: (0, 0))

    return pl.pallas_call(
        project_body,
        grid=(3,),
        out_shape=(sds((rows, 1152), BF), sds((rows, 768), F32), sds((rows, 768), BF)),
        in_specs=[
            SMEM_SPEC,
            *[whole(q.shape) for q in quarters],
            whole(shared.shape),
            pl.BlockSpec((768, 384), lambda i: (0, i)),
            whole(biases.shape),
            ANY_SPEC,
        ],
        out_specs=(
            pl.BlockSpec((rows, 384), lambda i: (0, i)),
            whole((rows, 768)),
            whole((rows, 768)),
        ),
        scratch_shapes=[pltpu.VMEM((3, 1, 384), F32)],
        compiler_params=params(),
        cost_estimate=cost(1.0, 5),
        name="project",
    )(flags, *quarters, shared, w_qkv, biases, later)


def head_masks(shape):
    lane = lax.broadcasted_iota(jnp.int32, shape, 1)
    return lane < HEAD_DIM, lane >= HEAD_DIM


def attend_body(cq_ref, ck_ref, q_ref, k_ref, v_ref, wo_ref, ctx_ref, p_ref, part_ref, vis):
    h = pl.program_id(0)

    @pl.when(h == 0)
    def _():
        cq, ck = cq_ref[...], ck_ref[...]
        seen = ((cq == -1) | (ck == -1) | (cq == ck)) & (ck != -2)
        vis[...] = jnp.where(seen, 1.0, 0.0)

    q, k, v = q_ref[...], k_ref[...], v_ref[...]
    masks = head_masks(q.shape)
    raws = [dot_back(jnp.where(masks[n], q, jnp.zeros_like(q)), k) for n in range(2)]
    outs = []
    for n in range(2):
        scores = jnp.where(vis[...] > 0.5, raws[n] * HEAD_DIM ** (-0.5), -1000000000.0)
        e = jnp.exp(scores - jnp.max(scores, axis=-1, keepdims=True))
        p = (e * (1.0 / jnp.sum(e, axis=-1, keepdims=True))).astype(BF)
        p_ref[n] = p
        outs.append(dot(p, v))
    ctx_ref[:, pl.ds(pl.multiple_of(h * 128, 128), 128)] = jnp.where(masks[0], outs[0], outs[1]).astype(BF)

    @pl.when(h == pl.num_programs(0) - 1)
    def _():
        part_ref[...] = dot(ctx_ref[...], wo_ref[...]).astype(BF)


def head_col(rows, off):
    return pl.BlockSpec((rows, 128), lambda h: (0, h + off))


def all_steps(shape):
    return pl.BlockSpec(shape, lambda h: (0,) * len(shape))


def attend(code_q, code_k, proj, w_out):
    rows = proj.shape[0]
    pairs = HEADS // 4
    return pl.pallas_call(
        attend_body,
        grid=(pairs,),
        out_shape=(sds((rows, 384), BF), sds((2 * pairs, rows, rows), BF), sds((rows, 768), BF)),
        in_specs=[
            all_steps((rows, 1)),
            all_steps((1, rows)),
            head_col(rows, 0),
            head_col(rows, pairs),
            head_col(rows, 2 * pairs),
            all_steps((384, 768)),
        ],
        out_specs=(
            all_steps((rows, 384)),
            pl.BlockSpec((2, rows, rows), lambda h: (h, 0, 0)),
            all_steps((rows, 768)),
        ),
        scratch_shapes=[pltpu.VMEM((rows, rows), F32)],
        compiler_params=params(),
        cost_estimate=cost(2.5, 8),
        name="attend",
    )(code_q, code_k, proj, proj, proj, w_out)


def both_cores(mine_ref, other_ref):
    half = mine_ref.shape[0] // 2
    other = jnp.concatenate([other_ref[half:, :], other_ref[:half, :]], axis=0)
    return mine_ref[...].astype(F32) + other.astype(F32)


def col_sum(v):
    return jnp.sum(v, axis=0, keepdims=True)


def feed_body(mine_ref, other_ref, x0_ref, sh_ref, b_ref, w1_hbm, w2_hbm, h_ref, n_ref, r_ref, act_ref, slope_ref, part_ref, w1, w2, acc, sems):
    copies = []
    for s in range(2):
        copies.append(pltpu.make_async_copy(w1_hbm.at[s], w1.at[s], sems.at[s]))
        copies.append(pltpu.make_async_copy(w2_hbm.at[s], w2.at[s], sems.at[2 + s]))
    for copy in copies:
        copy.start()
    total = both_cores(mine_ref, other_ref) + sh_ref[0:1, :] + x0_ref[...]
    h_one, normed, inverse = norm_parts(total, sh_ref[1:2, :], sh_ref[2:3, :])
    h_ref[...] = h_one.astype(BF)
    n_ref[...] = normed
    r_ref[...] = inverse
    for s in range(2):
        copies[2 * s].wait()
        pre = dot(h_ref[...], w1[s]) + b_ref[s : s + 1, 384:]
        cdf = 0.5 * (1.0 + lax.erf(pre * 0.7071067811865476))
        act_ref[s] = (pre * cdf).astype(BF)
        slope_ref[s] = (cdf + pre * jnp.exp(-0.5 * pre * pre) * 0.3989422804014327).astype(BF)
        copies[2 * s + 1].wait()
        part = dot(act_ref[s], w2[s])
        acc[...] = part if s == 0 else acc[...] + part
    part_ref[...] = acc[...].astype(BF)


def feed(mine, other, x_zero, shared, biases, w1, w2):
    rows = x_zero.shape[0]
    one, two = sds((rows, 768), BF), sds((2, rows, 768), BF)
    return pl.pallas_call(
        feed_body,
        out_shape=(one, sds((rows, 768), F32), sds((rows, 1), F32), two, two, one),
        in_specs=[VMEM_SPEC] * 5 + [ANY_SPEC] * 2,
        out_specs=(VMEM_SPEC,) * 6,
        scratch_shapes=[
            pltpu.VMEM((2, 768, 768), BF),
            pltpu.VMEM((2, 768, 768), BF),
            pltpu.VMEM((rows, 768), F32),
            pltpu.SemaphoreType.DMA((4,)),
        ],
        compiler_params=params(),
        cost_estimate=cost(2.8, 16),
        name="feed",
    )(mine, other, x_zero, shared, biases, w1, w2)


def feed_back_body(mine_ref, other_ref, n_ref, slope_ref, ca, cb, cc, cd, sh_ref, w1_hbm, w2_hbm, out_ref, d2_ref, d2b_ref, dpre_ref, part_ref, sums_ref, bsum_ref, w1, w2, g, acc, sems):
    copies = []
    for s in range(2):
        copies.append(pltpu.make_async_copy(w2_hbm.at[s], w2.at[s], sems.at[2 + s]))
        copies.append(pltpu.make_async_copy(w1_hbm.at[s], w1.at[s], sems.at[s]))
    for copy in copies:
        copy.start()
    n = ca.shape[0]
    for k, ref in enumerate((ca, cb, cc, cd)):
        g[k * RP : k * RP + n, :] = ref[...].astype(F32)
        g[k * RP + n : k * RP + RP, :] = jnp.zeros((RP - n, 768), F32)
    own = g.shape[0] // 2

    def row(i):
        return sh_ref[i : i + 1, :]

    h_one = n_ref[...] * row(1) + row(2)
    total = both_cores(mine_ref, other_ref) + row(3) + h_one
    rows_out, normed, inverse = norm_parts(total, row(4), row(5))
    out_ref[...] = rows_out[:own].astype(BF)
    grad = g[...]
    d_two = norm_back(grad, normed, inverse, row(4))
    d2_ref[...] = d_two
    d2b_ref[...] = d_two.astype(BF)
    sums_ref[0:3, :] = jnp.concatenate(
        [col_sum(d_two[:own]), col_sum(grad[:own] * normed[:own]), col_sum(grad[:own])], axis=0
    )
    sums_ref[3:8, :] = jnp.zeros((5, 768), F32)
    for s in range(2):
        copies[2 * s].wait()
        d_pre = dot_back(d2b_ref[...], w2[s]) * slope_ref[s].astype(F32)
        bsum_ref[s : s + 1, :] = col_sum(d_pre)
        dpre_ref[s] = d_pre.astype(BF)
        copies[2 * s + 1].wait()
        part = dot_back(dpre_ref[s], w1[s])
        acc[...] = part if s == 0 else acc[...] + part
    part_ref[...] = acc[...].astype(BF)


def feed_back(mine, other, normed, slope, cots, shared, w1, w2):
    rows = normed.shape[0]
    one = sds((rows, 768), BF)
    return pl.pallas_call(
        feed_back_body,
        out_shape=(
            sds((rows // 2, 768), BF),
            sds((rows, 768), F32),
            one,
            sds((2, rows, 768), BF),
            one,
            sds((8, 768), F32),
            sds((2, 768), F32),
        ),
        in_specs=[VMEM_SPEC] * 9 + [ANY_SPEC] * 2,
        out_specs=(VMEM_SPEC,) * 7,
        scratch_shapes=[
            pltpu.VMEM((2, 768, 768), BF),
            pltpu.VMEM((2, 768, 768), BF),
            pltpu.VMEM((rows, 768), F32),
            pltpu.VMEM((rows, 768), F32),
            pltpu.SemaphoreType.DMA((4,)),
        ],
        compiler_params=params(),
        cost_estimate=cost(2.8, 16),
        name="feed_back",
    )(mine, other, normed, slope, *cots, shared, w1, w2)


def attend_back_body(mine_ref, other_ref, d2_ref, n_ref, r_ref, sh_ref, wo_ref, wqkv_ref, x_ref, ctx_ref, later_ref, p_ref, q_ref, k_ref, v_ref, d1_ref, gq_ref, go_ref, part_ref, send_ref, sums_ref, bsum_ref, d1b_ref, dproj_ref, dctx):
    h = pl.program_id(0)
    pairs = pl.num_programs(0)
    own = d1_ref.shape[0]

    @pl.when(h == 0)
    def _():
        dh = both_cores(mine_ref, other_ref) + d2_ref[...]
        normed = n_ref[...]
        d_one = norm_back(dh, normed, r_ref[...], sh_ref[1:2, :])
        d1_ref[...] = d_one[:own]
        d1b_ref[...] = d_one.astype(BF)
        sums_ref[0:3, :] = jnp.concatenate(
            [col_sum(d_one[:own]), col_sum(dh[:own] * normed[:own]), col_sum(dh[:own])], axis=0
        )
        sums_ref[3:8, :] = jnp.zeros((5, 768), F32)
        back = dot_back(d1b_ref[...], wo_ref[...]).astype(BF)
        for m in range(3):
            dctx[m] = back[:, m * 128 : m * 128 + 128]

    q, k, v, dc = q_ref[...], k_ref[...], v_ref[...], dctx[h]
    masks = head_masks(q.shape)
    dqs, dks, dvs = [], [], []
    dps = [dot_back(jnp.where(masks[m], dc, jnp.zeros_like(dc)), v) for m in range(2)]
    for m in range(2):
        dvs.append(inner_rows(p_ref[m], dc))
        pf = p_ref[m].astype(F32)
        row = jnp.sum(dps[m] * pf, axis=-1, keepdims=True)
        ds = (pf * (dps[m] - row) * HEAD_DIM ** (-0.5)).astype(BF)
        dqs.append(dot(ds, k))
        dks.append(inner_rows(ds, q))
    dq, dk, dv = (jnp.where(masks[0], d[0], d[1]) for d in (dqs, dks, dvs))
    for part, d in enumerate((dq, dk, dv)):
        dproj_ref[:, pl.ds(pl.multiple_of(part * 384 + h * 128, 128), 128)] = d.astype(BF)
    bsum_ref[...] = jnp.concatenate([col_sum(dq), col_sum(dv), jnp.zeros((6, 128), F32)], axis=0)

    @pl.when(h == pairs - 1)
    def _():
        share = dot_back(dproj_ref[...], wqkv_ref[...]).astype(BF)
        part_ref[...] = share[:own]
        send_ref[...] = share[own:]
        product(ctx_ref, d1b_ref, go_ref, 128)
        product(x_ref, dproj_ref, gq_ref)


def attend_back(mine, other, d_two, normed, inverse, shared, w_out, w_qkv, x_in, context, later, probs, proj):
    rows = proj.shape[0]
    pairs = HEADS // 4
    return pl.pallas_call(
        attend_back_body,
        grid=(pairs,),
        out_shape=(
            sds((rows // 2, 768), F32),
            sds((768, 1152), BF),
            sds((384, 768), BF),
            sds((rows // 2, 768), BF),
            sds((rows // 2, 768), BF),
            sds((8, 768), F32),
            sds((8, 384), F32),
        ),
        in_specs=[
            all_steps((rows, 768)),
            all_steps((rows, 768)),
            all_steps((rows, 768)),
            all_steps((rows, 768)),
            all_steps((rows, 1)),
            all_steps(shared.shape),
            all_steps((384, 768)),
            all_steps((768, 1152)),
            all_steps((rows, 768)),
            all_steps((rows, 384)),
            ANY_SPEC,
            pl.BlockSpec((2, rows, rows), lambda h: (h, 0, 0)),
            head_col(rows, 0),
            head_col(rows, pairs),
            head_col(rows, 2 * pairs),
        ],
        out_specs=(
            all_steps((rows // 2, 768)),
            all_steps((768, 1152)),
            all_steps((384, 768)),
            all_steps((rows // 2, 768)),
            all_steps((rows // 2, 768)),
            all_steps((8, 768)),
            pl.BlockSpec((8, 128), lambda h: (0, h)),
        ),
        scratch_shapes=[
            pltpu.VMEM((rows, 768), BF),
            pltpu.VMEM((rows, 1152), BF),
            pltpu.VMEM((3, rows, 128), BF),
        ],
        compiler_params=params(),
        cost_estimate=pl.CostEstimate(
            flops=2 * rows * rows * 64 * 4 * HEADS, bytes_accessed=10 * 1024 * 1024, transcendentals=0
        ),
        name="attend_back",
    )(mine, other, d_two, normed, inverse, shared, w_out, w_qkv, x_in, context, later, probs, proj, proj, proj)


def finish_body(flags_ref, part_ref, other_ref, d1_ref, gin_ref, mem_ref):
    d_zero = part_ref[...].astype(F32) + other_ref[...].astype(F32) + d1_ref[...]
    gin_ref[...] = d_zero.astype(BF)
    mem_ref[...] = jnp.zeros_like(mem_ref)
    for k in range(2):

        @pl.when((flags_ref[0] == k) & (flags_ref[1] == 1))
        def _(k=k):
            row = lax.broadcasted_iota(jnp.int32, (16, d_zero.shape[1]), 0)
            top = d_zero[k * RP : k * RP + 16, :]
            mem_ref[...] = jnp.where(row < MEM, top, 0.0)
            gin_ref[k * RP : k * RP + 16, :] = jnp.where(row < MEM, 0.0, top).astype(BF)


def finish(flags, part, other, d_one):
    return pl.pallas_call(
        finish_body,
        out_shape=(sds(d_one.shape, BF), sds((16, 768), F32)),
        in_specs=[SMEM_SPEC] + [VMEM_SPEC] * 3,
        out_specs=(VMEM_SPEC,) * 2,
        compiler_params=params(),
        cost_estimate=cost(0.1, 4),
        name="finish",
    )(flags, part, other, d_one)


def soap_body(n_terms, *refs):
    terms = refs[:n_terms]
    w_ref, m_ref, v_ref, sl_ref, sr_ref, l_ref, r_ref = refs[n_terms : n_terms + 7]
    nw_ref, nc_ref, nm_ref, nv_ref, nl_ref, nr_ref = refs[n_terms + 7 :]
    blocks = w_ref.shape[0]
    if n_terms == 1:
        grads = [terms[0][b] for b in range(blocks)]
    else:
        grads = []
        for g in range(blocks // GROUP):
            tiles = [sum(ref[g, k].astype(F32) for ref in terms) for k in range(TILES)]
            grads += [tile[:, :96] for tile in tiles]
            grads.append(jnp.concatenate([tile[:, 96:] for tile in tiles], axis=-1))
    every = range(blocks)
    gb = [g.astype(BF) for g in grads]
    lb, rb = [l_ref[b].astype(BF) for b in every], [r_ref[b].astype(BF) for b in every]
    half = [inner_rows(lb[b], gb[b]).astype(BF) for b in every]
    for b in every:
        nl_ref[b] = beta_two * sl_ref[b] + (1.0 - beta_two) * dot_back(gb[b], gb[b])
    turned = [dot(half[b], rb[b]) for b in every]
    for b in every:
        nr_ref[b] = beta_two * sr_ref[b] + (1.0 - beta_two) * inner_rows(gb[b], gb[b])
    steps = []
    for b in every:
        new_first = beta_one * m_ref[b] + (1.0 - beta_one) * turned[b]
        new_second = beta_two * v_ref[b] + (1.0 - beta_two) * turned[b] * turned[b]
        nm_ref[b] = new_first
        nv_ref[b] = new_second
        direction = (
            new_first
            / (1.0 - beta_one**STEP)
            / (jnp.sqrt(new_second / (1.0 - beta_two**STEP)) + adam_eps)
        )
        steps.append(direction.astype(BF))
    half = [dot(lb[b], steps[b]).astype(BF) for b in every]
    for b in every:
        new_weight = w_ref[b] - rate_matrix * dot_back(half[b], rb[b])
        nw_ref[b] = new_weight
        nc_ref[b] = new_weight.astype(BF)


def soap(terms, master, first, second, left, right, left_rot, right_rot):
    count = master.shape[0]
    many = next(n for n in (3, 2, 1) if terms[0].shape[0] % n == 0)
    step = many * GROUP if len(terms) > 1 else 1
    spec = pl.BlockSpec((step, 96, 96), lambda i: (i, 0, 0))
    packed = pl.BlockSpec((many, TILES, 96, 128), lambda i: (i, 0, 0, 0))
    full = sds(master.shape, F32)
    return pl.pallas_call(
        functools.partial(soap_body, len(terms)),
        grid=(count // step,),
        out_shape=(full, sds(master.shape, BF), full, full, full, full),
        in_specs=[packed if len(terms) > 1 else spec] * len(terms) + [spec] * 7,
        out_specs=(spec,) * 6,
        compiler_params=params(BIG_LIMIT),
        cost_estimate=cost(0.3, 24),
        name="soap",
    )(*terms, master, first, second, left, right, left_rot, right_rot)


def norm_parts(values, gain_vec, shift_vec):
    centred = values - jnp.mean(values, axis=-1, keepdims=True)
    inverse = lax.rsqrt(jnp.mean(centred * centred, axis=-1, keepdims=True) + norm_eps)
    normed = centred * inverse
    return (normed * gain_vec + shift_vec, normed, inverse)


def norm_back(upstream, normed, inverse, gain_vec):
    scaled = upstream * gain_vec
    result = inverse * (
        scaled
        - jnp.mean(scaled, axis=-1, keepdims=True)
        - normed * jnp.mean(scaled * normed, axis=-1, keepdims=True)
    )
    return result


def dot(left, right):
    return jnp.dot(left, right, preferred_element_type=F32)


def dot_back(left, right):
    return lax.dot_general(left, right, (((1,), (1,)), ((), ())), preferred_element_type=F32)


def inner_rows(left, right):
    return lax.dot_general(left, right, (((0,), (0,)), ((), ())), preferred_element_type=F32)


def adam_update(values, grad_vec, first_mom, second_mom, step_rate):
    new_first = beta_one * first_mom + (1.0 - beta_one) * grad_vec
    new_second = beta_two * second_mom + (1.0 - beta_two) * grad_vec * grad_vec
    direction = (
        new_first
        / (1.0 - beta_one**STEP)
        / (jnp.sqrt(new_second / (1.0 - beta_two**STEP)) + adam_eps)
    )
    return (values - step_rate * direction, new_first, new_second)


def per_device(
    n_dp,
    n_tensor,
    layer_in,
    cotangent,
    doc_ids,
    reset_flags,
    block_slot,
    master,
    first_moment,
    second_moment,
    left_stats,
    right_stats,
    left_basis,
    right_basis,
    split_params,
    split_first,
    split_second,
    shared,
    shared_first,
    shared_second,
):
    meshed = n_dp == 8 and master.shape[1] % GROUP == 0
    dp = lax.axis_index("dp")
    t = lax.axis_index("tensor")
    y, c = t // 2, t % 2
    me = jnp.stack([dp, t])
    barrier = lax.optimization_barrier
    slots = block_slot.shape[0]
    quarter = layer_in.shape[1]

    def swap(axis, step):
        size = n_dp if axis == "dp" else n_tensor
        return lambda v: lax.ppermute(v, axis, xor_pairs(size, step))

    core, yswap, xswap = swap("tensor", 1), swap("tensor", 2), swap("dp", 1)

    def along_z(*pairs):
        return lambda v: lax.ppermute(v, "dp", z_pairs(pairs))

    outer, middle = along_z((0, 1), (1, 0), (2, 3), (3, 2)), along_z((1, 2), (2, 1))
    inward, outward = along_z((0, 1), (3, 2)), along_z((1, 0), (2, 3))

    docs = lax.dynamic_index_in_dim(doc_ids, y, 0, keepdims=False)
    edge = jnp.full((MEM,), -1, jnp.int32)
    codes = jnp.concatenate([edge, docs, edge]).reshape(4, quarter)
    codes = jnp.pad(codes, ((0, 0), (0, RP - quarter)), constant_values=-2)
    codes = jnp.concatenate(
        [lax.dynamic_index_in_dim(codes, t ^ j, 0, keepdims=False) for j in (0, 2, 1, 3)]
    )
    code_q, code_k = codes[:, None], codes[None, :]
    reset_now = lax.dynamic_index_in_dim(reset_flags, y, 0, keepdims=False) == 1
    flags = jnp.stack([y + 2 * c, reset_now.astype(jnp.int32)])

    split_other = yswap(split_params)
    biases = jnp.concatenate(
        [jnp.where(y == 0, split_params, split_other), jnp.where(y == 0, split_other, split_params)], axis=0
    )
    def inputs_of(arr):
        mine = lax.dynamic_index_in_dim(arr, y, 0, keepdims=False)
        other = lax.dynamic_index_in_dim(arr, 1 - y, 0, keepdims=False)
        return mine, other

    (in_mine, in_send), (cot_mine, cot_send) = inputs_of(layer_in), inputs_of(cotangent)

    if meshed:
        own = pack_owned(master[0])
        near, mid = outer(own), middle(own)
        x0, y0 = xswap(own), yswap(own)
        tok = biases[:, :128]
        near, mid, x0, y0, tok = barrier((near, mid, x0, y0, tok))
        far_mid, far_end = middle(near), outward(mid)
        x1, diag0 = xswap(near), yswap(x0)
        small = (code_q, code_k, flags, biases, me, in_send, cot_send, fence(tok))
        x1, diag0, far_mid, far_end, small = barrier((x1, diag0, far_mid, far_end, small))
        code_q, code_k, flags, biases, me, in_send, cot_send, tok = small
        far = far_mid + far_end
        last_end = outward(far_mid)
        x2, y2 = xswap(far), yswap(far)
        x2, y2, last_end, tok = barrier((x2, y2, last_end, fence(tok)))
        last = mid + last_end
        x3, y3, y1 = xswap(last), yswap(last), outer(y0)
        x3, y3, y1, in_send, tok = barrier((x3, y3, y1, in_send, fence(tok)))
        diag3, diag2, diag1 = xswap(y3), yswap(x2), outer(diag0)
        in_other = yswap(in_send)
        diag3, diag2, diag1, cot_send, tok = barrier((diag3, diag2, diag1, cot_send, fence(tok)))
        me = after(me, fence(tok))
        pieces, places = [], []
        for jz, vals in enumerate(
            ((own, x0, y0, diag0), (near, x1, y1, diag1), (far, x2, y2, diag2), (last, x3, y3, diag3))
        ):
            pieces.extend(vals)
            places.extend([(0, 2 * jz), (0, 2 * jz + 1), (1, 2 * jz), (1, 2 * jz + 1)])
    else:
        every = lax.all_gather(master.astype(BF), "dp", axis=1, tiled=True)
        every_other = yswap(every)
        every = jnp.concatenate(
            [jnp.where(y == 0, every, every_other), jnp.where(y == 0, every_other, every)], axis=0
        )
        pieces, places = [pack_plain(every)], [(0, None)]
        in_other = yswap(in_send)
    w_qkv, w_out, w_up, w_down = build_weights(block_slot, me, pieces, tuple(places), slots)

    cot_other = yswap(cot_send)
    quarters = (in_mine, in_other, core(in_mine), core(in_other))
    proj, x_zero, x_in = project(flags, quarters, shared, w_qkv, biases, cot_other)
    cots = (cot_mine, cot_other, core(cot_mine), core(cot_other))
    context, probs, attn = attend(code_q, code_k, proj, w_out)
    h_in, normed, inverse, act, slope, ffn = feed(attn, core(attn), x_zero, shared, biases, w_up, w_down)
    rows_out, d_two, d_two_b, d_pre, d_hidden, sums_two, up_sums = feed_back(
        ffn, core(ffn), normed, slope, cots, shared, w_up, w_down
    )
    d_hidden_other = core(d_hidden)
    g_down, g_up = down_grads(act, d_two_b), up_grads(h_in, d_pre)
    d_one, g_qkv, g_out, d_in, d_in_send, sums_one, head_sums = attend_back(
        d_hidden, d_hidden_other, d_two, normed, inverse, shared, w_out, w_qkv, x_in, context, g_down, probs, proj
    )
    def to_owner(arr):
        mine, other = arr[:quarter], yswap(arr[RP : RP + quarter])
        both = jnp.stack([mine, other])
        return jnp.where(y == 0, both, both[::-1])

    layer_out = to_owner(rows_out)
    me = after(me, layer_out)
    d_in_other = core(d_in_send)
    grad_rows, memory_grad = finish(flags, d_in, d_in_other, d_one)
    grads = (g_down, g_up, g_out, g_qkv, memory_grad)
    vec = jnp.concatenate([sums_one[:3], sums_two[:3], memory_grad[:MEM]], axis=0)
    halves = head_sums[:2].reshape(2, 2, 192).swapaxes(0, 1).reshape(2, 384)
    splits = jnp.concatenate([halves, up_sums], axis=1).reshape(3, 768)

    def add_core(vec):
        return jnp.concatenate([vec + core(vec), splits], axis=0)

    if meshed:
        per = master.shape[1] // GROUP
        half = per // 2
        places, shapes = [], []
        for jz in RS_ORDER:
            for jy in range(2):
                for jx in range(2):
                    places.append((jy, 2 * jz + jx))
                    shapes.append((per, TILES, 96, 128))
        token, *packed = pack_grads(block_slot, me, grads, tuple(places), shapes, slots)
        own, x_unit, y_unit, diag = {}, {}, {}, {}
        for n, jz in enumerate(RS_ORDER):
            own[jz], x_unit[jz], y_unit[jz], diag[jz] = packed[4 * n : 4 * n + 4]

        def plus(*vals):
            return sum(v.astype(F32) for v in vals).astype(BF)

        vec = after(add_core(vec), token)
        d3, d2, n1 = xswap(diag[3]), yswap(diag[2]), outer(diag[1])
        vec = vec + yswap(vec)
        d3, d2, n1, vec, tok = barrier((d3, d2, n1, vec, fence(token)))
        x3, y3, m1 = xswap(x_unit[3]), yswap(plus(y_unit[3], d3)), outer(y_unit[1])
        vec = vec + swap("dp", 1)(vec)
        x3, y3, m1, vec, tok = barrier((x3, y3, m1, vec, fence(tok)))
        x2, y2 = xswap(plus(x_unit[2], d2)), yswap(y_unit[2])
        part3 = plus(own[3], x3, y3)
        e3 = inward(part3)
        vec = vec + swap("dp", 2)(vec)
        x2, y2, e3, vec, tok = barrier((x2, y2, e3, vec, fence(tok)))
        x1, d0 = xswap(x_unit[1]), yswap(plus(diag[0], n1))
        part2 = plus(own[2], x2, y2, e3)
        fm, fe = middle(part2), inward(part2)
        vec = vec + swap("dp", 4)(vec)
        x1, d0, fm, fe, vec, tok = barrier((x1, d0, fm, fe, vec, fence(tok)))
        x0, y0 = xswap(plus(x_unit[0], d0)), yswap(plus(y_unit[0], m1))
        near, mid = outer(plus(own[1], x1, fm)), middle(plus(part3, fe))
        x0, y0, near, mid, grad_rows, tok = barrier((x0, y0, near, mid, grad_rows, fence(tok)))
        terms = (own[0], x0, y0, near, mid)
    else:
        packed = pack_grads(
            block_slot, me, grads, ((0, None),), [(2, slots // GROUP, TILES, 96, 128)], slots
        )[1]
        blocks = unpack_plain(packed)
        blocks = lax.psum_scatter(blocks, "dp", scatter_dimension=1, tiled=True)
        mine = lax.dynamic_index_in_dim(blocks, y, 0, keepdims=False)
        other = yswap(lax.dynamic_index_in_dim(blocks, 1 - y, 0, keepdims=False))
        terms = (mine.astype(F32) + other.astype(F32),)

        vec = add_core(vec)
        vec = vec + yswap(vec)
        step = 1
        while step < n_dp:
            vec = vec + swap("dp", step)(vec)
            step *= 2

    grad_in = to_owner(grad_rows)
    total_shared = vec[:16]
    grad_split = lax.dynamic_index_in_dim(vec[16:].reshape(2, -1), y, 0, keepdims=True)

    new_master, new_copy, new_first, new_second, new_left, new_right = soap(
        terms,
        master[0],
        first_moment[0],
        second_moment[0],
        left_stats[0],
        right_stats[0],
        left_basis[0],
        right_basis[0],
    )
    new_split, new_split_first, new_split_second = adam_update(
        split_params, grad_split, split_first, split_second, rate_vector
    )
    new_shared, new_shared_first, new_shared_second = adam_update(
        shared, total_shared, shared_first, shared_second, rate_shared
    )
    return (
        layer_out,
        grad_in,
        new_master[None],
        new_copy[None],
        new_first[None],
        new_second[None],
        new_left[None],
        new_right[None],
        new_split,
        new_split_first,
        new_split_second,
        new_shared,
        new_shared_first,
        new_shared_second,
    )


def solution(mesh):
    rows = P("dp", "tensor", None)
    state = P("tensor", "dp", None, None)
    split = P("tensor", None)
    return jax.shard_map(
        functools.partial(per_device, mesh.shape["dp"], mesh.shape["tensor"]),
        mesh=mesh,
        in_specs=(rows, rows, P("dp", None), P("dp"), P()) + (state,) * 7 + (split,) * 3 + (P(),) * 3,
        out_specs=(rows, rows) + (state,) * 6 + (split,) * 3 + (P(),) * 3,
        check_vma=False,
    )
```

```python
import functools

import jax
import jax.numpy as jnp
from jax import lax
from jax.experimental import pallas as pl
from jax.experimental.pallas import tpu as pltpu
from jax.sharding import PartitionSpec as P

HEADS = 12
HEAD_DIM = 64
FF = 3072
SEG_TOK = 512
MEM = 10
STEP = 10

beta_one = 0.9
beta_two = 0.95
adam_eps = 1e-08
norm_eps = 1e-12
rate_matrix = 0.05
rate_vector = 0.1
rate_shared = 0.75

BF = jnp.bfloat16
F32 = jnp.float32
VMEM_LIMIT = 24 * 1024 * 1024
BIG_LIMIT = 61 * 1024 * 1024
VMEM_SPEC = pl.BlockSpec(memory_space=pltpu.VMEM)
SMEM_SPEC = pl.BlockSpec(memory_space=pltpu.SMEM)
ANY_SPEC = pl.BlockSpec(memory_space=pl.ANY)
HBM_SPEC = pl.BlockSpec(memory_space=pltpu.HBM)
GROUP = 4
TILES = 3
UNROLL = 4
RP = 144
RS_ORDER = (3, 2, 1, 0)


def sds(shape, dtype):
    return jax.ShapeDtypeStruct(shape, dtype)


def params(limit=VMEM_LIMIT):
    return pltpu.CompilerParams(vmem_limit_bytes=limit)


def after(vals, deps):
    return lax.optimization_barrier((vals, deps))[0]


def cost(gflop, mbytes):
    return pl.CostEstimate(
        flops=int(gflop * 1e9), bytes_accessed=int(mbytes * 1e6), transcendentals=0
    )


def copy_body(v_ref, out_ref):
    out_ref[...] = v_ref[...]


def fence(token):
    return pl.pallas_call(
        copy_body,
        out_shape=sds(token.shape, token.dtype),
        in_specs=[VMEM_SPEC],
        out_specs=VMEM_SPEC,
        compiler_params=params(BIG_LIMIT),
        name="fence",
    )(token)


def xor_pairs(size, step):
    return [(i, i ^ step) for i in range(size)]


def z_pairs(pairs):
    return [(2 * a + x, 2 * b + x) for a, b in pairs for x in range(2)]


def pack_plain(blocks):
    lead = blocks.shape[:-3]
    grp = blocks.reshape(lead + (-1, GROUP, 96, 96))
    last = jnp.swapaxes(grp[..., 3, :, :].reshape(lead + (-1, 96, 3, 32)), -3, -2)
    return jnp.concatenate([grp[..., :3, :, :], last], axis=-1)


def unpack_plain(groups):
    last = jnp.swapaxes(groups[..., 96:], -3, -2)
    last = last.reshape(groups.shape[:-3] + (1, 96, 96))
    grp = jnp.concatenate([groups[..., :96], last], axis=-3)
    return grp.reshape(groups.shape[:-4] + (-1, 96, 96))


def pack_owned_body(m_ref, out_ref):
    for g in range(out_ref.shape[0]):
        last = m_ref[GROUP * g + 3].astype(BF)
        for k in range(TILES):
            out_ref[g, k] = jnp.concatenate(
                [m_ref[GROUP * g + k].astype(BF), last[:, 32 * k : 32 * k + 32]], axis=-1
            )


def pack_owned(blocks):
    n = blocks.shape[0] // GROUP
    return pl.pallas_call(
        pack_owned_body,
        out_shape=sds((n, TILES, 96, 128), BF),
        in_specs=[VMEM_SPEC],
        out_specs=VMEM_SPEC,
        compiler_params=params(),
        cost_estimate=cost(0.1, 2),
        name="pack_owned",
    )(blocks)


def weights_body(n_pieces, places, pos_ref, me_ref, *refs):
    pieces = refs[:n_pieces]
    outs = refs[n_pieces : n_pieces + 4]
    wqkv_ref, wo_ref, w1_ref, w2_ref, al, sems, out_sem = refs[n_pieces + 4 :]
    dp, y = me_ref[0], me_ref[1] // 2
    groups = al.shape[1]
    copies = []
    for ref, (jy, jd) in zip(pieces, places):
        n = ref.shape[-4]
        if jd is None:
            for s in range(2):
                dst = al.at[s, :, pl.ds(0, TILES)]
                copies.append(((s,), pltpu.make_async_copy(ref.at[s], dst, sems.at[s])))
        else:
            dst = al.at[y ^ jy, pl.ds((dp ^ jd) * n, n), pl.ds(0, TILES)]
            copies.append(((0, 1), pltpu.make_async_copy(ref, dst, sems.at[y ^ jy])))
    for _, copy in copies:
        copy.start()
    for s in range(2):
        whole = al.at[s, :, pl.ds(0, TILES)]
        pltpu.make_async_copy(whole, whole, sems.at[s]).wait()

        def fix(g, carry, s=s):
            rolled = [pltpu.roll(al[s, g, k], 32 + 32 * k, 1) for k in range(TILES)]
            lane = lax.broadcasted_iota(jnp.int32, rolled[0].shape, 1)
            al[s, g, 3] = jnp.where(lane < 32, rolled[0], jnp.where(lane < 64, rolled[1], rolled[2]))
            return carry

        lax.fori_loop(0, groups, fix, 0, unroll=16)

    def block(s, b):
        p = pos_ref[b]
        return al[s, p // GROUP, p % GROUP][:, :96]

    def strip_qkv(i, carry):
        rows = pl.ds(pl.multiple_of(i * 96, 96), 96)
        for part in range(3):
            wqkv_ref[rows, part * 384 : part * 384 + 384] = jnp.concatenate(
                [block(j // 2, i * 6 + part * 2 + j % 2) for j in range(4)], axis=-1
            )
        return carry

    def strip(i, carry, ref, first):
        rows = pl.ds(pl.multiple_of(i * 96, 96), 96)
        for s in range(2):
            for half in range(2):
                ref[s, rows, half * 384 : half * 384 + 384] = jnp.concatenate(
                    [block(s, first + i * 8 + half * 4 + j) for j in range(4)], axis=-1
                )
        return carry

    def send(k):
        copy = pltpu.make_async_copy((wqkv_ref, wo_ref, w1_ref, w2_ref)[k], outs[k], out_sem.at[k])
        copy.start()
        return copy

    lax.fori_loop(0, 8, functools.partial(strip, ref=w1_ref, first=64), 0, unroll=UNROLL)
    sent = [send(2)]
    lax.fori_loop(0, 8, functools.partial(strip, ref=w2_ref, first=128), 0, unroll=UNROLL)
    sent.append(send(3))
    lax.fori_loop(0, 8, strip_qkv, 0, unroll=UNROLL)
    sent.append(send(0))
    for i in range(4):
        for half in range(2):
            wo_ref[i * 96 : i * 96 + 96, half * 384 : half * 384 + 384] = jnp.concatenate(
                [block(i // 2, 48 + (i % 2) * 8 + half * 4 + j) for j in range(4)], axis=-1
            )
    sent.append(send(1))
    for copy in sent:
        copy.wait()


def build_weights(pos, me, pieces, places, slots):
    return pl.pallas_call(
        functools.partial(weights_body, len(pieces), places),
        out_shape=(
            sds((768, 1152), BF),
            sds((384, 768), BF),
            sds((2, 768, 768), BF),
            sds((2, 768, 768), BF),
        ),
        in_specs=[SMEM_SPEC, SMEM_SPEC] + [HBM_SPEC] * len(pieces),
        out_specs=(HBM_SPEC,) * 4,
        scratch_shapes=[
            pltpu.VMEM((768, 1152), BF),
            pltpu.VMEM((384, 768), BF),
            pltpu.VMEM((2, 768, 768), BF),
            pltpu.VMEM((2, 768, 768), BF),
            pltpu.VMEM((2, slots // GROUP, GROUP, 96, 128), BF),
            pltpu.SemaphoreType.DMA((2,)),
            pltpu.SemaphoreType.DMA((4,)),
        ],
        compiler_params=params(BIG_LIMIT),
        cost_estimate=cost(0.1, 30),
        name="build_weights",
    )(pos, me, *pieces)


def product(left, right, out, width=384):
    def step(i, carry):
        col = pl.multiple_of(i * width, width)
        out[pl.ds(col, width), :] = inner_rows(left[:, pl.ds(col, width)], right[...]).astype(BF)
        return carry

    lax.fori_loop(0, out.shape[0] // width, step, 0)


def down_grads_body(act_ref, d2_ref, out_ref):
    for s in range(2):
        product(act_ref.at[s], d2_ref, out_ref.at[s])


def up_grads_body(h_ref, dpre_ref, out_ref):
    for s in range(2):
        product(h_ref, dpre_ref.at[s], out_ref.at[s])


def down_grads(act, d_two):
    return pl.pallas_call(
        down_grads_body,
        out_shape=sds((2, 768, 768), BF),
        in_specs=[VMEM_SPEC] * 2,
        out_specs=VMEM_SPEC,
        compiler_params=params(),
        cost_estimate=cost(1.4, 8),
        name="down_grads",
    )(act, d_two)


def up_grads(h_in, d_pre):
    return pl.pallas_call(
        up_grads_body,
        out_shape=sds((2, 768, 768), BF),
        in_specs=[VMEM_SPEC] * 2,
        out_specs=VMEM_SPEC,
        compiler_params=params(),
        cost_estimate=cost(1.4, 8),
        name="up_grads",
    )(h_in, d_pre)


def tile_of(vals, j):
    if j < 3:
        return vals[:, 96 * j : 96 * j + 128]
    return pltpu.roll(vals[:, 256:384], 96, 1)


def pack_body(places, pos_ref, me_ref, *refs):
    token_ref = refs[5]
    outs = refs[6 : 6 + len(places)]
    g2, g1, go, gq, al, sem, sems = refs[6 + len(places) :]
    loads = [pltpu.make_async_copy(src, dst, sems.at[k]) for k, (src, dst) in enumerate(zip(refs, (g2, g1, go, gq)))]
    for load in loads:
        load.start()
    groups = al.shape[1]
    token_ref[...] = jnp.zeros_like(token_ref)

    def put(s, b, blk):
        p = pos_ref[b]
        al[s, p // GROUP, p % GROUP] = blk

    def strip(i, carry, ref, first):
        rows = pl.ds(pl.multiple_of(i * 96, 96), 96)
        for s in range(2):
            for half in range(2):
                vals = ref[s, rows, half * 384 : half * 384 + 384]
                for j in range(4):
                    put(s, first + i * 8 + half * 4 + j, tile_of(vals, j))
        return carry

    def strip_qkv(i, carry):
        rows = pl.ds(pl.multiple_of(i * 96, 96), 96)
        for part in range(3):
            vals = gq[rows, part * 384 : part * 384 + 384]
            for j in range(4):
                put(j // 2, i * 6 + part * 2 + j % 2, tile_of(vals, j))
        return carry

    loads[0].wait()
    lax.fori_loop(0, 8, functools.partial(strip, ref=g2, first=128), 0, unroll=UNROLL)
    loads[1].wait()
    lax.fori_loop(0, 8, functools.partial(strip, ref=g1, first=64), 0, unroll=UNROLL)
    loads[2].wait()
    for i in range(4):
        for half in range(2):
            vals = go[i * 96 : i * 96 + 96, half * 384 : half * 384 + 384]
            for j in range(4):
                put(i // 2, 48 + (i % 2) * 8 + half * 4 + j, tile_of(vals, j))
    loads[3].wait()
    lax.fori_loop(0, 8, strip_qkv, 0, unroll=UNROLL)

    dp, y = me_ref[0], me_ref[1] // 2
    copies = []
    for s in range(2):

        def fix(g, carry, s=s):
            last = al[s, g, 3]
            low = lax.broadcasted_iota(jnp.int32, last.shape, 1) < 96
            for k in range(TILES):
                al[s, g, k] = jnp.where(low, al[s, g, k], pltpu.roll(last, 96 - 32 * k, 1))
            return carry

        lax.fori_loop(0, groups, fix, 0, unroll=16)
        for ref, (jy, jd) in zip(outs, places):
            if jd is None:
                copies.append((None, pltpu.make_async_copy(al.at[s, :, pl.ds(0, TILES)], ref.at[s], sem)))
            else:
                n = ref.shape[0]
                src = al.at[s, pl.ds((dp ^ jd) * n, n), pl.ds(0, TILES)]
                copies.append(((y ^ jy) == s, pltpu.make_async_copy(src, ref, sem)))
        for mine, copy in copies[s * len(outs) :]:
            if mine is None:
                copy.start()
            else:
                pl.when(mine)(copy.start)
    for mine, copy in copies:
        if mine is None:
            copy.wait()
        else:
            pl.when(mine)(copy.wait)


def pack_grads(pos, me, grads, places, out_shapes, slots):
    return pl.pallas_call(
        functools.partial(pack_body, places),
        out_shape=(sds((8, 128), F32), *(sds(s, BF) for s in out_shapes)),
        in_specs=[SMEM_SPEC, SMEM_SPEC] + [HBM_SPEC] * 4 + [ANY_SPEC],
        out_specs=(VMEM_SPEC,) + (HBM_SPEC,) * len(places),
        scratch_shapes=[
            pltpu.VMEM((2, 768, 768), BF),
            pltpu.VMEM((2, 768, 768), BF),
            pltpu.VMEM((384, 768), BF),
            pltpu.VMEM((768, 1152), BF),
            pltpu.VMEM((2, slots // GROUP, GROUP, 96, 128), BF),
            pltpu.SemaphoreType.DMA,
            pltpu.SemaphoreType.DMA((4,)),
        ],
        compiler_params=params(BIG_LIMIT),
        cost_estimate=cost(0.1, 30),
        name="pack_grads",
    )(pos, me, *grads)


def project_body(flags_ref, xa, xb, xc, xd, sh_ref, w_ref, b_ref, later_ref, proj_ref, x0_ref, xin_ref, bias):
    @pl.when(pl.program_id(0) == 0)
    def _():
        n = xa.shape[0]
        gap = jnp.zeros((RP - n, x0_ref.shape[1]), F32)
        for k, ref in enumerate((xa, xb, xc, xd)):
            x0_ref[k * RP : k * RP + n, :] = ref[...].astype(F32)
            x0_ref[k * RP + n : k * RP + RP, :] = gap

            @pl.when((flags_ref[0] == k) & (flags_ref[1] == 1))
            def _(k=k):
                x0_ref[k * RP : k * RP + MEM, :] = sh_ref[6 : 6 + MEM, :]

        xin_ref[...] = x0_ref[...].astype(BF)
        for part, col in ((0, 0), (2, 192)):
            bias[part] = jnp.concatenate([b_ref[s : s + 1, col : col + 192] for s in range(2)], axis=1)
        bias[1] = jnp.zeros((1, 384), F32)

    proj_ref[...] = (dot(xin_ref[...], w_ref[...]) + bias[pl.program_id(0)]).astype(BF)


def project(flags, quarters, shared, w_qkv, biases, later):
    rows = 4 * RP

    def whole(shape):
        return pl.BlockSpec(shape, lambda i: (0, 0))

    return pl.pallas_call(
        project_body,
        grid=(3,),
        out_shape=(sds((rows, 1152), BF), sds((rows, 768), F32), sds((rows, 768), BF)),
        in_specs=[
            SMEM_SPEC,
            *[whole(q.shape) for q in quarters],
            whole(shared.shape),
            pl.BlockSpec((768, 384), lambda i: (0, i)),
            whole(biases.shape),
            ANY_SPEC,
        ],
        out_specs=(
            pl.BlockSpec((rows, 384), lambda i: (0, i)),
            whole((rows, 768)),
            whole((rows, 768)),
        ),
        scratch_shapes=[pltpu.VMEM((3, 1, 384), F32)],
        compiler_params=params(),
        cost_estimate=cost(1.0, 5),
        name="project",
    )(flags, *quarters, shared, w_qkv, biases, later)


def head_masks(shape):
    lane = lax.broadcasted_iota(jnp.int32, shape, 1)
    return lane < HEAD_DIM, lane >= HEAD_DIM


def attend_body(cq_ref, ck_ref, q_ref, k_ref, v_ref, wo_ref, ctx_ref, p_ref, part_ref, vis):
    h = pl.program_id(0)

    @pl.when(h == 0)
    def _():
        cq, ck = cq_ref[...], ck_ref[...]
        seen = ((cq == -1) | (ck == -1) | (cq == ck)) & (ck != -2)
        vis[...] = jnp.where(seen, 1.0, 0.0)

    q, k, v = q_ref[...], k_ref[...], v_ref[...]
    masks = head_masks(q.shape)
    raws = [dot_back(jnp.where(masks[n], q, jnp.zeros_like(q)), k) for n in range(2)]
    outs = []
    for n in range(2):
        scores = jnp.where(vis[...] > 0.5, raws[n] * HEAD_DIM ** (-0.5), -1000000000.0)
        e = jnp.exp(scores - jnp.max(scores, axis=-1, keepdims=True))
        p = (e * (1.0 / jnp.sum(e, axis=-1, keepdims=True))).astype(BF)
        p_ref[n] = p
        outs.append(dot(p, v))
    ctx_ref[:, pl.ds(pl.multiple_of(h * 128, 128), 128)] = jnp.where(masks[0], outs[0], outs[1]).astype(BF)

    @pl.when(h == pl.num_programs(0) - 1)
    def _():
        part_ref[...] = dot(ctx_ref[...], wo_ref[...]).astype(BF)


def head_col(rows, off):
    return pl.BlockSpec((rows, 128), lambda h: (0, h + off))


def all_steps(shape):
    return pl.BlockSpec(shape, lambda h: (0,) * len(shape))


def attend(code_q, code_k, proj, w_out):
    rows = proj.shape[0]
    pairs = HEADS // 4
    return pl.pallas_call(
        attend_body,
        grid=(pairs,),
        out_shape=(sds((rows, 384), BF), sds((2 * pairs, rows, rows), BF), sds((rows, 768), BF)),
        in_specs=[
            all_steps((rows, 1)),
            all_steps((1, rows)),
            head_col(rows, 0),
            head_col(rows, pairs),
            head_col(rows, 2 * pairs),
            all_steps((384, 768)),
        ],
        out_specs=(
            all_steps((rows, 384)),
            pl.BlockSpec((2, rows, rows), lambda h: (h, 0, 0)),
            all_steps((rows, 768)),
        ),
        scratch_shapes=[pltpu.VMEM((rows, rows), F32)],
        compiler_params=params(),
        cost_estimate=cost(2.5, 8),
        name="attend",
    )(code_q, code_k, proj, proj, proj, w_out)


def both_cores(mine_ref, other_ref):
    half = mine_ref.shape[0] // 2
    other = jnp.concatenate([other_ref[half:, :], other_ref[:half, :]], axis=0)
    return mine_ref[...].astype(F32) + other.astype(F32)


def col_sum(v):
    return jnp.sum(v, axis=0, keepdims=True)


def feed_body(mine_ref, other_ref, x0_ref, sh_ref, b_ref, w1_hbm, w2_hbm, h_ref, n_ref, r_ref, act_ref, slope_ref, part_ref, w1, w2, acc, sems):
    copies = []
    for s in range(2):
        copies.append(pltpu.make_async_copy(w1_hbm.at[s], w1.at[s], sems.at[s]))
        copies.append(pltpu.make_async_copy(w2_hbm.at[s], w2.at[s], sems.at[2 + s]))
    for copy in copies:
        copy.start()
    total = both_cores(mine_ref, other_ref) + sh_ref[0:1, :] + x0_ref[...]
    h_one, normed, inverse = norm_parts(total, sh_ref[1:2, :], sh_ref[2:3, :])
    h_ref[...] = h_one.astype(BF)
    n_ref[...] = normed
    r_ref[...] = inverse
    for s in range(2):
        copies[2 * s].wait()
        pre = dot(h_ref[...], w1[s]) + b_ref[s : s + 1, 384:]
        cdf = 0.5 * (1.0 + lax.erf(pre * 0.7071067811865476))
        act_ref[s] = (pre * cdf).astype(BF)
        slope_ref[s] = (cdf + pre * jnp.exp(-0.5 * pre * pre) * 0.3989422804014327).astype(BF)
        copies[2 * s + 1].wait()
        part = dot(act_ref[s], w2[s])
        acc[...] = part if s == 0 else acc[...] + part
    part_ref[...] = acc[...].astype(BF)


def feed(mine, other, x_zero, shared, biases, w1, w2):
    rows = x_zero.shape[0]
    one, two = sds((rows, 768), BF), sds((2, rows, 768), BF)
    return pl.pallas_call(
        feed_body,
        out_shape=(one, sds((rows, 768), F32), sds((rows, 1), F32), two, two, one),
        in_specs=[VMEM_SPEC] * 5 + [ANY_SPEC] * 2,
        out_specs=(VMEM_SPEC,) * 6,
        scratch_shapes=[
            pltpu.VMEM((2, 768, 768), BF),
            pltpu.VMEM((2, 768, 768), BF),
            pltpu.VMEM((rows, 768), F32),
            pltpu.SemaphoreType.DMA((4,)),
        ],
        compiler_params=params(),
        cost_estimate=cost(2.8, 16),
        name="feed",
    )(mine, other, x_zero, shared, biases, w1, w2)


def feed_back_body(mine_ref, other_ref, n_ref, slope_ref, ca, cb, cc, cd, sh_ref, w1_hbm, w2_hbm, out_ref, d2_ref, d2b_ref, dpre_ref, part_ref, sums_ref, bsum_ref, w1, w2, g, acc, sems):
    copies = []
    for s in range(2):
        copies.append(pltpu.make_async_copy(w2_hbm.at[s], w2.at[s], sems.at[2 + s]))
        copies.append(pltpu.make_async_copy(w1_hbm.at[s], w1.at[s], sems.at[s]))
    for copy in copies:
        copy.start()
    n = ca.shape[0]
    for k, ref in enumerate((ca, cb, cc, cd)):
        g[k * RP : k * RP + n, :] = ref[...].astype(F32)
        g[k * RP + n : k * RP + RP, :] = jnp.zeros((RP - n, 768), F32)
    own = g.shape[0] // 2

    def row(i):
        return sh_ref[i : i + 1, :]

    h_one = n_ref[...] * row(1) + row(2)
    total = both_cores(mine_ref, other_ref) + row(3) + h_one
    rows_out, normed, inverse = norm_parts(total, row(4), row(5))
    out_ref[...] = rows_out[:own].astype(BF)
    grad = g[...]
    d_two = norm_back(grad, normed, inverse, row(4))
    d2_ref[...] = d_two
    d2b_ref[...] = d_two.astype(BF)
    sums_ref[0:3, :] = jnp.concatenate(
        [col_sum(d_two[:own]), col_sum(grad[:own] * normed[:own]), col_sum(grad[:own])], axis=0
    )
    sums_ref[3:8, :] = jnp.zeros((5, 768), F32)
    for s in range(2):
        copies[2 * s].wait()
        d_pre = dot_back(d2b_ref[...], w2[s]) * slope_ref[s].astype(F32)
        bsum_ref[s : s + 1, :] = col_sum(d_pre)
        dpre_ref[s] = d_pre.astype(BF)
        copies[2 * s + 1].wait()
        part = dot_back(dpre_ref[s], w1[s])
        acc[...] = part if s == 0 else acc[...] + part
    part_ref[...] = acc[...].astype(BF)


def feed_back(mine, other, normed, slope, cots, shared, w1, w2):
    rows = normed.shape[0]
    one = sds((rows, 768), BF)
    return pl.pallas_call(
        feed_back_body,
        out_shape=(
            sds((rows // 2, 768), BF),
            sds((rows, 768), F32),
            one,
            sds((2, rows, 768), BF),
            one,
            sds((8, 768), F32),
            sds((2, 768), F32),
        ),
        in_specs=[VMEM_SPEC] * 9 + [ANY_SPEC] * 2,
        out_specs=(VMEM_SPEC,) * 7,
        scratch_shapes=[
            pltpu.VMEM((2, 768, 768), BF),
            pltpu.VMEM((2, 768, 768), BF),
            pltpu.VMEM((rows, 768), F32),
            pltpu.VMEM((rows, 768), F32),
            pltpu.SemaphoreType.DMA((4,)),
        ],
        compiler_params=params(),
        cost_estimate=cost(2.8, 16),
        name="feed_back",
    )(mine, other, normed, slope, *cots, shared, w1, w2)


def attend_back_body(mine_ref, other_ref, d2_ref, n_ref, r_ref, sh_ref, wo_ref, wqkv_ref, x_ref, ctx_ref, later_ref, p_ref, q_ref, k_ref, v_ref, d1_ref, gq_ref, go_ref, part_ref, send_ref, sums_ref, bsum_ref, d1b_ref, dproj_ref, dctx):
    h = pl.program_id(0)
    pairs = pl.num_programs(0)
    own = d1_ref.shape[0]

    @pl.when(h == 0)
    def _():
        dh = both_cores(mine_ref, other_ref) + d2_ref[...]
        normed = n_ref[...]
        d_one = norm_back(dh, normed, r_ref[...], sh_ref[1:2, :])
        d1_ref[...] = d_one[:own]
        d1b_ref[...] = d_one.astype(BF)
        sums_ref[0:3, :] = jnp.concatenate(
            [col_sum(d_one[:own]), col_sum(dh[:own] * normed[:own]), col_sum(dh[:own])], axis=0
        )
        sums_ref[3:8, :] = jnp.zeros((5, 768), F32)
        back = dot_back(d1b_ref[...], wo_ref[...]).astype(BF)
        for m in range(3):
            dctx[m] = back[:, m * 128 : m * 128 + 128]

    q, k, v, dc = q_ref[...], k_ref[...], v_ref[...], dctx[h]
    masks = head_masks(q.shape)
    dqs, dks, dvs = [], [], []
    dps = [dot_back(jnp.where(masks[m], dc, jnp.zeros_like(dc)), v) for m in range(2)]
    for m in range(2):
        dvs.append(inner_rows(p_ref[m], dc))
        pf = p_ref[m].astype(F32)
        row = jnp.sum(dps[m] * pf, axis=-1, keepdims=True)
        ds = (pf * (dps[m] - row) * HEAD_DIM ** (-0.5)).astype(BF)
        dqs.append(dot(ds, k))
        dks.append(inner_rows(ds, q))
    dq, dk, dv = (jnp.where(masks[0], d[0], d[1]) for d in (dqs, dks, dvs))
    for part, d in enumerate((dq, dk, dv)):
        dproj_ref[:, pl.ds(pl.multiple_of(part * 384 + h * 128, 128), 128)] = d.astype(BF)
    bsum_ref[...] = jnp.concatenate([col_sum(dq), col_sum(dv), jnp.zeros((6, 128), F32)], axis=0)

    @pl.when(h == pairs - 1)
    def _():
        share = dot_back(dproj_ref[...], wqkv_ref[...]).astype(BF)
        part_ref[...] = share[:own]
        send_ref[...] = share[own:]
        product(ctx_ref, d1b_ref, go_ref)
        product(x_ref, dproj_ref, gq_ref)


def attend_back(mine, other, d_two, normed, inverse, shared, w_out, w_qkv, x_in, context, later, probs, proj):
    rows = proj.shape[0]
    pairs = HEADS // 4
    return pl.pallas_call(
        attend_back_body,
        grid=(pairs,),
        out_shape=(
            sds((rows // 2, 768), F32),
            sds((768, 1152), BF),
            sds((384, 768), BF),
            sds((rows // 2, 768), BF),
            sds((rows // 2, 768), BF),
            sds((8, 768), F32),
            sds((8, 384), F32),
        ),
        in_specs=[
            all_steps((rows, 768)),
            all_steps((rows, 768)),
            all_steps((rows, 768)),
            all_steps((rows, 768)),
            all_steps((rows, 1)),
            all_steps(shared.shape),
            all_steps((384, 768)),
            all_steps((768, 1152)),
            all_steps((rows, 768)),
            all_steps((rows, 384)),
            ANY_SPEC,
            pl.BlockSpec((2, rows, rows), lambda h: (h, 0, 0)),
            head_col(rows, 0),
            head_col(rows, pairs),
            head_col(rows, 2 * pairs),
        ],
        out_specs=(
            all_steps((rows // 2, 768)),
            all_steps((768, 1152)),
            all_steps((384, 768)),
            all_steps((rows // 2, 768)),
            all_steps((rows // 2, 768)),
            all_steps((8, 768)),
            pl.BlockSpec((8, 128), lambda h: (0, h)),
        ),
        scratch_shapes=[
            pltpu.VMEM((rows, 768), BF),
            pltpu.VMEM((rows, 1152), BF),
            pltpu.VMEM((3, rows, 128), BF),
        ],
        compiler_params=params(),
        cost_estimate=pl.CostEstimate(
            flops=2 * rows * rows * 64 * 4 * HEADS, bytes_accessed=10 * 1024 * 1024, transcendentals=0
        ),
        name="attend_back",
    )(mine, other, d_two, normed, inverse, shared, w_out, w_qkv, x_in, context, later, probs, proj, proj, proj)


def finish_body(flags_ref, part_ref, other_ref, d1_ref, gin_ref, mem_ref):
    d_zero = part_ref[...].astype(F32) + other_ref[...].astype(F32) + d1_ref[...]
    gin_ref[...] = d_zero.astype(BF)
    mem_ref[...] = jnp.zeros_like(mem_ref)
    for k in range(2):

        @pl.when((flags_ref[0] == k) & (flags_ref[1] == 1))
        def _(k=k):
            row = lax.broadcasted_iota(jnp.int32, (16, d_zero.shape[1]), 0)
            top = d_zero[k * RP : k * RP + 16, :]
            mem_ref[...] = jnp.where(row < MEM, top, 0.0)
            gin_ref[k * RP : k * RP + 16, :] = jnp.where(row < MEM, 0.0, top).astype(BF)


def finish(flags, part, other, d_one):
    return pl.pallas_call(
        finish_body,
        out_shape=(sds(d_one.shape, BF), sds((16, 768), F32)),
        in_specs=[SMEM_SPEC] + [VMEM_SPEC] * 3,
        out_specs=(VMEM_SPEC,) * 2,
        compiler_params=params(),
        cost_estimate=cost(0.1, 4),
        name="finish",
    )(flags, part, other, d_one)


def soap_body(n_terms, *refs):
    terms = refs[:n_terms]
    w_ref, m_ref, v_ref, sl_ref, sr_ref, l_ref, r_ref = refs[n_terms : n_terms + 7]
    nw_ref, nc_ref, nm_ref, nv_ref, nl_ref, nr_ref = refs[n_terms + 7 :]
    blocks = w_ref.shape[0]
    if n_terms == 1:
        grads = [terms[0][b] for b in range(blocks)]
    else:
        grads = []
        for g in range(blocks // GROUP):
            tiles = [sum(ref[g, k].astype(F32) for ref in terms) for k in range(TILES)]
            grads += [tile[:, :96] for tile in tiles]
            grads.append(jnp.concatenate([tile[:, 96:] for tile in tiles], axis=-1))
    every = range(blocks)
    gb = [g.astype(BF) for g in grads]
    lb, rb = [l_ref[b].astype(BF) for b in every], [r_ref[b].astype(BF) for b in every]
    half = [inner_rows(lb[b], gb[b]).astype(BF) for b in every]
    for b in every:
        nl_ref[b] = beta_two * sl_ref[b] + (1.0 - beta_two) * dot_back(gb[b], gb[b])
    turned = [dot(half[b], rb[b]) for b in every]
    for b in every:
        nr_ref[b] = beta_two * sr_ref[b] + (1.0 - beta_two) * inner_rows(gb[b], gb[b])
    steps = []
    for b in every:
        new_first = beta_one * m_ref[b] + (1.0 - beta_one) * turned[b]
        new_second = beta_two * v_ref[b] + (1.0 - beta_two) * turned[b] * turned[b]
        nm_ref[b] = new_first
        nv_ref[b] = new_second
        direction = (
            new_first
            / (1.0 - beta_one**STEP)
            / (jnp.sqrt(new_second / (1.0 - beta_two**STEP)) + adam_eps)
        )
        steps.append(direction.astype(BF))
    half = [dot(lb[b], steps[b]).astype(BF) for b in every]
    for b in every:
        new_weight = w_ref[b] - rate_matrix * dot_back(half[b], rb[b])
        nw_ref[b] = new_weight
        nc_ref[b] = new_weight.astype(BF)


def soap(terms, master, first, second, left, right, left_rot, right_rot):
    count = master.shape[0]
    many = next(n for n in (3, 2, 1) if terms[0].shape[0] % n == 0)
    step = many * GROUP if len(terms) > 1 else 1
    spec = pl.BlockSpec((step, 96, 96), lambda i: (i, 0, 0))
    packed = pl.BlockSpec((many, TILES, 96, 128), lambda i: (i, 0, 0, 0))
    full = sds(master.shape, F32)
    return pl.pallas_call(
        functools.partial(soap_body, len(terms)),
        grid=(count // step,),
        out_shape=(full, sds(master.shape, BF), full, full, full, full),
        in_specs=[packed if len(terms) > 1 else spec] * len(terms) + [spec] * 7,
        out_specs=(spec,) * 6,
        compiler_params=params(BIG_LIMIT),
        cost_estimate=cost(0.3, 24),
        name="soap",
    )(*terms, master, first, second, left, right, left_rot, right_rot)


def norm_parts(values, gain_vec, shift_vec):
    centred = values - jnp.mean(values, axis=-1, keepdims=True)
    inverse = lax.rsqrt(jnp.mean(centred * centred, axis=-1, keepdims=True) + norm_eps)
    normed = centred * inverse
    return (normed * gain_vec + shift_vec, normed, inverse)


def norm_back(upstream, normed, inverse, gain_vec):
    scaled = upstream * gain_vec
    result = inverse * (
        scaled
        - jnp.mean(scaled, axis=-1, keepdims=True)
        - normed * jnp.mean(scaled * normed, axis=-1, keepdims=True)
    )
    return result


def dot(left, right):
    return jnp.dot(left, right, preferred_element_type=F32)


def dot_back(left, right):
    return lax.dot_general(left, right, (((1,), (1,)), ((), ())), preferred_element_type=F32)


def inner_rows(left, right):
    return lax.dot_general(left, right, (((0,), (0,)), ((), ())), preferred_element_type=F32)


def adam_update(values, grad_vec, first_mom, second_mom, step_rate):
    new_first = beta_one * first_mom + (1.0 - beta_one) * grad_vec
    new_second = beta_two * second_mom + (1.0 - beta_two) * grad_vec * grad_vec
    direction = (
        new_first
        / (1.0 - beta_one**STEP)
        / (jnp.sqrt(new_second / (1.0 - beta_two**STEP)) + adam_eps)
    )
    return (values - step_rate * direction, new_first, new_second)


def per_device(
    n_dp,
    n_tensor,
    layer_in,
    cotangent,
    doc_ids,
    reset_flags,
    block_slot,
    master,
    first_moment,
    second_moment,
    left_stats,
    right_stats,
    left_basis,
    right_basis,
    split_params,
    split_first,
    split_second,
    shared,
    shared_first,
    shared_second,
):
    meshed = n_dp == 8 and master.shape[1] % GROUP == 0
    dp = lax.axis_index("dp")
    t = lax.axis_index("tensor")
    y, c = t // 2, t % 2
    me = jnp.stack([dp, t])
    barrier = lax.optimization_barrier
    slots = block_slot.shape[0]
    quarter = layer_in.shape[1]

    def swap(axis, step):
        size = n_dp if axis == "dp" else n_tensor
        return lambda v: lax.ppermute(v, axis, xor_pairs(size, step))

    core, yswap, xswap = swap("tensor", 1), swap("tensor", 2), swap("dp", 1)

    def along_z(*pairs):
        return lambda v: lax.ppermute(v, "dp", z_pairs(pairs))

    outer, middle = along_z((0, 1), (1, 0), (2, 3), (3, 2)), along_z((1, 2), (2, 1))
    inward, outward = along_z((0, 1), (3, 2)), along_z((1, 0), (2, 3))

    docs = lax.dynamic_index_in_dim(doc_ids, y, 0, keepdims=False)
    edge = jnp.full((MEM,), -1, jnp.int32)
    codes = jnp.concatenate([edge, docs, edge]).reshape(4, quarter)
    codes = jnp.pad(codes, ((0, 0), (0, RP - quarter)), constant_values=-2)
    codes = jnp.concatenate(
        [lax.dynamic_index_in_dim(codes, t ^ j, 0, keepdims=False) for j in (0, 2, 1, 3)]
    )
    code_q, code_k = codes[:, None], codes[None, :]
    reset_now = lax.dynamic_index_in_dim(reset_flags, y, 0, keepdims=False) == 1
    flags = jnp.stack([y + 2 * c, reset_now.astype(jnp.int32)])

    split_other = yswap(split_params)
    biases = jnp.concatenate(
        [jnp.where(y == 0, split_params, split_other), jnp.where(y == 0, split_other, split_params)], axis=0
    )
    def inputs_of(arr):
        mine = lax.dynamic_index_in_dim(arr, y, 0, keepdims=False)
        other = lax.dynamic_index_in_dim(arr, 1 - y, 0, keepdims=False)
        return mine, other

    (in_mine, in_send), (cot_mine, cot_send) = inputs_of(layer_in), inputs_of(cotangent)

    if meshed:
        own = pack_owned(master[0])
        near, mid = outer(own), middle(own)
        x0, y0 = xswap(own), yswap(own)
        tok = biases[:, :128]
        near, mid, x0, y0, tok = barrier((near, mid, x0, y0, tok))
        far_mid, far_end = middle(near), outward(mid)
        x1, diag0 = xswap(near), yswap(x0)
        small = (code_q, code_k, flags, biases, me, in_send, cot_send, fence(tok))
        x1, diag0, far_mid, far_end, small = barrier((x1, diag0, far_mid, far_end, small))
        code_q, code_k, flags, biases, me, in_send, cot_send, tok = small
        far = far_mid + far_end
        last_end = outward(far_mid)
        x2, y2 = xswap(far), yswap(far)
        x2, y2, last_end, tok = barrier((x2, y2, last_end, fence(tok)))
        last = mid + last_end
        x3, y3, y1 = xswap(last), yswap(last), outer(y0)
        x3, y3, y1, in_send, tok = barrier((x3, y3, y1, in_send, fence(tok)))
        diag3, diag2, diag1 = xswap(y3), yswap(x2), outer(diag0)
        in_other = yswap(in_send)
        diag3, diag2, diag1, cot_send, tok = barrier((diag3, diag2, diag1, cot_send, fence(tok)))
        me = after(me, fence(tok))
        pieces, places = [], []
        for jz, vals in enumerate(
            ((own, x0, y0, diag0), (near, x1, y1, diag1), (far, x2, y2, diag2), (last, x3, y3, diag3))
        ):
            pieces.extend(vals)
            places.extend([(0, 2 * jz), (0, 2 * jz + 1), (1, 2 * jz), (1, 2 * jz + 1)])
    else:
        every = lax.all_gather(master.astype(BF), "dp", axis=1, tiled=True)
        every_other = yswap(every)
        every = jnp.concatenate(
            [jnp.where(y == 0, every, every_other), jnp.where(y == 0, every_other, every)], axis=0
        )
        pieces, places = [pack_plain(every)], [(0, None)]
        in_other = yswap(in_send)
    w_qkv, w_out, w_up, w_down = build_weights(block_slot, me, pieces, tuple(places), slots)

    cot_other = yswap(cot_send)
    quarters = (in_mine, in_other, core(in_mine), core(in_other))
    proj, x_zero, x_in = project(flags, quarters, shared, w_qkv, biases, cot_other)
    cots = (cot_mine, cot_other, core(cot_mine), core(cot_other))
    context, probs, attn = attend(code_q, code_k, proj, w_out)
    h_in, normed, inverse, act, slope, ffn = feed(attn, core(attn), x_zero, shared, biases, w_up, w_down)
    rows_out, d_two, d_two_b, d_pre, d_hidden, sums_two, up_sums = feed_back(
        ffn, core(ffn), normed, slope, cots, shared, w_up, w_down
    )
    d_hidden_other = core(d_hidden)
    g_down, g_up = down_grads(act, d_two_b), up_grads(h_in, d_pre)
    d_one, g_qkv, g_out, d_in, d_in_send, sums_one, head_sums = attend_back(
        d_hidden, d_hidden_other, d_two, normed, inverse, shared, w_out, w_qkv, x_in, context, g_down, probs, proj
    )
    def to_owner(arr):
        mine, other = arr[:quarter], yswap(arr[RP : RP + quarter])
        both = jnp.stack([mine, other])
        return jnp.where(y == 0, both, both[::-1])

    layer_out = to_owner(rows_out)
    me = after(me, layer_out)
    d_in_other = core(d_in_send)
    grad_rows, memory_grad = finish(flags, d_in, d_in_other, d_one)
    grads = (g_down, g_up, g_out, g_qkv, memory_grad)
    vec = jnp.concatenate([sums_one[:3], sums_two[:3], memory_grad[:MEM]], axis=0)
    halves = head_sums[:2].reshape(2, 2, 192).swapaxes(0, 1).reshape(2, 384)
    splits = jnp.concatenate([halves, up_sums], axis=1).reshape(3, 768)

    def add_core(vec):
        return jnp.concatenate([vec + core(vec), splits], axis=0)

    if meshed:
        per = master.shape[1] // GROUP
        half = per // 2
        places, shapes = [], []
        for jz in RS_ORDER:
            for jy in range(2):
                for jx in range(2):
                    places.append((jy, 2 * jz + jx))
                    shapes.append((per, TILES, 96, 128))
        token, *packed = pack_grads(block_slot, me, grads, tuple(places), shapes, slots)
        own, x_unit, y_unit, diag = {}, {}, {}, {}
        for n, jz in enumerate(RS_ORDER):
            own[jz], x_unit[jz], y_unit[jz], diag[jz] = packed[4 * n : 4 * n + 4]

        def plus(*vals):
            return sum(v.astype(F32) for v in vals).astype(BF)

        vec = after(add_core(vec), token)
        d3, d2, n1 = xswap(diag[3]), yswap(diag[2]), outer(diag[1])
        vec = vec + yswap(vec)
        d3, d2, n1, vec, tok = barrier((d3, d2, n1, vec, fence(token)))
        x3, y3, m1 = xswap(x_unit[3]), yswap(plus(y_unit[3], d3)), outer(y_unit[1])
        vec = vec + swap("dp", 1)(vec)
        x3, y3, m1, vec, tok = barrier((x3, y3, m1, vec, fence(tok)))
        x2, y2 = xswap(plus(x_unit[2], d2)), yswap(y_unit[2])
        part3 = plus(own[3], x3, y3)
        e3 = inward(part3)
        vec = vec + swap("dp", 2)(vec)
        x2, y2, e3, vec, tok = barrier((x2, y2, e3, vec, fence(tok)))
        x1, d0 = xswap(x_unit[1]), yswap(plus(diag[0], n1))
        part2 = plus(own[2], x2, y2, e3)
        fm, fe = middle(part2), inward(part2)
        vec = vec + swap("dp", 4)(vec)
        x1, d0, fm, fe, vec, tok = barrier((x1, d0, fm, fe, vec, fence(tok)))
        x0, y0 = xswap(plus(x_unit[0], d0)), yswap(plus(y_unit[0], m1))
        near, mid = outer(plus(own[1], x1, fm)), middle(plus(part3, fe))
        x0, y0, near, mid, grad_rows, tok = barrier((x0, y0, near, mid, grad_rows, fence(tok)))
        terms = (own[0], x0, y0, near, mid)
    else:
        packed = pack_grads(
            block_slot, me, grads, ((0, None),), [(2, slots // GROUP, TILES, 96, 128)], slots
        )[1]
        blocks = unpack_plain(packed)
        blocks = lax.psum_scatter(blocks, "dp", scatter_dimension=1, tiled=True)
        mine = lax.dynamic_index_in_dim(blocks, y, 0, keepdims=False)
        other = yswap(lax.dynamic_index_in_dim(blocks, 1 - y, 0, keepdims=False))
        terms = (mine.astype(F32) + other.astype(F32),)

        vec = add_core(vec)
        vec = vec + yswap(vec)
        step = 1
        while step < n_dp:
            vec = vec + swap("dp", step)(vec)
            step *= 2

    grad_in = to_owner(grad_rows)
    total_shared = vec[:16]
    grad_split = lax.dynamic_index_in_dim(vec[16:].reshape(2, -1), y, 0, keepdims=True)

    new_master, new_copy, new_first, new_second, new_left, new_right = soap(
        terms,
        master[0],
        first_moment[0],
        second_moment[0],
        left_stats[0],
        right_stats[0],
        left_basis[0],
        right_basis[0],
    )
    new_split, new_split_first, new_split_second = adam_update(
        split_params, grad_split, split_first, split_second, rate_vector
    )
    new_shared, new_shared_first, new_shared_second = adam_update(
        shared, total_shared, shared_first, shared_second, rate_shared
    )
    return (
        layer_out,
        grad_in,
        new_master[None],
        new_copy[None],
        new_first[None],
        new_second[None],
        new_left[None],
        new_right[None],
        new_split,
        new_split_first,
        new_split_second,
        new_shared,
        new_shared_first,
        new_shared_second,
    )


def solution(mesh):
    rows = P("dp", "tensor", None)
    state = P("tensor", "dp", None, None)
    split = P("tensor", None)
    return jax.shard_map(
        functools.partial(per_device, mesh.shape["dp"], mesh.shape["tensor"]),
        mesh=mesh,
        in_specs=(rows, rows, P("dp", None), P("dp"), P()) + (state,) * 7 + (split,) * 3 + (P(),) * 3,
        out_specs=(rows, rows) + (state,) * 6 + (split,) * 3 + (P(),) * 3,
        check_vma=False,
    )
```
